32 devices in a mesh: group: 4 (over x, core), blk: 2 (over y), head: 4 (over z).
Axes of the slice: x: 2, y: 2, z: 4, core: 2. Of those that a mesh axis runs over, the one named last changes fastest.
Arguments:
- latents: bfloat16 [4, 1024, 1024], P('group', 'blk'), may hold values from -6 to 6
- inputs: bfloat16 [4, 512, 1024], P('group', 'blk'), may hold values from -6 to 6
- latent_group: int32 [4, 1024], P('group', 'blk'), may hold values from 0 to 15
- latent_valid: int32 [4, 1024], P('group', 'blk'), may hold values 0 or 1
- input_group: int32 [4, 512], P('group', 'blk'), may hold values from 0 to 15
- input_valid: int32 [4, 512], P('group', 'blk'), may hold values 0 or 1
- gains: float32 [5, 1024], replicated, may hold values from 0.1 to 1.9
- w_q_cross: bfloat16 [1024, 1024], P(None, 'head'), may hold values from -0.1875 to 0.1875
- w_kv_cross: bfloat16 [1024, 2, 1024], P(None, None, 'head'), may hold values from -0.1875 to 0.1875
- w_o_cross: bfloat16 [1024, 1024], P(None, 'head'), may hold values from -1.5 to 1.5
- w_in_a: bfloat16 [1024, 4096], P(None, 'head'), may hold values from -0.1875 to 0.1875
- w_out_a: bfloat16 [1024, 4096], P(None, 'head'), may hold values from -0.09375 to 0.09375
- w_qkv_self: bfloat16 [1024, 3, 1024], P(None, None, 'head'), may hold values from -0.1875 to 0.1875
- w_o_self: bfloat16 [1024, 1024], P(None, 'head'), may hold values from -1.5 to 1.5
- w_in_b: bfloat16 [1024, 4096], P(None, 'head'), may hold values from -0.1875 to 0.1875
- w_out_b: bfloat16 [1024, 4096], P(None, 'head'), may hold values from -0.09375 to 0.09375
- out_grad: bfloat16 [4, 1024, 1024], P('group', 'blk'), may hold values from -6 to 6
Outputs:
- latents_out: bfloat16 [4, 1024, 1024], P('group', 'blk')
- latent_grad: float32 [4, 1024, 1024], P('group', 'blk')
- input_grad: float32 [4, 512, 1024], P('group', 'blk')
- gains_grad: float32 [5, 1024], replicated
- grad_w_q_cross: float32 [1024, 1024], P(None, 'head')
- grad_w_kv_cross: float32 [1024, 2, 1024], P(None, None, 'head')
- grad_w_o_cross: float32 [1024, 1024], P(None, 'head')
- grad_w_in_a: float32 [1024, 4096], P(None, 'head')
- grad_w_out_a: float32 [1024, 4096], P(None, 'head')
- grad_w_qkv_self: float32 [1024, 3, 1024], P(None, None, 'head')
- grad_w_o_self: float32 [1024, 1024], P(None, 'head')
- grad_w_in_b: float32 [1024, 4096], P(None, 'head')
- grad_w_out_b: float32 [1024, 4096], P(None, 'head')
The draws below stay inside these ranges and needn't reach their ends.
Inputs may be any that keep to these rules, and one draw needn't show every extreme that they name: `latent_group`: a latent attends only to inputs and latents of its own group. `latent_valid`: padded tokens are never attended to as keys.
All inputs are finite; a program needn't handle non-finite values. No bound on the sum of `latent_valid` or of `input_valid` on one device may be relied on, other than what follows from the above.
Results may differ from the reference program's by a relative error of at most 0.024.
Values may be sent and summed in bfloat16 or wider, within the bound.
A program may use at most 192 MiB of HBM per device.

```python
import math
import jax
import jax.numpy as jnp
from jax import lax

D = 1024
HEAD_DIM = 128
FF = 4096
SUBG = 16
INNER = 1024
GROUPS = 4
LAT = 1024
INP = 512


def place_ends(values, own_key, low, top_value):
    shape = values.shape
    spot = [jax.random.randint(jax.random.fold_in(own_key, axis), (), 0, shape[axis]) for axis in range(len(shape))]
    values = values.at[tuple(spot)].set(low)
    longest = shape.index(max(shape))
    spot[longest] = (spot[longest] + 1) % shape[longest]
    return values.at[tuple(spot)].set(top_value)


def level_of(stream_key, extent, shards, least, top_value):
    gain, own = 1.0, jax.random.fold_in(stream_key, 6)
    for position, blocks in shards:
        steps = jnp.exp(jax.random.uniform(jax.random.fold_in(own, position), (blocks,), jnp.float32, least / len(shards), top_value / len(shards)))
        gain = gain * jnp.repeat(steps, extent[position] // blocks).reshape([-1 if axis == position else 1 for axis in range(len(extent))])
    return gain


def noise(key, extent, width, limit, shards=(), dtype=jnp.bfloat16):
    values = width * jax.random.normal(key, extent, jnp.float32)
    if shards:
        values = values * level_of(key, extent, shards, -0.22, 0.18)
    return jnp.clip(values, -limit, limit).astype(dtype)


def setup_inputs(seed: int = 0) -> dict:
    key_list = jax.random.split(jax.random.key(seed), 18)
    latents = noise(key_list[0], (GROUPS, LAT, D), 1.0, 6.0, ((0, 4), (1, 2)))
    inputs = noise(key_list[1], (GROUPS, INP, D), 1.0, 6.0, ((0, 4), (1, 2)))
    latent_group = place_ends(jax.random.randint(key_list[2], (GROUPS, LAT), 0, SUBG), jax.random.fold_in(key_list[2], 1), 0, SUBG - 1).astype(jnp.int32)
    latent_valid = place_ends((jax.random.randint(key_list[3], (GROUPS, LAT), 0, 8) < 7).astype(jnp.int32), jax.random.fold_in(key_list[3], 1), 0, 1)
    input_group = place_ends(jax.random.randint(key_list[4], (GROUPS, INP), 0, SUBG), jax.random.fold_in(key_list[4], 1), 0, SUBG - 1).astype(jnp.int32)
    input_valid = place_ends((jax.random.randint(key_list[5], (GROUPS, INP), 0, 8) < 7).astype(jnp.int32), jax.random.fold_in(key_list[5], 1), 0, 1)
    gains = jnp.clip(1.0 + 0.18 * jax.random.normal(key_list[6], (5, D), jnp.float32), 0.1, 1.9)
    w_q_cross = noise(key_list[7], (D, INNER), D ** -0.5, 0.1875, ((1, 4),))
    w_kv_cross = noise(key_list[8], (D, 2, INNER), D ** -0.5, 0.1875, ((2, 4),))
    w_o_cross = noise(key_list[9], (D, INNER), (INNER // 64) ** -0.5, 1.5, ((1, 4),))
    w_in_a = noise(key_list[10], (D, FF), D ** -0.5, 0.1875, ((1, 4),))
    w_out_a = noise(key_list[11], (D, FF), FF ** -0.5, 0.09375, ((1, 4),))
    w_qkv_self = noise(key_list[12], (D, 3, INNER), D ** -0.5, 0.1875, ((2, 4),))
    w_o_self = noise(key_list[13], (D, INNER), (INNER // 64) ** -0.5, 1.5, ((1, 4),))
    w_in_b = noise(key_list[14], (D, FF), D ** -0.5, 0.1875, ((1, 4),))
    w_out_b = noise(key_list[15], (D, FF), FF ** -0.5, 0.09375, ((1, 4),))
    out_grad = noise(key_list[16], (GROUPS, LAT, D), 1.0, 6.0, ((0, 4), (1, 2)))
    return dict(latents=latents, inputs=inputs, latent_group=latent_group, latent_valid=latent_valid, input_group=input_group, input_valid=input_valid, gains=gains, w_q_cross=w_q_cross, w_kv_cross=w_kv_cross, w_o_cross=w_o_cross, w_in_a=w_in_a, w_out_a=w_out_a, w_qkv_self=w_qkv_self, w_o_self=w_o_self, w_in_b=w_in_b, w_out_b=w_out_b, out_grad=out_grad)


@jax.custom_vjp
def low(v):
    return lax.optimization_barrier(v.astype(jnp.bfloat16)).astype(jnp.float32)

@jax.custom_vjp
def low_back(v):
    return v

def low_keep(v):
    return (low(v), None)

def low_pass(kept, grad):
    return (grad,)

def back_keep(v):
    return (v, None)

def back_low(kept, grad):
    return (low(grad),)
low.defvjp(low_keep, low_pass)
low_back.defvjp(back_keep, back_low)
highest = lax.Precision.HIGHEST
masked_fill = -1000.0

def both_ways(values):
    return low_back(low(values))

def layer_norm(values, gains_row):
    centred = values - lax.optimization_barrier(jnp.mean(values, axis=-1, keepdims=True))
    variance = lax.optimization_barrier(jnp.mean(centred * centred, axis=-1, keepdims=True))
    return centred * lax.rsqrt(variance + 1e-05) * gains_row

def matmul(left, right):
    return jnp.dot(left, right, precision=highest)

def matmul_out(left, right):
    return jnp.einsum('tn,dn->td', left, right, precision=highest)

def attention(queries, key_rows, value_rows, query_code, key_code):
    row_count = queries.shape[0]
    block_size = math.gcd(row_count, 512)
    head_count = queries.shape[1] // HEAD_DIM
    key_heads = key_rows.reshape(key_rows.shape[0], head_count, HEAD_DIM)
    value_heads = value_rows.reshape(value_rows.shape[0], head_count, HEAD_DIM)

    def one_block(block_data):
        query_block, code_block = block_data
        query_heads = query_block.reshape(block_size, head_count, HEAD_DIM)
        scores = jnp.einsum('qhd,khd->hqk', query_heads, key_heads, precision=highest) * HEAD_DIM ** (-0.5)
        allowed = code_block[:, None] == key_code[None, :]
        scores = low_back(jnp.where(allowed[None], scores, masked_fill))
        weights_soft = low(jax.nn.softmax(scores, axis=-1))
        mixed = jnp.einsum('hqk,khd->qhd', weights_soft, value_heads, precision=highest)
        return mixed.reshape(block_size, head_count * HEAD_DIM)
    stacked = lax.map(jax.checkpoint(one_block), (queries.reshape(row_count // block_size, block_size, queries.shape[1]), query_code.reshape(row_count // block_size, block_size)))
    return stacked.reshape(row_count, queries.shape[1])

def feed_forward(stream, gains_row, weight_in, weight_out):
    hidden_in = low(layer_norm(stream, gains_row))
    hidden = low_back(matmul(hidden_in, weight_in))
    return stream + low_back(matmul_out(low(jax.nn.gelu(hidden)), weight_out))

def forward(params, latent_code, input_code, self_code):
    latent_rows, input_rows, gains, w_q_cross, w_kv_cross, w_o_cross, w_in_a, w_out_a, w_qkv_self, w_o_self, w_in_b, w_out_b = params
    inner_width = w_q_cross.shape[1]
    cross_in = low(layer_norm(latent_rows, gains[0]))
    cross_kv_in = low(layer_norm(input_rows, gains[1]))
    queries = both_ways(matmul(cross_in, w_q_cross))
    paired = matmul(cross_kv_in, w_kv_cross.reshape(w_kv_cross.shape[0], 2 * inner_width))
    key_rows = both_ways(paired[:, :inner_width])
    value_rows = both_ways(paired[:, inner_width:])
    mixed = both_ways(attention(queries, key_rows, value_rows, latent_code, input_code))
    stream = latent_rows + low_back(matmul_out(mixed, w_o_cross))
    stream = feed_forward(stream, gains[2], w_in_a, w_out_a)
    self_in = low(layer_norm(stream, gains[3]))
    triple = matmul(self_in, w_qkv_self.reshape(w_qkv_self.shape[0], 3 * inner_width))
    self_queries = both_ways(triple[:, :inner_width])
    self_keys = both_ways(triple[:, inner_width:2 * inner_width])
    self_values = both_ways(triple[:, 2 * inner_width:])
    self_mixed = both_ways(attention(self_queries, self_keys, self_values, latent_code, self_code))
    stream = stream + low_back(matmul_out(self_mixed, w_o_self))
    return feed_forward(stream, gains[4], w_in_b, w_out_b)

def reference(latents, inputs, latent_group, latent_valid, input_group, input_valid, gains, w_q_cross, w_kv_cross, w_o_cross, w_in_a, w_out_a, w_qkv_self, w_o_self, w_in_b, w_out_b, out_grad):
    matrices = tuple((matrix.astype(jnp.float32) for matrix in (w_q_cross, w_kv_cross, w_o_cross, w_in_a, w_out_a, w_qkv_self, w_o_self, w_in_b, w_out_b)))
    shared = (gains.astype(jnp.float32),) + matrices

    def per_group(totals, slices):
        latent_rows, input_rows, group_lat, valid_lat, group_in, valid_in, cotangent = slices
        input_code = jnp.where(valid_in == 1, group_in, -1).astype(jnp.int32)
        self_code = jnp.where(valid_lat == 1, group_lat, -1).astype(jnp.int32)
        params = (latent_rows.astype(jnp.float32), input_rows.astype(jnp.float32)) + shared

        def closed(params_all):
            return forward(params_all, group_lat, input_code, self_code)
        result, pullback = jax.vjp(closed, params)
        grads = pullback(cotangent.astype(jnp.float32))[0]
        totals = tuple((running + grad_one for running, grad_one in zip(totals, grads[2:])))
        return (totals, (result.astype(jnp.bfloat16), grads[0], grads[1]))
    zeros_init = tuple((jnp.zeros_like(entry) for entry in shared))
    totals, stacked = lax.scan(per_group, zeros_init, (latents, inputs, latent_group, latent_valid, input_group, input_valid, out_grad))
    return (stacked[0], stacked[1], stacked[2], totals[0], totals[1], totals[2], totals[3], totals[4], totals[5], totals[6], totals[7], totals[8], totals[9])
```

```python
import functools
import types

import jax
import jax.numpy as jnp
from jax import lax
from jax.experimental import pallas as pl
from jax.experimental.pallas import tpu as pltpu
from jax.sharding import PartitionSpec as P

HEAD_DIM = 128


masked_fill = -1000.0
contract_last = (((1,), (1,)), ((), ()))


def layer_norm(values, gains_row):
    centred = values - jnp.mean(values, axis=-1, keepdims=True)
    variance = jnp.mean(centred * centred, axis=-1, keepdims=True)
    return centred * lax.rsqrt(variance + 1e-05) * gains_row


def norm_back(values, gains_row, cotangent):
    unused, pullback = jax.vjp(layer_norm, values, gains_row)
    return pullback(cotangent)


def out_product(left, right):
    return lax.dot_general(left, right, contract_last, preferred_element_type=jnp.float32)


def block_rows(item_count):
    if item_count > 1024 and item_count % 1024 == 0:
        return 1024
    return item_count


def head_sum(partial_sum):
    return lax.psum(partial_sum, "head")


def head_grad_sum(partial_sum):
    return lax.psum(partial_sum, "head")


def score_block(query_heads, key_heads, query_code, key_code):
    scores = jnp.einsum(
        "qhd,khd->hqk", query_heads, key_heads, preferred_element_type=jnp.float32
    ) * HEAD_DIM ** (-0.5)
    allowed = query_code[:, None] == key_code[None, :]
    return (jnp.where(allowed[None], scores, masked_fill), allowed)


def cycle_attend(queries, query_code, key_rows, value_rows, key_code):
    row_count = queries.shape[0]
    heads_local = queries.shape[1] // HEAD_DIM
    query_heads = queries.reshape(row_count, heads_local, HEAD_DIM)

    def stats_block(state_carry, block_data):
        running, totals = state_carry
        key_block, code_block = block_data
        key_heads = key_block.reshape(key_block.shape[0], heads_local, HEAD_DIM)
        scores, allowed = score_block(query_heads, key_heads, query_code, code_block)
        largest = jnp.maximum(running, jnp.max(scores, axis=-1))
        totals = totals * jnp.exp(running - largest) + jnp.sum(
            jnp.exp(scores - largest[:, :, None]), axis=-1
        )
        return ((largest, totals), None)

    stats_init = (
        jnp.full((heads_local, row_count), -jnp.inf, jnp.float32),
        jnp.zeros((heads_local, row_count), jnp.float32),
    )
    state_carry = stats_init
    key_piece = lax.all_gather(key_rows, "blk", axis=0, tiled=True)
    code_piece = lax.all_gather(key_code, "blk", axis=0, tiled=True)
    item_count = key_piece.shape[0]
    step_rows = block_rows(item_count)
    block_count = item_count // step_rows
    stacked = (
        key_piece.reshape(block_count, step_rows, key_piece.shape[1]),
        code_piece.reshape(block_count, step_rows),
    )
    state_carry, unused = lax.scan(stats_block, state_carry, stacked)
    running, totals = state_carry
    log_sums = running + jnp.log(totals)

    def one_block(accumulated, block_data):
        key_block, value_block, code_block = block_data
        key_heads = key_block.reshape(key_block.shape[0], heads_local, HEAD_DIM)
        value_heads = value_block.reshape(value_block.shape[0], heads_local, HEAD_DIM)
        scores, allowed = score_block(query_heads, key_heads, query_code, code_block)
        prob_rows = jnp.exp(scores - log_sums[:, :, None]).astype(jnp.bfloat16)
        accumulated = accumulated + jnp.einsum(
            "hqk,khd->qhd", prob_rows, value_heads, preferred_element_type=jnp.float32
        )
        return (accumulated, None)

    initial = jnp.zeros((row_count, heads_local, HEAD_DIM), jnp.float32)
    accumulated = initial
    key_piece = lax.all_gather(key_rows, "blk", axis=0, tiled=True)
    value_piece = lax.all_gather(value_rows, "blk", axis=0, tiled=True)
    code_piece = lax.all_gather(key_code, "blk", axis=0, tiled=True)
    item_count = key_piece.shape[0]
    step_rows = block_rows(item_count)
    block_count = item_count // step_rows
    stacked = (
        key_piece.reshape(block_count, step_rows, key_piece.shape[1]),
        value_piece.reshape(block_count, step_rows, value_piece.shape[1]),
        code_piece.reshape(block_count, step_rows),
    )
    accumulated, unused = lax.scan(one_block, accumulated, stacked)
    mixed = accumulated.reshape(row_count, heads_local * HEAD_DIM)
    return (mixed, log_sums)


def grad_parts(query_rows, grad_rows, query_code, log_sums, deltas, key_rows, value_rows, key_code):
    heads_local = query_rows.shape[1] // HEAD_DIM
    query_heads = query_rows.reshape(query_rows.shape[0], heads_local, HEAD_DIM)
    grad_heads = grad_rows.reshape(grad_rows.shape[0], heads_local, HEAD_DIM)
    key_heads = key_rows.reshape(key_rows.shape[0], heads_local, HEAD_DIM)
    value_heads = value_rows.reshape(value_rows.shape[0], heads_local, HEAD_DIM)
    scores, allowed = score_block(query_heads, key_heads, query_code, key_code)
    prob_rows = jnp.exp(scores - log_sums[:, :, None])
    grad_probs = jnp.einsum(
        "qhd,khd->hqk", grad_heads, value_heads, preferred_element_type=jnp.float32
    )
    grad_scores = jnp.where(
        allowed[None], prob_rows * (grad_probs - deltas[:, :, None]), 0.0
    ).astype(jnp.bfloat16)
    return (query_heads, grad_heads, key_heads, grad_scores, prob_rows)


def query_part(grad_scores, key_heads, row_shape):
    grad_query = jnp.einsum(
        "hqk,khd->qhd", grad_scores, key_heads, preferred_element_type=jnp.float32
    ) * HEAD_DIM ** (-0.5)
    return grad_query.reshape(row_shape)


def key_parts(grad_scores, prob_rows, query_heads, grad_heads, row_shape):
    grad_key = jnp.einsum(
        "hqk,qhd->khd", grad_scores, query_heads, preferred_element_type=jnp.float32
    ) * HEAD_DIM ** (-0.5)
    grad_value = jnp.einsum(
        "hqk,qhd->khd",
        prob_rows.astype(jnp.bfloat16),
        grad_heads,
        preferred_element_type=jnp.float32,
    )
    return (grad_key.reshape(row_shape), grad_value.reshape(row_shape))


def row_delta(grad_mixed, mixed):
    row_count = mixed.shape[0]
    heads_local = mixed.shape[1] // HEAD_DIM
    product = (grad_mixed.astype(jnp.float32) * mixed).reshape(row_count, heads_local, HEAD_DIM)
    return jnp.sum(product, axis=-1).T


def attend_back(queries, grad_mixed, query_code, log_sums, deltas, key_rows, value_rows, key_code):
    row_count = queries.shape[0]
    col_width = queries.shape[1]
    heads_local = col_width // HEAD_DIM
    all_keys, all_values, all_kcodes, all_queries, all_grads, all_qcodes = (
        lax.all_gather(key_rows, "blk", axis=0, tiled=True),
        lax.all_gather(value_rows, "blk", axis=0, tiled=True),
        lax.all_gather(key_code, "blk", axis=0, tiled=True),
        lax.all_gather(queries, "blk", axis=0, tiled=True),
        lax.all_gather(grad_mixed, "blk", axis=0, tiled=True),
        lax.all_gather(query_code, "blk", axis=0, tiled=True),
    )
    all_sums, all_deltas = (
        lax.all_gather(log_sums, "blk", axis=1, tiled=True),
        lax.all_gather(deltas, "blk", axis=1, tiled=True),
    )
    key_total = all_keys.shape[0]
    key_step = block_rows(key_total)
    key_blocks = key_total // key_step

    def own_queries(grad_query, block_data):
        key_block_rows, value_block_rows, code_block = block_data
        parts = grad_parts(
            queries,
            grad_mixed,
            query_code,
            log_sums,
            deltas,
            key_block_rows,
            value_block_rows,
            code_block,
        )
        return (grad_query + query_part(parts[3], parts[2], queries.shape), None)

    key_stack = (
        all_keys.reshape(key_blocks, key_step, col_width),
        all_values.reshape(key_blocks, key_step, col_width),
        all_kcodes.reshape(key_blocks, key_step),
    )
    grad_query, unused = lax.scan(
        own_queries, jnp.zeros((row_count, col_width), jnp.float32), key_stack
    )
    query_total = all_queries.shape[0]
    query_step = block_rows(query_total)
    query_blocks = query_total // query_step
    key_count = key_rows.shape[0]

    def own_keys(state_carry, block_data):
        grad_key, grad_value = state_carry
        query_block_rows, grad_block_rows, code_block, sums_block, deltas_block = block_data
        query_heads, grad_heads, key_heads, grad_scores, prob_rows = grad_parts(
            query_block_rows,
            grad_block_rows,
            code_block,
            sums_block,
            deltas_block,
            key_rows,
            value_rows,
            key_code,
        )
        part_key, part_value = key_parts(
            grad_scores, prob_rows, query_heads, grad_heads, key_rows.shape
        )
        return ((grad_key + part_key, grad_value + part_value), None)

    query_stack = (
        all_queries.reshape(query_blocks, query_step, col_width),
        all_grads.reshape(query_blocks, query_step, col_width),
        all_qcodes.reshape(query_blocks, query_step),
        all_sums.reshape(heads_local, query_blocks, query_step).transpose(1, 0, 2),
        all_deltas.reshape(heads_local, query_blocks, query_step).transpose(1, 0, 2),
    )
    zeros_keys = jnp.zeros((key_count, col_width), jnp.float32)
    (grad_key, grad_value), unused = lax.scan(own_keys, (zeros_keys, zeros_keys), query_stack)
    return (grad_query, grad_key, grad_value)


def mlp_forward(stream, gains_row, weight_in, weight_out):
    hidden_in = layer_norm(stream, gains_row).astype(jnp.bfloat16)
    hidden = jnp.dot(hidden_in, weight_in, preferred_element_type=jnp.float32)
    activated = jax.nn.gelu(hidden).astype(jnp.bfloat16)
    branch = head_sum(out_product(activated, weight_out))
    return (stream + branch, (hidden_in, hidden, activated))


def mlp_backward(stream, gains_row, weight_in, weight_out, saved, grad_stream):
    hidden_in, hidden, activated = saved
    grad_low = grad_stream.astype(jnp.bfloat16)
    grad_weight_out = jnp.einsum(
        "td,tf->df", grad_low, activated, preferred_element_type=jnp.float32
    )
    grad_activated = jnp.dot(grad_low, weight_out, preferred_element_type=jnp.float32)
    unused, gelu_back = jax.vjp(jax.nn.gelu, hidden)
    grad_hidden = gelu_back(grad_activated)[0].astype(jnp.bfloat16)
    grad_weight_in = jnp.einsum(
        "td,tf->df", hidden_in, grad_hidden, preferred_element_type=jnp.float32
    )
    grad_normed = head_grad_sum(out_product(grad_hidden, weight_in))
    grad_input, grad_gain = norm_back(stream, gains_row, grad_normed)
    return (grad_stream + grad_input, grad_gain, grad_weight_in, grad_weight_out)


def self_forward(stream, gains_row, weight_triple, weight_out, query_code, key_code):
    normed_low = layer_norm(stream, gains_row).astype(jnp.bfloat16)
    col_width = weight_triple.shape[2]
    triple = jnp.dot(
        normed_low,
        weight_triple.reshape(weight_triple.shape[0], 3 * col_width),
        preferred_element_type=jnp.float32,
    ).astype(jnp.bfloat16)
    queries = triple[:, :col_width]
    key_rows = triple[:, col_width : 2 * col_width]
    value_rows = triple[:, 2 * col_width :]
    mixed, log_sums = cycle_attend(queries, query_code, key_rows, value_rows, key_code)
    mixed_low = mixed.astype(jnp.bfloat16)
    branch = head_sum(out_product(mixed_low, weight_out))
    return (
        stream + branch,
        (normed_low, queries, key_rows, value_rows, mixed, mixed_low, log_sums),
    )


def self_backward(
    stream, gains_row, weight_triple, weight_out, saved, grad_stream, query_code, key_code
):
    normed_low, queries, key_rows, value_rows, mixed, mixed_low, log_sums = saved
    grad_low = grad_stream.astype(jnp.bfloat16)
    grad_weight_out = jnp.einsum(
        "td,ti->di", grad_low, mixed_low, preferred_element_type=jnp.float32
    )
    grad_mixed = jnp.dot(grad_low, weight_out, preferred_element_type=jnp.float32).astype(
        jnp.bfloat16
    )
    deltas = row_delta(grad_mixed, mixed)
    grad_query, grad_key, grad_value = attend_back(
        queries, grad_mixed, query_code, log_sums, deltas, key_rows, value_rows, key_code
    )
    grad_triple = jnp.concatenate([grad_query, grad_key, grad_value], axis=1).astype(jnp.bfloat16)
    grad_weight_triple = jnp.einsum(
        "td,tc->dc", normed_low, grad_triple, preferred_element_type=jnp.float32
    ).reshape(weight_triple.shape)
    grad_normed = head_grad_sum(
        out_product(grad_triple, weight_triple.reshape(weight_triple.shape[0], -1))
    )
    grad_input, grad_gain = norm_back(stream, gains_row, grad_normed)
    return (grad_stream + grad_input, grad_gain, grad_weight_triple, grad_weight_out)


def cross_forward(
    stream, input_rows, gains, weight_query, weight_pairs, weight_out, query_code, key_code
):
    latent_low = layer_norm(stream, gains[0]).astype(jnp.bfloat16)
    input_low = layer_norm(input_rows, gains[1]).astype(jnp.bfloat16)
    col_width = weight_query.shape[1]
    queries = jnp.dot(latent_low, weight_query, preferred_element_type=jnp.float32).astype(
        jnp.bfloat16
    )
    paired = jnp.dot(
        input_low,
        weight_pairs.reshape(weight_pairs.shape[0], 2 * col_width),
        preferred_element_type=jnp.float32,
    ).astype(jnp.bfloat16)
    key_rows = paired[:, :col_width]
    value_rows = paired[:, col_width:]
    mixed, log_sums = cycle_attend(queries, query_code, key_rows, value_rows, key_code)
    mixed_low = mixed.astype(jnp.bfloat16)
    branch = head_sum(out_product(mixed_low, weight_out))
    return (
        stream + branch,
        (latent_low, input_low, queries, key_rows, value_rows, mixed, mixed_low, log_sums),
    )


def cross_backward(
    stream,
    input_rows,
    gains,
    weight_query,
    weight_pairs,
    weight_out,
    saved,
    grad_stream,
    query_code,
    key_code,
):
    latent_low, input_low, queries, key_rows, value_rows, mixed, mixed_low, log_sums = saved
    grad_low = grad_stream.astype(jnp.bfloat16)
    grad_weight_out = jnp.einsum(
        "td,ti->di", grad_low, mixed_low, preferred_element_type=jnp.float32
    )
    grad_mixed = jnp.dot(grad_low, weight_out, preferred_element_type=jnp.float32).astype(
        jnp.bfloat16
    )
    deltas = row_delta(grad_mixed, mixed)
    grad_query, grad_key, grad_value = attend_back(
        queries, grad_mixed, query_code, log_sums, deltas, key_rows, value_rows, key_code
    )
    grad_query_low = grad_query.astype(jnp.bfloat16)
    grad_pairs = jnp.concatenate([grad_key, grad_value], axis=1).astype(jnp.bfloat16)
    grad_weight_query = jnp.einsum(
        "td,tc->dc", latent_low, grad_query_low, preferred_element_type=jnp.float32
    )
    grad_weight_pairs = jnp.einsum(
        "td,tc->dc", input_low, grad_pairs, preferred_element_type=jnp.float32
    ).reshape(weight_pairs.shape)
    latent_part = out_product(grad_query_low, weight_query)
    input_part = out_product(grad_pairs, weight_pairs.reshape(weight_pairs.shape[0], -1))
    latent_normed, input_normed = lax.psum((latent_part, input_part), "head")
    grad_latent, gain_zero = norm_back(stream, gains[0], latent_normed)
    grad_inputs, gain_one = norm_back(input_rows, gains[1], input_normed)
    return (
        grad_stream + grad_latent,
        grad_inputs,
        gain_zero,
        gain_one,
        grad_weight_query,
        grad_weight_pairs,
        grad_weight_out,
    )


def per_device(
    latents,
    inputs,
    latent_group,
    latent_valid,
    input_group,
    input_valid,
    gains,
    w_q_cross,
    w_kv_cross,
    w_o_cross,
    w_in_a,
    w_out_a,
    w_qkv_self,
    w_o_self,
    w_in_b,
    w_out_b,
    out_grad,
):
    start_stream = latents[0].astype(jnp.float32)
    input_rows = inputs[0].astype(jnp.float32)
    query_code = latent_group[0].astype(jnp.bfloat16)
    input_code = jnp.where(input_valid[0] == 1, input_group[0], -1).astype(jnp.bfloat16)
    self_code = jnp.where(latent_valid[0] == 1, latent_group[0], -1).astype(jnp.bfloat16)
    cross_stream, cross_saved = cross_forward(
        start_stream, input_rows, gains, w_q_cross, w_kv_cross, w_o_cross, query_code, input_code
    )
    middle_stream, first_saved = mlp_forward(cross_stream, gains[2], w_in_a, w_out_a)
    self_stream, self_saved = self_forward(
        middle_stream, gains[3], w_qkv_self, w_o_self, query_code, self_code
    )
    final_stream, second_saved = mlp_forward(self_stream, gains[4], w_in_b, w_out_b)
    grad_stream = out_grad[0].astype(jnp.float32)
    grad_stream, gain_four, grad_in_b, grad_out_b = mlp_backward(
        self_stream, gains[4], w_in_b, w_out_b, second_saved, grad_stream
    )
    grad_stream, gain_three, grad_qkv_self, grad_o_self = self_backward(
        middle_stream,
        gains[3],
        w_qkv_self,
        w_o_self,
        self_saved,
        grad_stream,
        query_code,
        self_code,
    )
    grad_stream, gain_two, grad_in_a, grad_out_a = mlp_backward(
        cross_stream, gains[2], w_in_a, w_out_a, first_saved, grad_stream
    )
    grad_stream, grad_inputs, gain_zero, gain_one, grad_q_cross, grad_kv_cross, grad_o_cross = (
        cross_backward(
            start_stream,
            input_rows,
            gains,
            w_q_cross,
            w_kv_cross,
            w_o_cross,
            cross_saved,
            grad_stream,
            query_code,
            input_code,
        )
    )
    gain_terms = jnp.stack([gain_zero, gain_one, gain_two, gain_three, gain_four], axis=1)
    (
        sum_gains,
        sum_q_cross,
        sum_kv_cross,
        sum_o_cross,
        sum_in_a,
        sum_out_a,
        sum_qkv_self,
        sum_o_self,
        sum_in_b,
        sum_out_b,
    ) = (
        lax.psum_scatter(gain_terms, ("group", "blk"), scatter_dimension=0, tiled=True),
        lax.psum_scatter(grad_q_cross, ("group", "blk"), scatter_dimension=0, tiled=True),
        lax.psum_scatter(grad_kv_cross, ("group", "blk"), scatter_dimension=0, tiled=True),
        lax.psum_scatter(grad_o_cross, ("group", "blk"), scatter_dimension=0, tiled=True),
        lax.psum_scatter(grad_in_a, ("group", "blk"), scatter_dimension=0, tiled=True),
        lax.psum_scatter(grad_out_a, ("group", "blk"), scatter_dimension=0, tiled=True),
        lax.psum_scatter(grad_qkv_self, ("group", "blk"), scatter_dimension=0, tiled=True),
        lax.psum_scatter(grad_o_self, ("group", "blk"), scatter_dimension=0, tiled=True),
        lax.psum_scatter(grad_in_b, ("group", "blk"), scatter_dimension=0, tiled=True),
        lax.psum_scatter(grad_out_b, ("group", "blk"), scatter_dimension=0, tiled=True),
    )
    (
        full_gains,
        full_q_cross,
        full_kv_cross,
        full_o_cross,
        full_in_a,
        full_out_a,
        full_qkv_self,
        full_o_self,
        full_in_b,
        full_out_b,
    ) = (
        lax.all_gather(sum_gains, ("group", "blk"), axis=0, tiled=True),
        lax.all_gather(sum_q_cross, ("group", "blk"), axis=0, tiled=True),
        lax.all_gather(sum_kv_cross, ("group", "blk"), axis=0, tiled=True),
        lax.all_gather(sum_o_cross, ("group", "blk"), axis=0, tiled=True),
        lax.all_gather(sum_in_a, ("group", "blk"), axis=0, tiled=True),
        lax.all_gather(sum_out_a, ("group", "blk"), axis=0, tiled=True),
        lax.all_gather(sum_qkv_self, ("group", "blk"), axis=0, tiled=True),
        lax.all_gather(sum_o_self, ("group", "blk"), axis=0, tiled=True),
        lax.all_gather(sum_in_b, ("group", "blk"), axis=0, tiled=True),
        lax.all_gather(sum_out_b, ("group", "blk"), axis=0, tiled=True),
    )
    return (
        final_stream.astype(jnp.bfloat16)[None],
        grad_stream[None],
        grad_inputs[None],
        full_gains.T,
        full_q_cross,
        full_kv_cross,
        full_o_cross,
        full_in_a,
        full_out_a,
        full_qkv_self,
        full_o_self,
        full_in_b,
        full_out_b,
    )


MESH = pl.DeviceIdType.MESH
bf16, f32 = jnp.bfloat16, jnp.float32
LANES = 128
SCALE = HEAD_DIM**-0.5
GELU_A = 0.7978845608028654
GELU_B = 0.044715


def dot_nn(a, b):
    return jnp.dot(a, b, preferred_element_type=f32)


def dot_nt(a, b):
    return lax.dot_general(a, b, (((1,), (1,)), ((), ())), preferred_element_type=f32)


def dot_tn(a, b):
    return lax.dot_general(a, b, (((0,), (0,)), ((), ())), preferred_element_type=f32)


def norm_rows(x):
    c = x - jnp.mean(x, axis=-1, keepdims=True)
    rstd = lax.rsqrt(jnp.mean(c * c, axis=-1, keepdims=True) + 1e-05)
    return c * rstd, rstd


def gelu_both(u):
    u2 = u * u
    t = jnp.tanh(GELU_A * u * (1.0 + GELU_B * u2))
    half = 0.5 * (1.0 + t)
    slope = half + 0.5 * u * (1.0 - t * t) * (GELU_A * (1.0 + 3.0 * GELU_B * u2))
    return u * half, slope


def loop(start, stop, body):
    def step(k, carry):
        body(k)
        return carry

    lax.fori_loop(start, stop, step, 0)


def block_kernel(names, T, I, D, C, F, CH, *refs):
    r = types.SimpleNamespace(**dict(zip(names, refs, strict=True)))
    NCH = T // CH
    ICH = I // CH
    HL = C // HEAD_DIM
    g = lax.axis_index("group")
    b = lax.axis_index("blk")
    h = lax.axis_index("head")
    is_mid = (h == 1) | (h == 2)
    is_end = jnp.logical_not(is_mid)
    at_pair = (g, b, h ^ 1)
    at_mid = (g, b, 3 - h)
    at_y = (g, 1 - b, h)
    at_x = (g ^ 2, b, h)
    at_core = (g ^ 1, b, h)
    core = g % 2
    xi = g // 2
    gains = r.gains

    def rows(c, n=CH):
        return pl.ds(pl.multiple_of(c * n, n), n)

    def remote(src, dst, send_sem, recv_sem, where):
        return pltpu.make_async_remote_copy(
            src_ref=src, dst_ref=dst, send_sem=send_sem, recv_sem=recv_sem, device_id=where, device_id_type=MESH
        )

    bar = pltpu.get_barrier_semaphore()
    for where in (at_pair, at_y, at_x, at_core):
        pl.semaphore_signal(bar, inc=1, device_id=where, device_id_type=MESH)

    @pl.when(is_mid)
    def _():
        pl.semaphore_signal(bar, inc=1, device_id=at_mid, device_id_type=MESH)

    loads = {}

    def load(src, dst, name):
        cp = pltpu.make_async_copy(src, dst, r.load_sem.at[len(loads)])
        cp.start()
        loads[name] = cp

    load(r.inputs, r.inp, "inp")
    load(r.w_kv_c, r.wkvc, "wkvc")
    load(r.latents, r.lat, "lat")
    load(r.w_q_c, r.wqc, "wqc")
    load(r.w_o_c, r.woc, "woc")
    load(r.w_in_a, r.wina, "wina")
    load(r.w_out_a, r.wouta, "wouta")
    load(r.w_qkv_s, r.wqkvs, "wqkvs")
    load(r.w_o_s, r.wos, "wos")
    load(r.w_in_b, r.winb, "winb")
    load(r.w_out_b, r.woutb, "woutb")
    load(r.out_grad, r.r4, "r4")

    lg = r.latent_group[...]
    ic = jnp.where(r.input_valid[...] == 1, r.input_group[...], -1).astype(f32)
    sc = jnp.where(r.latent_valid[...] == 1, lg, -1).astype(f32)
    lgf = lg.astype(f32)
    r.codes[:, 0:I] = jnp.broadcast_to(ic, (8, I))
    r.codes[:, I : I + T] = jnp.broadcast_to(sc, (8, T))
    r.codes[:, I + T : I + 2 * T] = jnp.broadcast_to(lgf, (8, T))

    def make_columns(line, dst):
        for j in range(T // LANES):
            dst[pl.ds(j * LANES, LANES), :] = jnp.transpose(
                jnp.broadcast_to(line[:, j * LANES : (j + 1) * LANES], (LANES, LANES))
            )

    make_columns(lgf, r.qcol)
    r.dg[...] = jnp.zeros_like(r.dg)

    @pl.when(is_mid)
    def _():
        pl.semaphore_wait(bar, 5)

    @pl.when(is_end)
    def _():
        pl.semaphore_wait(bar, 4)

    def to_y(src, dst, k):
        return remote(src, dst, r.y_snd.at[k], r.y_rcv.at[k], at_y)

    codes_cp = to_y(r.codes, r.codes_o, 0)
    codes_cp.start()

    def cp_in(p, c):
        return remote(r.part.at[p, rows(c)], r.rin.at[p, rows(c)], r.ar_snd.at[p, c], r.ar_in.at[p, c], at_pair)

    def cp_mid(p, c):
        return remote(r.part.at[p, rows(c)], r.rmid.at[p, rows(c)], r.ar_snd.at[p, c], r.ar_mid.at[p, c], at_mid)

    def cp_tot(p, c):
        return remote(r.rin.at[p, rows(c)], r.rin.at[p, rows(c)], r.ar_tot.at[p, c], r.ar_in.at[p, c], at_pair)

    def ar_send(p, c):
        @pl.when(is_end)
        def _():
            cp_in(p, c).start()

    def ar_put(p, c, value):
        r.part[p, rows(c)] = value.astype(bf16)
        ar_send(p, c)

    def ar_b(p, c):
        @pl.when(is_mid)
        def _():
            cp_in(p, c).wait_recv()
            total = r.part[p, rows(c)].astype(f32) + r.rin[p, rows(c)].astype(f32)
            r.part[p, rows(c)] = total.astype(bf16)
            cp_mid(p, c).start()

    def ar_c(p, c, prev=None):
        @pl.when(is_mid)
        def _():
            cp_mid(p, c).wait_recv()
            cp_mid(p, c).wait_send()
            total = r.part[p, rows(c)].astype(f32) + r.rmid[p, rows(c)].astype(f32)
            r.rin[p, rows(c)] = total.astype(bf16)
            if prev is not None:
                cp_tot(prev, c).wait_send()
            cp_tot(p, c).start()

        @pl.when(is_end)
        def _():
            cp_in(p, c).wait_send()
            cp_tot(p, c).wait_recv()

    def total_of(p, c):
        return r.rin[p, rows(c)].astype(f32)

    half, quarter, eighth, piece = D // 2, D // 4, D // 8, D // 16
    own = core * half
    p_own = own + xi * eighth
    p_oth = own + (1 - xi) * eighth
    q_base = own + quarter
    q_own = q_base + b * eighth
    q_oth = q_base + (1 - b) * eighth
    p_fin, p_fin_oth = p_own + b * piece, p_own + (1 - b) * piece
    q_fin, q_fin_oth = q_own + xi * piece, q_own + (1 - xi) * piece

    def span(start, n):
        return pl.ds(pl.multiple_of(start, piece), n)

    class Job:
        def __init__(self, index, w, slot, out, parts):
            self.j, self.w, self.s, self.out, self.parts = index, w, slot, out, parts

        def tile(self, t):
            col = 0
            rw = rows(t, LANES)
            for lhs, rhs in self.parts:
                n = rhs.shape[1]
                self.w[rw, col : col + n] = dot_tn(lhs[:, rw], rhs[...]).astype(bf16)
                col += n

        def cp(self, k, src, dst, where):
            return remote(src, dst, r.j_snd.at[self.j, k], r.j_rcv.at[self.j, k], where)

        def cp_core(self):
            return self.cp(0, self.w.at[span((1 - core) * half, half)], r.rc.at[self.s], at_core)

        def cp_p1(self):
            return self.cp(1, self.w.at[span(p_oth, eighth)], r.r1p.at[self.s], at_x)

        def cp_q1(self):
            return self.cp(2, self.w.at[span(q_oth, eighth)], r.r1q.at[self.s], at_y)

        def cp_p2(self):
            return self.cp(3, self.w.at[span(p_fin_oth, piece)], r.r2p.at[self.s], at_y)

        def cp_q2(self):
            return self.cp(4, self.w.at[span(q_fin_oth, piece)], r.r2q.at[self.s], at_x)

        def cp_p3(self):
            return self.cp(5, self.w.at[span(p_fin, piece)], self.out.at[span(p_fin, piece)], at_y)

        def cp_q3(self):
            return self.cp(6, self.w.at[span(q_fin, piece)], self.out.at[span(q_fin, piece)], at_x)

        def cp_p4(self):
            return self.cp(7, self.out.at[span(p_own, eighth)], self.out.at[span(p_own, eighth)], at_x)

        def cp_q4(self):
            return self.cp(8, self.out.at[span(q_own, eighth)], self.out.at[span(q_own, eighth)], at_y)

        def cp_all(self):
            return self.cp(9, self.out.at[span(own, half)], self.out.at[span(own, half)], at_core)

        def cp_keep(self):
            return (
                pltpu.make_async_copy(
                    self.w.at[span(p_fin, piece)], self.out.at[span(p_fin, piece)], r.j_own.at[self.j, 0]
                ),
                pltpu.make_async_copy(
                    self.w.at[span(q_fin, piece)], self.out.at[span(q_fin, piece)], r.j_own.at[self.j, 1]
                ),
            )

        def add(self, start, n, other):
            rw = span(start, n)
            self.w[rw] = (self.w[rw].astype(f32) + other[...].astype(f32)).astype(bf16)

        def start(self):
            self.cp_core().start()

        def s1(self):
            self.cp_core().wait_recv()
            self.add(p_oth, eighth, r.rc.at[self.s, span(p_oth - own, eighth)])
            self.cp_p1().start()
            self.add(q_oth, eighth, r.rc.at[self.s, span(q_oth - own, eighth)])
            self.cp_q1().start()
            self.add(p_own, eighth, r.rc.at[self.s, span(p_own - own, eighth)])
            self.add(q_own, eighth, r.rc.at[self.s, span(q_own - own, eighth)])

        def s2(self):
            self.cp_p1().wait_recv()
            self.add(p_own, eighth, r.r1p.at[self.s])
            self.cp_p2().start()
            self.cp_q1().wait_recv()
            self.add(q_own, eighth, r.r1q.at[self.s])
            self.cp_q2().start()

        def s3(self):
            self.cp_p2().wait_recv()
            self.add(p_fin, piece, r.r2p.at[self.s])
            self.cp_p3().start()
            self.cp_q2().wait_recv()
            self.add(q_fin, piece, r.r2q.at[self.s])
            self.cp_q3().start()
            for cp in self.cp_keep():
                cp.start()

        def s4(self):
            for cp in self.cp_keep():
                cp.wait()
            self.cp_p3().wait_recv()
            self.cp_p4().start()
            self.cp_q3().wait_recv()
            self.cp_q4().start()
            for cp in (self.cp_core(), self.cp_p1(), self.cp_q1(), self.cp_p2(), self.cp_q2(), self.cp_p3(), self.cp_q3()):
                cp.wait_send()

        def s5(self):
            self.cp_p4().wait_recv()
            self.cp_q4().wait_recv()
            self.cp_all().start()
            self.cp_p4().wait_send()
            self.cp_q4().wait_send()

        def s6(self):
            self.cp_all().wait()

    job_out_b = Job(0, r.woutb, 0, r.g_out_b, [(r.r4, r.z2)])
    job_in_b = Job(1, r.winb, 1, r.g_in_b, [(r.h2, r.du2)])
    job_self = Job(2, r.wj, 2, r.g_self, [(r.cs, r.dqkv), (r.ra, r.o_s)])
    job_out_a = Job(3, r.woutb, 0, r.g_out_a, [(r.rb, r.z1)])
    job_in_a = Job(4, r.winb, 1, r.g_in_a, [(r.h1, r.du1)])
    job_cross = Job(5, r.wj, 2, r.g_cross, [(r.bn, r.dkv), (r.an, r.dq), (r.ra, r.o_c)])

    def norm_out(x, gain_row, out, rstd_out, rw):
        xhat, rstd = norm_rows(x)
        rstd_out[rw] = jnp.broadcast_to(rstd, (rstd.shape[0], LANES))
        low = (xhat * gains[gain_row : gain_row + 1, :]).astype(bf16)
        out[rw] = low
        return low

    def norm_grad(cot, low_ref, gain_row, rstd_ref, rw):
        gain = gains[gain_row : gain_row + 1, :]
        xhat = low_ref[rw].astype(f32) * (1.0 / gain)
        scaled = cot * gain
        mean_one = jnp.mean(scaled, axis=-1, keepdims=True)
        mean_two = jnp.mean(scaled * xhat, axis=-1, keepdims=True)
        r.dg[gain_row : gain_row + 1, :] += jnp.sum(cot * xhat, axis=0, keepdims=True)
        return rstd_ref[rw, 0:1] * (scaled - mean_one - xhat * mean_two)

    loads["inp"].wait()
    loads["wkvc"].wait()

    def kv_chunk(k):
        rw = rows(k, LANES)
        low = norm_out(r.inp[rw].astype(f32), 1, r.bn, r.rs1, rw)
        r.kv[rw] = dot_nn(low, r.wkvc[...]).astype(bf16)

    loop(0, I // LANES, kv_chunk)
    kv_cp = to_y(r.kv.at[pl.ds(0, I)], r.kv.at[pl.ds(I, I)], 1)
    kv_cp.start()
    loads["lat"].wait()
    loads["wqc"].wait()

    def q_chunk(k):
        rw = rows(k, LANES)
        low = norm_out(r.lat[rw].astype(f32), 0, r.an, r.rs0, rw)
        r.q[rw] = dot_nn(low, r.wqc[...]).astype(bf16)

    loop(0, T // LANES, q_chunk)
    codes_cp.wait()
    make_columns(r.codes_o[0:1, I + T : I + 2 * T], r.qcol_o)
    kv_cp.wait()
    loads["woc"].wait()

    def attend_chunk(k, q_ref, kv_ref, p_ref, o_ref, start, n):
        rw = rows(k)
        kc = jnp.concatenate([r.codes[0:1, start : start + n], r.codes_o[0:1, start : start + n]], axis=1)
        allowed = r.qcol[rw, 0:1] == kc
        for hd in range(HL):
            cols = slice(hd * HEAD_DIM, (hd + 1) * HEAD_DIM)
            vcols = slice(C + hd * HEAD_DIM, C + (hd + 1) * HEAD_DIM)
            s = jnp.where(allowed, dot_nt(q_ref[rw, cols], kv_ref[:, cols]) * SCALE, masked_fill)
            e = jnp.exp(s - jnp.max(s, axis=-1, keepdims=True))
            p = (e * (1.0 / jnp.sum(e, axis=-1, keepdims=True))).astype(bf16)
            p_ref[hd, rw, :] = p
            o_ref[rw, cols] = dot_nn(p, kv_ref[:, vcols]).astype(bf16)

    def cross_chunk(k):
        attend_chunk(k, r.q, r.kv, r.p_c, r.o_c, 0, I)
        ar_put(0, k, dot_nt(r.o_c[rows(k)], r.woc[...]))

        @pl.when(k >= 4)
        def _():
            ar_b(0, k - 4)

    loop(0, NCH, cross_chunk)
    back_cross = [
        to_y(r.p_c.at[:, :, pl.ds(I, I)], r.pr_c, 2), to_y(r.q, r.qr_c, 3), to_y(r.o_c, r.or_c, 4),
    ]
    for cp in back_cross:
        cp.start()
    loads["wina"].wait()
    loads["wouta"].wait()

    def first_chunk(m):
        @pl.when((m >= 2) & (m < NCH - 2))
        def _():
            ar_b(0, m + 2)

        ar_c(0, m)
        rw = rows(m)
        x = r.lat[rw].astype(f32) + total_of(0, m)
        r.xs[rw] = x
        low = norm_out(x, 2, r.h1, r.rs2, rw)
        z, slope = gelu_both(dot_nn(low, r.wina[...]))
        z = z.astype(bf16)
        r.z1[rw] = z
        r.s1[rw] = slope.astype(bf16)
        ar_put(1, m, dot_nt(z, r.wouta[...]))

        @pl.when(m >= NCH - 2)
        def _():
            ar_b(1, m + 2 - NCH)

    loop(0, NCH, first_chunk)
    loads["wqkvs"].wait()
    loads["wos"].wait()

    def kv2_cp(c):
        return remote(r.kv2.at[rows(c)], r.kv2.at[rows(c + NCH)], r.kv_snd.at[c], r.kv_rcv.at[c], at_y)

    def second_chunk(m):
        @pl.when(m < NCH - 2)
        def _():
            ar_b(1, m + 2)

        ar_c(1, m, 0)
        rw = rows(m)
        x = r.xs[rw] + total_of(1, m)
        r.xs[rw] = x
        low = norm_out(x, 3, r.cs, r.rs3, rw)
        qkv = dot_nn(low, r.wqkvs[...]).astype(bf16)
        r.q2[rw] = qkv[:, :C]
        r.kv2[rw] = qkv[:, C:]
        kv2_cp(m).start()

    loop(0, NCH, second_chunk)
    loop(0, NCH, lambda c: kv2_cp(c).wait())

    def self_chunk(k):
        attend_chunk(k, r.q2, r.kv2, r.p_s, r.o_s, I, T)
        ar_put(0, k, dot_nt(r.o_s[rows(k)], r.wos[...]))

        @pl.when(k >= 4)
        def _():
            ar_b(0, k - 4)

    loop(0, NCH, self_chunk)
    back_self = [
        to_y(r.p_s.at[:, :, pl.ds(T, T)], r.pr_s, 5), to_y(r.q2, r.qr_s, 6), to_y(r.o_s, r.or_s, 7),
    ]
    for cp in back_self:
        cp.start()
    loads["winb"].wait()
    loads["woutb"].wait()
    loads["r4"].wait()

    def third_chunk(m):
        @pl.when((m >= 2) & (m < NCH - 2))
        def _():
            ar_b(0, m + 2)

        ar_c(0, m, 1)
        rw = rows(m)
        x = r.xs[rw] + total_of(0, m)
        r.xs[rw] = x
        low = norm_out(x, 4, r.h2, r.rs4, rw)
        z, slope = gelu_both(dot_nn(low, r.winb[...]))
        z = z.astype(bf16)
        r.z2[rw] = z
        du = (dot_nn(r.r4[rw], r.woutb[...]) * slope).astype(bf16)
        r.du2[rw] = du
        ar_put(1, m, dot_nt(du, r.winb[...]))
        r.part[2, rw] = dot_nt(z, r.woutb[...]).astype(bf16)

        @pl.when(m >= NCH - 2)
        def _():
            ar_b(1, m + 2 - NCH)

    loop(0, NCH, third_chunk)

    def d_o_cp(k, c):
        return remote(r.do.at[k, rows(c)], r.do_o.at[k, rows(c)], r.do_snd.at[k, c], r.do_rcv.at[k, c], at_y)

    def fifth_chunk(m):
        @pl.when(m < NCH - 2)
        def _():
            ar_b(1, m + 2)

        ar_c(1, m, 0)
        rw = rows(m)
        dx = r.r4[rw].astype(f32) + norm_grad(total_of(1, m), r.h2, 4, r.rs4, rw)
        r.dxs[rw] = dx
        low = dx.astype(bf16)
        r.ra[rw] = low
        r.do[0, rw] = dot_nn(low, r.wos[...]).astype(bf16)
        d_o_cp(0, m).start()

        @pl.when(m < NCH // 2)
        def _():
            job_out_b.tile(2 * m)
            job_out_b.tile(2 * m + 1)

        @pl.when(m == NCH // 2)
        def _():
            job_out_b.start()

        @pl.when(m >= NCH // 2)
        def _():
            job_in_b.tile(2 * m - NCH)
            job_in_b.tile(2 * m + 1 - NCH)

    loop(0, NCH, fifth_chunk)
    job_in_b.start()

    def late_sends(lo, hi):
        loop(lo, hi, lambda c: ar_send(2, c))

    def late_out(c):
        ar_c(2, c)
        rw = rows(c)
        r.part[2, rw] = (r.xs[rw] + total_of(2, c)).astype(bf16)

    late_sends(0, NCH // 2)

    QB = 128

    def attend_back(hd, do, do_o, q_ref, qr_ref, kv_ref, p_ref, pr_ref, o_ref, or_ref, n, start, dq_ref, dq_col, dkv_ref, dkv_col, between, waits):
        cols = slice(hd * HEAD_DIM, (hd + 1) * HEAD_DIM)
        vcols = slice(C + hd * HEAD_DIM, C + (hd + 1) * HEAD_DIM)

        def own_queries(k):
            rw = rows(k, QB)
            grad = do[rw, cols]
            delta = jnp.sum(grad.astype(f32) * o_ref[rw, cols].astype(f32), axis=-1, keepdims=True)
            kc = jnp.concatenate([r.codes[0:1, start : start + n], r.codes_o[0:1, start : start + n]], axis=1)
            diff = dot_nt(grad, kv_ref[:, vcols]) - delta
            ds = jnp.where(r.qcol[rw, 0:1] == kc, p_ref[hd, rw, :].astype(f32) * diff, 0.0).astype(bf16)
            r.ds[rw, 0:n] = ds[:, 0:n]
            dq_ref[rw, dq_col + hd * HEAD_DIM : dq_col + (hd + 1) * HEAD_DIM] = (
                dot_nn(ds, kv_ref[:, cols]) * SCALE
            ).astype(bf16)

        loop(0, T // QB, own_queries)
        between()
        for wait in waits:
            wait()

        def other_queries(k):
            rw = rows(k, QB)
            grad = do_o[rw, cols]
            delta = jnp.sum(grad.astype(f32) * or_ref[rw, cols].astype(f32), axis=-1, keepdims=True)
            diff = dot_nt(grad, kv_ref[0:n, vcols]) - delta
            allowed = r.qcol_o[rw, 0:1] == r.codes[0:1, start : start + n]
            ds = jnp.where(allowed, pr_ref[hd, rw, :].astype(f32) * diff, 0.0).astype(bf16)
            r.ds[rows(k + T // QB, QB), 0:n] = ds

        loop(0, T // QB, other_queries)
        dk = dot_tn(r.ds[0:T, 0:n], q_ref[:, cols]) + dot_tn(r.ds[T : 2 * T, 0:n], qr_ref[:, cols])
        dkv_ref[:, dkv_col + hd * HEAD_DIM : dkv_col + (hd + 1) * HEAD_DIM] = (dk * SCALE).astype(bf16)
        dv = dot_tn(p_ref[hd, :, 0:n], do[:, cols]) + dot_tn(pr_ref[hd], do_o[:, cols])
        dkv_ref[:, dkv_col + C + hd * HEAD_DIM : dkv_col + C + (hd + 1) * HEAD_DIM] = dv.astype(bf16)

    def wait_d_o(k):
        loop(0, NCH, lambda c: d_o_cp(k, c).wait())

    for hd in range(HL):
        waits = [] if hd else [functools.partial(wait_d_o, 0)] + [cp.wait for cp in back_self]
        attend_back(
            hd, r.do.at[0], r.do_o.at[0], r.q2, r.qr_s, r.kv2, r.p_s, r.pr_s, r.o_s, r.or_s, T, I, r.dqkv, 0, r.dqkv, C,
            (lambda: None) if hd else job_out_b.s1, waits,
        )
        if hd == 0:
            ar_b(2, 0)
            ar_b(2, 1)
            job_in_b.s1()

    def sixth_put(k):
        ar_put(0, k, dot_nt(r.dqkv[rows(k)], r.wqkvs[...]))

    loop(0, NCH, sixth_put)
    job_out_b.s2()
    loop(2, NCH // 2, lambda c: ar_b(2, c))
    job_in_b.s2()
    loop(0, 2, lambda c: ar_b(0, c))

    def sixth_chunk(m):
        @pl.when(m < NCH - 2)
        def _():
            ar_b(0, m + 2)

        ar_c(0, m, 1)
        rw = rows(m)
        dx = r.dxs[rw] + norm_grad(total_of(0, m), r.cs, 3, r.rs3, rw)
        r.dxs[rw] = dx
        low = dx.astype(bf16)
        r.rb[rw] = low
        du = (dot_nn(low, r.wouta[...]) * r.s1[rw].astype(f32)).astype(bf16)
        r.du1[rw] = du
        ar_put(1, m, dot_nt(du, r.wina[...]))

        @pl.when(m >= NCH - 2)
        def _():
            ar_b(1, m + 2 - NCH)

        @pl.when(m < NCH // 2)
        def _():
            late_out(m)
            job_self.tile(2 * m)
            job_self.tile(2 * m + 1)

        @pl.when(m == 1)
        def _():
            job_out_b.s3()

        @pl.when(m == 2)
        def _():
            job_in_b.s3()

        @pl.when(m == NCH // 2)
        def _():
            job_self.start()
            job_out_b.s4()

        @pl.when(m == NCH // 2 + 1)
        def _():
            job_in_b.s4()

        @pl.when(m == NCH // 2 + 2)
        def _():
            job_self.s1()
            job_out_b.s5()

        @pl.when(m == NCH // 2 + 3)
        def _():
            job_in_b.s5()

    loop(0, NCH, sixth_chunk)
    late_rows = [pl.ds(0, T // 2), pl.ds(T // 2, T // 2)]
    late_cps = [
        pltpu.make_async_copy(r.part.at[2, rw], r.latents_out.at[rw], r.out_sem.at[2 + k])
        for k, rw in enumerate(late_rows)
    ]
    late_cps[0].start()

    def seventh_chunk(m):
        @pl.when(m < NCH - 2)
        def _():
            ar_b(1, m + 2)

        @pl.when(is_mid & (m < NCH // 2))
        def _():
            cp_tot(2, m).wait_send()

        ar_c(1, m, 0)
        rw = rows(m)
        dx = r.dxs[rw] + norm_grad(total_of(1, m), r.h1, 2, r.rs2, rw)
        r.dxs[rw] = dx
        low = dx.astype(bf16)
        r.ra[rw] = low
        r.do[1, rw] = dot_nn(low, r.woc[...]).astype(bf16)
        d_o_cp(1, m).start()

        @pl.when(m < NCH // 2)
        def _():
            job_out_a.tile(2 * m)
            job_out_a.tile(2 * m + 1)

        @pl.when(m == 0)
        def _():
            job_out_b.s6()
            job_self.s2()

        @pl.when(m == 1)
        def _():
            job_in_b.s6()

        @pl.when(m == 2)
        def _():
            job_self.s3()

        @pl.when(m == NCH // 2)
        def _():
            job_out_a.start()
            job_self.s4()

        @pl.when(m >= NCH // 2)
        def _():
            job_in_a.tile(2 * m - NCH)
            job_in_a.tile(2 * m + 1 - NCH)

        @pl.when(m == NCH // 2 + 2)
        def _():
            job_out_a.s1()
            job_self.s5()

    loop(0, NCH, seventh_chunk)
    job_in_a.start()
    late_sends(NCH // 2, NCH)

    for hd in range(HL):
        waits = [] if hd else [functools.partial(wait_d_o, 1)] + [cp.wait for cp in back_cross]
        attend_back(
            hd, r.do.at[1], r.do_o.at[1], r.q, r.qr_c, r.kv, r.p_c, r.pr_c, r.o_c, r.or_c, I, 0, r.dq, 0, r.dkv, 0,
            (lambda: None) if hd else job_in_a.s1, waits,
        )
        if hd == 0:
            ar_b(2, NCH // 2)
            ar_b(2, NCH // 2 + 1)
            job_out_a.s2()

    late_cps[0].wait()
    loop(0, ICH, lambda k: ar_put(2, k, dot_nt(r.dkv[rows(k)], r.wkvc[...])))
    loop(0, NCH, lambda k: ar_put(0, k, dot_nt(r.dq[rows(k)], r.wqc[...])))
    job_self.s6()
    loop(0, D // LANES, job_cross.tile)
    job_cross.start()
    loop(NCH // 2 + 2, NCH, lambda c: ar_b(2, c))
    loop(0, 2, lambda c: ar_b(2, c))
    job_in_a.s2()
    job_out_a.s3()

    def input_chunk(m):
        @pl.when(m < ICH - 2)
        def _():
            ar_b(2, m + 2)

        @pl.when(m >= ICH - 2)
        def _():
            ar_b(0, m + 2 - ICH)

        ar_c(2, m)
        rw = rows(m)
        r.gin[rw] = norm_grad(total_of(2, m), r.bn, 1, r.rs1, rw)

    loop(0, ICH, input_chunk)
    job_cross.s1()
    job_in_a.s3()
    job_out_a.s4()

    def last_chunk(m):
        @pl.when(m < NCH - 2)
        def _():
            ar_b(0, m + 2)

        ar_c(0, m, 1)
        rw = rows(m)
        r.dxs[rw] += norm_grad(total_of(0, m), r.an, 0, r.rs0, rw)

        @pl.when(m < NCH // 2)
        def _():
            late_out(m + NCH // 2)

        @pl.when(m == 2)
        def _():
            job_cross.s2()
            job_in_a.s4()

        @pl.when(m == 3)
        def _():
            job_out_a.s5()

        @pl.when(m == 5)
        def _():
            job_cross.s3()
            job_in_a.s5()

    loop(0, NCH, last_chunk)

    outs = [
        pltpu.make_async_copy(r.dxs, r.latent_grad, r.out_sem.at[0]),
        pltpu.make_async_copy(r.gin, r.input_grad, r.out_sem.at[1]),
        late_cps[1],
    ]
    for cp in outs:
        cp.start()
    for k, where in enumerate((at_core, at_x, at_y)):
        cp = remote(r.dg, r.dgr.at[k], r.dg_snd.at[k], r.dg_rcv.at[k], where)
        cp.start()
        cp.wait()
        r.dg[...] += r.dgr[k]
        if k == 0:
            job_cross.s4()
            job_out_a.s6()
    r.gains_grad[...] = r.dg[...]
    job_cross.s5()
    job_in_a.s6()
    job_cross.s6()

    @pl.when(is_mid)
    def _():
        loop(0, NCH, lambda c: cp_tot(2, c).wait_send())
        loop(0, NCH, lambda c: cp_tot(0, c).wait_send())

    for cp in outs:
        cp.wait()


def block_call(latents, inputs, latent_group, latent_valid, input_group, input_valid, gains, weights, out_grad):
    T, D = latents.shape
    I = inputs.shape[0]
    C = weights["w_q_c"].shape[1]
    F = weights["w_in_a"].shape[1]
    CH = 64
    NCH = T // CH
    HL = C // HEAD_DIM
    in_vmem = dict(
        latent_group=latent_group, latent_valid=latent_valid, input_group=input_group,
        input_valid=input_valid, gains=gains,
    )
    in_any = dict(latents=latents, inputs=inputs, **weights, out_grad=out_grad)
    S = jax.ShapeDtypeStruct
    out_any = dict(
        latents_out=S((T, D), bf16), latent_grad=S((T, D), f32), input_grad=S((I, D), f32),
        g_out_b=S((D, F), bf16), g_in_b=S((D, F), bf16), g_self=S((D, 4 * C), bf16),
        g_out_a=S((D, F), bf16), g_in_a=S((D, F), bf16), g_cross=S((D, 4 * C), bf16),
    )
    out_vmem = dict(gains_grad=S((8, D), f32))
    V, DMA = pltpu.VMEM, pltpu.SemaphoreType.DMA
    half, eighth, piece = D // 2, D // 8, D // 16
    scratch = dict(
        inp=V((I, D), bf16), lat=V((T, D), bf16), r4=V((T, D), bf16),
        wkvc=V((D, 2 * C), bf16), wqc=V((D, C), bf16), woc=V((D, C), bf16),
        wina=V((D, F), bf16), wouta=V((D, F), bf16), wqkvs=V((D, 3 * C), bf16),
        wos=V((D, C), bf16), winb=V((D, F), bf16), woutb=V((D, F), bf16), wj=V((D, F), bf16),
        codes=V((8, I + 2 * T), f32), codes_o=V((8, I + 2 * T), f32),
        qcol=V((T, LANES), f32), qcol_o=V((T, LANES), f32),
        part=V((3, T, D), bf16), rin=V((3, T, D), bf16), rmid=V((3, T, D), bf16),
        xs=V((T, D), f32), dxs=V((T, D), f32), gin=V((I, D), f32),
        an=V((T, D), bf16), bn=V((I, D), bf16), h1=V((T, D), bf16), cs=V((T, D), bf16), h2=V((T, D), bf16),
        rs0=V((T, LANES), f32), rs1=V((I, LANES), f32), rs2=V((T, LANES), f32), rs3=V((T, LANES), f32),
        rs4=V((T, LANES), f32),
        z1=V((T, F), bf16), s1=V((T, F), bf16), du1=V((T, F), bf16), z2=V((T, F), bf16), du2=V((T, F), bf16),
        ra=V((T, D), bf16), rb=V((T, D), bf16),
        q=V((T, C), bf16), kv=V((2 * I, 2 * C), bf16), p_c=V((HL, T, 2 * I), bf16), o_c=V((T, C), bf16),
        q2=V((T, C), bf16), kv2=V((2 * T, 2 * C), bf16), p_s=V((HL, T, 2 * T), bf16), o_s=V((T, C), bf16),
        pr_c=V((HL, T, I), bf16), qr_c=V((T, C), bf16), or_c=V((T, C), bf16),
        pr_s=V((HL, T, T), bf16), qr_s=V((T, C), bf16), or_s=V((T, C), bf16),
        do=V((2, T, C), bf16), do_o=V((2, T, C), bf16), ds=V((2 * T, max(T, I)), bf16),
        dqkv=V((T, 3 * C), bf16), dq=V((T, C), bf16), dkv=V((I, 2 * C), bf16),
        rc=V((3, half, F), bf16), r1p=V((3, eighth, F), bf16), r1q=V((3, eighth, F), bf16),
        r2p=V((3, piece, F), bf16), r2q=V((3, piece, F), bf16),
        dg=V((8, D), f32), dgr=V((3, 8, D), f32),
        load_sem=DMA((16,)), out_sem=DMA((4,)),
        y_snd=DMA((8,)), y_rcv=DMA((8,)),
        kv_snd=DMA((NCH,)), kv_rcv=DMA((NCH,)), do_snd=DMA((2, NCH)), do_rcv=DMA((2, NCH)),
        ar_snd=DMA((3, NCH)), ar_tot=DMA((3, NCH)), ar_in=DMA((3, NCH)), ar_mid=DMA((3, NCH)),
        j_snd=DMA((6, 10)), j_rcv=DMA((6, 10)), j_own=DMA((6, 2)), dg_snd=DMA((3,)), dg_rcv=DMA((3,)),
    )
    names = [*in_vmem, *in_any, *out_any, *out_vmem, *scratch]
    outs = pl.pallas_call(
        functools.partial(block_kernel, names, T, I, D, C, F, CH),
        out_shape=(*out_any.values(), *out_vmem.values()),
        in_specs=[pl.BlockSpec(memory_space=pltpu.VMEM)] * len(in_vmem)
        + [pl.BlockSpec(memory_space=pl.ANY)] * len(in_any),
        out_specs=tuple(
            [pl.BlockSpec(memory_space=pl.ANY)] * len(out_any)
            + [pl.BlockSpec(memory_space=pltpu.VMEM)] * len(out_vmem)
        ),
        scratch_shapes=list(scratch.values()),
        compiler_params=pltpu.CompilerParams(
            collective_id=0, has_side_effects=True, vmem_limit_bytes=63 * 2**20
        ),
        name="block_kernel",
    )(*in_vmem.values(), *in_any.values())
    return dict(zip([*out_any, *out_vmem], outs, strict=True))


def per_device_fast(
    latents, inputs, latent_group, latent_valid, input_group, input_valid, gains,
    w_q_cross, w_kv_cross, w_o_cross, w_in_a, w_out_a, w_qkv_self, w_o_self, w_in_b, w_out_b, out_grad,
):
    D = latents.shape[2]
    C = w_q_cross.shape[1]
    weights = dict(
        w_q_c=w_q_cross, w_kv_c=w_kv_cross.reshape(D, 2 * C), w_o_c=w_o_cross, w_in_a=w_in_a,
        w_out_a=w_out_a, w_qkv_s=w_qkv_self.reshape(D, 3 * C), w_o_s=w_o_self, w_in_b=w_in_b, w_out_b=w_out_b,
    )
    o = block_call(
        latents[0], inputs[0], latent_group, latent_valid, input_group, input_valid, gains, weights, out_grad[0]
    )
    g_cross, g_self = o["g_cross"], o["g_self"]
    return (
        o["latents_out"][None],
        o["latent_grad"][None],
        o["input_grad"][None],
        o["gains_grad"][: gains.shape[0]],
        g_cross[:, 2 * C : 3 * C].astype(f32),
        g_cross[:, : 2 * C].astype(f32).reshape(D, 2, C),
        g_cross[:, 3 * C :].astype(f32),
        o["g_in_a"].astype(f32),
        o["g_out_a"].astype(f32),
        g_self[:, : 3 * C].astype(f32).reshape(D, 3, C),
        g_self[:, 3 * C :].astype(f32),
        o["g_in_b"].astype(f32),
        o["g_out_b"].astype(f32),
    )


def solution(mesh):
    fast = dict(mesh.shape) == {"group": 4, "blk": 2, "head": 4}
    return jax.shard_map(
        per_device_fast if fast else per_device,
        mesh=mesh,
        in_specs=(
            P("group", "blk", None),
            P("group", "blk", None),
            P("group", "blk"),
            P("group", "blk"),
            P("group", "blk"),
            P("group", "blk"),
            P(),
            P(None, "head"),
            P(None, None, "head"),
            P(None, "head"),
            P(None, "head"),
            P(None, "head"),
            P(None, None, "head"),
            P(None, "head"),
            P(None, "head"),
            P(None, "head"),
            P("group", "blk", None),
        ),
        out_specs=(
            P("group", "blk", None),
            P("group", "blk", None),
            P("group", "blk", None),
            P(),
            P(None, "head"),
            P(None, None, "head"),
            P(None, "head"),
            P(None, "head"),
            P(None, "head"),
            P(None, None, "head"),
            P(None, "head"),
            P(None, "head"),
            P(None, "head"),
        ),
        check_vma=False,
    )
```

```python
import functools
import types

import jax
import jax.numpy as jnp
from jax import lax
from jax.experimental import pallas as pl
from jax.experimental.pallas import tpu as pltpu
from jax.sharding import PartitionSpec as P

HEAD_DIM = 128


masked_fill = -1000.0
contract_last = (((1,), (1,)), ((), ()))


def layer_norm(values, gains_row):
    centred = values - jnp.mean(values, axis=-1, keepdims=True)
    variance = jnp.mean(centred * centred, axis=-1, keepdims=True)
    return centred * lax.rsqrt(variance + 1e-05) * gains_row


def norm_back(values, gains_row, cotangent):
    unused, pullback = jax.vjp(layer_norm, values, gains_row)
    return pullback(cotangent)


def out_product(left, right):
    return lax.dot_general(left, right, contract_last, preferred_element_type=jnp.float32)


def block_rows(item_count):
    if item_count > 1024 and item_count % 1024 == 0:
        return 1024
    return item_count


def head_sum(partial_sum):
    return lax.psum(partial_sum, "head")


def head_grad_sum(partial_sum):
    return lax.psum(partial_sum, "head")


def score_block(query_heads, key_heads, query_code, key_code):
    scores = jnp.einsum(
        "qhd,khd->hqk", query_heads, key_heads, preferred_element_type=jnp.float32
    ) * HEAD_DIM ** (-0.5)
    allowed = query_code[:, None] == key_code[None, :]
    return (jnp.where(allowed[None], scores, masked_fill), allowed)


def cycle_attend(queries, query_code, key_rows, value_rows, key_code):
    row_count = queries.shape[0]
    heads_local = queries.shape[1] // HEAD_DIM
    query_heads = queries.reshape(row_count, heads_local, HEAD_DIM)

    def stats_block(state_carry, block_data):
        running, totals = state_carry
        key_block, code_block = block_data
        key_heads = key_block.reshape(key_block.shape[0], heads_local, HEAD_DIM)
        scores, allowed = score_block(query_heads, key_heads, query_code, code_block)
        largest = jnp.maximum(running, jnp.max(scores, axis=-1))
        totals = totals * jnp.exp(running - largest) + jnp.sum(
            jnp.exp(scores - largest[:, :, None]), axis=-1
        )
        return ((largest, totals), None)

    stats_init = (
        jnp.full((heads_local, row_count), -jnp.inf, jnp.float32),
        jnp.zeros((heads_local, row_count), jnp.float32),
    )
    state_carry = stats_init
    key_piece = lax.all_gather(key_rows, "blk", axis=0, tiled=True)
    code_piece = lax.all_gather(key_code, "blk", axis=0, tiled=True)
    item_count = key_piece.shape[0]
    step_rows = block_rows(item_count)
    block_count = item_count // step_rows
    stacked = (
        key_piece.reshape(block_count, step_rows, key_piece.shape[1]),
        code_piece.reshape(block_count, step_rows),
    )
    state_carry, unused = lax.scan(stats_block, state_carry, stacked)
    running, totals = state_carry
    log_sums = running + jnp.log(totals)

    def one_block(accumulated, block_data):
        key_block, value_block, code_block = block_data
        key_heads = key_block.reshape(key_block.shape[0], heads_local, HEAD_DIM)
        value_heads = value_block.reshape(value_block.shape[0], heads_local, HEAD_DIM)
        scores, allowed = score_block(query_heads, key_heads, query_code, code_block)
        prob_rows = jnp.exp(scores - log_sums[:, :, None]).astype(jnp.bfloat16)
        accumulated = accumulated + jnp.einsum(
            "hqk,khd->qhd", prob_rows, value_heads, preferred_element_type=jnp.float32
        )
        return (accumulated, None)

    initial = jnp.zeros((row_count, heads_local, HEAD_DIM), jnp.float32)
    accumulated = initial
    key_piece = lax.all_gather(key_rows, "blk", axis=0, tiled=True)
    value_piece = lax.all_gather(value_rows, "blk", axis=0, tiled=True)
    code_piece = lax.all_gather(key_code, "blk", axis=0, tiled=True)
    item_count = key_piece.shape[0]
    step_rows = block_rows(item_count)
    block_count = item_count // step_rows
    stacked = (
        key_piece.reshape(block_count, step_rows, key_piece.shape[1]),
        value_piece.reshape(block_count, step_rows, value_piece.shape[1]),
        code_piece.reshape(block_count, step_rows),
    )
    accumulated, unused = lax.scan(one_block, accumulated, stacked)
    mixed = accumulated.reshape(row_count, heads_local * HEAD_DIM)
    return (mixed, log_sums)


def grad_parts(query_rows, grad_rows, query_code, log_sums, deltas, key_rows, value_rows, key_code):
    heads_local = query_rows.shape[1] // HEAD_DIM
    query_heads = query_rows.reshape(query_rows.shape[0], heads_local, HEAD_DIM)
    grad_heads = grad_rows.reshape(grad_rows.shape[0], heads_local, HEAD_DIM)
    key_heads = key_rows.reshape(key_rows.shape[0], heads_local, HEAD_DIM)
    value_heads = value_rows.reshape(value_rows.shape[0], heads_local, HEAD_DIM)
    scores, allowed = score_block(query_heads, key_heads, query_code, key_code)
    prob_rows = jnp.exp(scores - log_sums[:, :, None])
    grad_probs = jnp.einsum(
        "qhd,khd->hqk", grad_heads, value_heads, preferred_element_type=jnp.float32
    )
    grad_scores = jnp.where(
        allowed[None], prob_rows * (grad_probs - deltas[:, :, None]), 0.0
    ).astype(jnp.bfloat16)
    return (query_heads, grad_heads, key_heads, grad_scores, prob_rows)


def query_part(grad_scores, key_heads, row_shape):
    grad_query = jnp.einsum(
        "hqk,khd->qhd", grad_scores, key_heads, preferred_element_type=jnp.float32
    ) * HEAD_DIM ** (-0.5)
    return grad_query.reshape(row_shape)


def key_parts(grad_scores, prob_rows, query_heads, grad_heads, row_shape):
    grad_key = jnp.einsum(
        "hqk,qhd->khd", grad_scores, query_heads, preferred_element_type=jnp.float32
    ) * HEAD_DIM ** (-0.5)
    grad_value = jnp.einsum(
        "hqk,qhd->khd",
        prob_rows.astype(jnp.bfloat16),
        grad_heads,
        preferred_element_type=jnp.float32,
    )
    return (grad_key.reshape(row_shape), grad_value.reshape(row_shape))


def row_delta(grad_mixed, mixed):
    row_count = mixed.shape[0]
    heads_local = mixed.shape[1] // HEAD_DIM
    product = (grad_mixed.astype(jnp.float32) * mixed).reshape(row_count, heads_local, HEAD_DIM)
    return jnp.sum(product, axis=-1).T


def attend_back(queries, grad_mixed, query_code, log_sums, deltas, key_rows, value_rows, key_code):
    row_count = queries.shape[0]
    col_width = queries.shape[1]
    heads_local = col_width // HEAD_DIM
    all_keys, all_values, all_kcodes, all_queries, all_grads, all_qcodes = (
        lax.all_gather(key_rows, "blk", axis=0, tiled=True),
        lax.all_gather(value_rows, "blk", axis=0, tiled=True),
        lax.all_gather(key_code, "blk", axis=0, tiled=True),
        lax.all_gather(queries, "blk", axis=0, tiled=True),
        lax.all_gather(grad_mixed, "blk", axis=0, tiled=True),
        lax.all_gather(query_code, "blk", axis=0, tiled=True),
    )
    all_sums, all_deltas = (
        lax.all_gather(log_sums, "blk", axis=1, tiled=True),
        lax.all_gather(deltas, "blk", axis=1, tiled=True),
    )
    key_total = all_keys.shape[0]
    key_step = block_rows(key_total)
    key_blocks = key_total // key_step

    def own_queries(grad_query, block_data):
        key_block_rows, value_block_rows, code_block = block_data
        parts = grad_parts(
            queries,
            grad_mixed,
            query_code,
            log_sums,
            deltas,
            key_block_rows,
            value_block_rows,
            code_block,
        )
        return (grad_query + query_part(parts[3], parts[2], queries.shape), None)

    key_stack = (
        all_keys.reshape(key_blocks, key_step, col_width),
        all_values.reshape(key_blocks, key_step, col_width),
        all_kcodes.reshape(key_blocks, key_step),
    )
    grad_query, unused = lax.scan(
        own_queries, jnp.zeros((row_count, col_width), jnp.float32), key_stack
    )
    query_total = all_queries.shape[0]
    query_step = block_rows(query_total)
    query_blocks = query_total // query_step
    key_count = key_rows.shape[0]

    def own_keys(state_carry, block_data):
        grad_key, grad_value = state_carry
        query_block_rows, grad_block_rows, code_block, sums_block, deltas_block = block_data
        query_heads, grad_heads, key_heads, grad_scores, prob_rows = grad_parts(
            query_block_rows,
            grad_block_rows,
            code_block,
            sums_block,
            deltas_block,
            key_rows,
            value_rows,
            key_code,
        )
        part_key, part_value = key_parts(
            grad_scores, prob_rows, query_heads, grad_heads, key_rows.shape
        )
        return ((grad_key + part_key, grad_value + part_value), None)

    query_stack = (
        all_queries.reshape(query_blocks, query_step, col_width),
        all_grads.reshape(query_blocks, query_step, col_width),
        all_qcodes.reshape(query_blocks, query_step),
        all_sums.reshape(heads_local, query_blocks, query_step).transpose(1, 0, 2),
        all_deltas.reshape(heads_local, query_blocks, query_step).transpose(1, 0, 2),
    )
    zeros_keys = jnp.zeros((key_count, col_width), jnp.float32)
    (grad_key, grad_value), unused = lax.scan(own_keys, (zeros_keys, zeros_keys), query_stack)
    return (grad_query, grad_key, grad_value)


def mlp_forward(stream, gains_row, weight_in, weight_out):
    hidden_in = layer_norm(stream, gains_row).astype(jnp.bfloat16)
    hidden = jnp.dot(hidden_in, weight_in, preferred_element_type=jnp.float32)
    activated = jax.nn.gelu(hidden).astype(jnp.bfloat16)
    branch = head_sum(out_product(activated, weight_out))
    return (stream + branch, (hidden_in, hidden, activated))


def mlp_backward(stream, gains_row, weight_in, weight_out, saved, grad_stream):
    hidden_in, hidden, activated = saved
    grad_low = grad_stream.astype(jnp.bfloat16)
    grad_weight_out = jnp.einsum(
        "td,tf->df", grad_low, activated, preferred_element_type=jnp.float32
    )
    grad_activated = jnp.dot(grad_low, weight_out, preferred_element_type=jnp.float32)
    unused, gelu_back = jax.vjp(jax.nn.gelu, hidden)
    grad_hidden = gelu_back(grad_activated)[0].astype(jnp.bfloat16)
    grad_weight_in = jnp.einsum(
        "td,tf->df", hidden_in, grad_hidden, preferred_element_type=jnp.float32
    )
    grad_normed = head_grad_sum(out_product(grad_hidden, weight_in))
    grad_input, grad_gain = norm_back(stream, gains_row, grad_normed)
    return (grad_stream + grad_input, grad_gain, grad_weight_in, grad_weight_out)


def self_forward(stream, gains_row, weight_triple, weight_out, query_code, key_code):
    normed_low = layer_norm(stream, gains_row).astype(jnp.bfloat16)
    col_width = weight_triple.shape[2]
    triple = jnp.dot(
        normed_low,
        weight_triple.reshape(weight_triple.shape[0], 3 * col_width),
        preferred_element_type=jnp.float32,
    ).astype(jnp.bfloat16)
    queries = triple[:, :col_width]
    key_rows = triple[:, col_width : 2 * col_width]
    value_rows = triple[:, 2 * col_width :]
    mixed, log_sums = cycle_attend(queries, query_code, key_rows, value_rows, key_code)
    mixed_low = mixed.astype(jnp.bfloat16)
    branch = head_sum(out_product(mixed_low, weight_out))
    return (
        stream + branch,
        (normed_low, queries, key_rows, value_rows, mixed, mixed_low, log_sums),
    )


def self_backward(
    stream, gains_row, weight_triple, weight_out, saved, grad_stream, query_code, key_code
):
    normed_low, queries, key_rows, value_rows, mixed, mixed_low, log_sums = saved
    grad_low = grad_stream.astype(jnp.bfloat16)
    grad_weight_out = jnp.einsum(
        "td,ti->di", grad_low, mixed_low, preferred_element_type=jnp.float32
    )
    grad_mixed = jnp.dot(grad_low, weight_out, preferred_element_type=jnp.float32).astype(
        jnp.bfloat16
    )
    deltas = row_delta(grad_mixed, mixed)
    grad_query, grad_key, grad_value = attend_back(
        queries, grad_mixed, query_code, log_sums, deltas, key_rows, value_rows, key_code
    )
    grad_triple = jnp.concatenate([grad_query, grad_key, grad_value], axis=1).astype(jnp.bfloat16)
    grad_weight_triple = jnp.einsum(
        "td,tc->dc", normed_low, grad_triple, preferred_element_type=jnp.float32
    ).reshape(weight_triple.shape)
    grad_normed = head_grad_sum(
        out_product(grad_triple, weight_triple.reshape(weight_triple.shape[0], -1))
    )
    grad_input, grad_gain = norm_back(stream, gains_row, grad_normed)
    return (grad_stream + grad_input, grad_gain, grad_weight_triple, grad_weight_out)


def cross_forward(
    stream, input_rows, gains, weight_query, weight_pairs, weight_out, query_code, key_code
):
    latent_low = layer_norm(stream, gains[0]).astype(jnp.bfloat16)
    input_low = layer_norm(input_rows, gains[1]).astype(jnp.bfloat16)
    col_width = weight_query.shape[1]
    queries = jnp.dot(latent_low, weight_query, preferred_element_type=jnp.float32).astype(
        jnp.bfloat16
    )
    paired = jnp.dot(
        input_low,
        weight_pairs.reshape(weight_pairs.shape[0], 2 * col_width),
        preferred_element_type=jnp.float32,
    ).astype(jnp.bfloat16)
    key_rows = paired[:, :col_width]
    value_rows = paired[:, col_width:]
    mixed, log_sums = cycle_attend(queries, query_code, key_rows, value_rows, key_code)
    mixed_low = mixed.astype(jnp.bfloat16)
    branch = head_sum(out_product(mixed_low, weight_out))
    return (
        stream + branch,
        (latent_low, input_low, queries, key_rows, value_rows, mixed, mixed_low, log_sums),
    )


def cross_backward(
    stream,
    input_rows,
    gains,
    weight_query,
    weight_pairs,
    weight_out,
    saved,
    grad_stream,
    query_code,
    key_code,
):
    latent_low, input_low, queries, key_rows, value_rows, mixed, mixed_low, log_sums = saved
    grad_low = grad_stream.astype(jnp.bfloat16)
    grad_weight_out = jnp.einsum(
        "td,ti->di", grad_low, mixed_low, preferred_element_type=jnp.float32
    )
    grad_mixed = jnp.dot(grad_low, weight_out, preferred_element_type=jnp.float32).astype(
        jnp.bfloat16
    )
    deltas = row_delta(grad_mixed, mixed)
    grad_query, grad_key, grad_value = attend_back(
        queries, grad_mixed, query_code, log_sums, deltas, key_rows, value_rows, key_code
    )
    grad_query_low = grad_query.astype(jnp.bfloat16)
    grad_pairs = jnp.concatenate([grad_key, grad_value], axis=1).astype(jnp.bfloat16)
    grad_weight_query = jnp.einsum(
        "td,tc->dc", latent_low, grad_query_low, preferred_element_type=jnp.float32
    )
    grad_weight_pairs = jnp.einsum(
        "td,tc->dc", input_low, grad_pairs, preferred_element_type=jnp.float32
    ).reshape(weight_pairs.shape)
    latent_part = out_product(grad_query_low, weight_query)
    input_part = out_product(grad_pairs, weight_pairs.reshape(weight_pairs.shape[0], -1))
    latent_normed, input_normed = lax.psum((latent_part, input_part), "head")
    grad_latent, gain_zero = norm_back(stream, gains[0], latent_normed)
    grad_inputs, gain_one = norm_back(input_rows, gains[1], input_normed)
    return (
        grad_stream + grad_latent,
        grad_inputs,
        gain_zero,
        gain_one,
        grad_weight_query,
        grad_weight_pairs,
        grad_weight_out,
    )


def per_device(
    latents,
    inputs,
    latent_group,
    latent_valid,
    input_group,
    input_valid,
    gains,
    w_q_cross,
    w_kv_cross,
    w_o_cross,
    w_in_a,
    w_out_a,
    w_qkv_self,
    w_o_self,
    w_in_b,
    w_out_b,
    out_grad,
):
    start_stream = latents[0].astype(jnp.float32)
    input_rows = inputs[0].astype(jnp.float32)
    query_code = latent_group[0].astype(jnp.bfloat16)
    input_code = jnp.where(input_valid[0] == 1, input_group[0], -1).astype(jnp.bfloat16)
    self_code = jnp.where(latent_valid[0] == 1, latent_group[0], -1).astype(jnp.bfloat16)
    cross_stream, cross_saved = cross_forward(
        start_stream, input_rows, gains, w_q_cross, w_kv_cross, w_o_cross, query_code, input_code
    )
    middle_stream, first_saved = mlp_forward(cross_stream, gains[2], w_in_a, w_out_a)
    self_stream, self_saved = self_forward(
        middle_stream, gains[3], w_qkv_self, w_o_self, query_code, self_code
    )
    final_stream, second_saved = mlp_forward(self_stream, gains[4], w_in_b, w_out_b)
    grad_stream = out_grad[0].astype(jnp.float32)
    grad_stream, gain_four, grad_in_b, grad_out_b = mlp_backward(
        self_stream, gains[4], w_in_b, w_out_b, second_saved, grad_stream
    )
    grad_stream, gain_three, grad_qkv_self, grad_o_self = self_backward(
        middle_stream,
        gains[3],
        w_qkv_self,
        w_o_self,
        self_saved,
        grad_stream,
        query_code,
        self_code,
    )
    grad_stream, gain_two, grad_in_a, grad_out_a = mlp_backward(
        cross_stream, gains[2], w_in_a, w_out_a, first_saved, grad_stream
    )
    grad_stream, grad_inputs, gain_zero, gain_one, grad_q_cross, grad_kv_cross, grad_o_cross = (
        cross_backward(
            start_stream,
            input_rows,
            gains,
            w_q_cross,
            w_kv_cross,
            w_o_cross,
            cross_saved,
            grad_stream,
            query_code,
            input_code,
        )
    )
    gain_terms = jnp.stack([gain_zero, gain_one, gain_two, gain_three, gain_four], axis=1)
    (
        sum_gains,
        sum_q_cross,
        sum_kv_cross,
        sum_o_cross,
        sum_in_a,
        sum_out_a,
        sum_qkv_self,
        sum_o_self,
        sum_in_b,
        sum_out_b,
    ) = (
        lax.psum_scatter(gain_terms, ("group", "blk"), scatter_dimension=0, tiled=True),
        lax.psum_scatter(grad_q_cross, ("group", "blk"), scatter_dimension=0, tiled=True),
        lax.psum_scatter(grad_kv_cross, ("group", "blk"), scatter_dimension=0, tiled=True),
        lax.psum_scatter(grad_o_cross, ("group", "blk"), scatter_dimension=0, tiled=True),
        lax.psum_scatter(grad_in_a, ("group", "blk"), scatter_dimension=0, tiled=True),
        lax.psum_scatter(grad_out_a, ("group", "blk"), scatter_dimension=0, tiled=True),
        lax.psum_scatter(grad_qkv_self, ("group", "blk"), scatter_dimension=0, tiled=True),
        lax.psum_scatter(grad_o_self, ("group", "blk"), scatter_dimension=0, tiled=True),
        lax.psum_scatter(grad_in_b, ("group", "blk"), scatter_dimension=0, tiled=True),
        lax.psum_scatter(grad_out_b, ("group", "blk"), scatter_dimension=0, tiled=True),
    )
    (
        full_gains,
        full_q_cross,
        full_kv_cross,
        full_o_cross,
        full_in_a,
        full_out_a,
        full_qkv_self,
        full_o_self,
        full_in_b,
        full_out_b,
    ) = (
        lax.all_gather(sum_gains, ("group", "blk"), axis=0, tiled=True),
        lax.all_gather(sum_q_cross, ("group", "blk"), axis=0, tiled=True),
        lax.all_gather(sum_kv_cross, ("group", "blk"), axis=0, tiled=True),
        lax.all_gather(sum_o_cross, ("group", "blk"), axis=0, tiled=True),
        lax.all_gather(sum_in_a, ("group", "blk"), axis=0, tiled=True),
        lax.all_gather(sum_out_a, ("group", "blk"), axis=0, tiled=True),
        lax.all_gather(sum_qkv_self, ("group", "blk"), axis=0, tiled=True),
        lax.all_gather(sum_o_self, ("group", "blk"), axis=0, tiled=True),
        lax.all_gather(sum_in_b, ("group", "blk"), axis=0, tiled=True),
        lax.all_gather(sum_out_b, ("group", "blk"), axis=0, tiled=True),
    )
    return (
        final_stream.astype(jnp.bfloat16)[None],
        grad_stream[None],
        grad_inputs[None],
        full_gains.T,
        full_q_cross,
        full_kv_cross,
        full_o_cross,
        full_in_a,
        full_out_a,
        full_qkv_self,
        full_o_self,
        full_in_b,
        full_out_b,
    )


MESH = pl.DeviceIdType.MESH
bf16, f32 = jnp.bfloat16, jnp.float32
LANES = 128
TILE = 256
SCALE = HEAD_DIM**-0.5
GELU_A = 0.7978845608028654
GELU_B = 0.044715


def dot_nn(a, b):
    return jnp.dot(a, b, preferred_element_type=f32)


def dot_nt(a, b):
    return lax.dot_general(a, b, (((1,), (1,)), ((), ())), preferred_element_type=f32)


def dot_tn(a, b):
    return lax.dot_general(a, b, (((0,), (0,)), ((), ())), preferred_element_type=f32)


def norm_rows(x):
    c = x - jnp.mean(x, axis=-1, keepdims=True)
    rstd = lax.rsqrt(jnp.mean(c * c, axis=-1, keepdims=True) + 1e-05)
    return c * rstd, rstd


def gelu_both(u):
    u2 = u * u
    t = jnp.tanh(GELU_A * u * (1.0 + GELU_B * u2))
    half = 0.5 * (1.0 + t)
    slope = half + 0.5 * u * (1.0 - t * t) * (GELU_A * (1.0 + 3.0 * GELU_B * u2))
    return u * half, slope


def loop(start, stop, body):
    def step(k, carry):
        body(k)
        return carry

    lax.fori_loop(start, stop, step, 0)


SCHEDULE = dict(
    fifth=["At", "Bt", "A1", "", "B1", "", "", ""],
    self_keys_0=[""],
    self_keys_1=["A2"],
    sixth_put=["B2 St"],
    sixth=["A3", "B3 S1", "A4", "B4", "S2", "A5", "S3", "B5"],
    seventh=["Ct S4", "Dt", "C1 A6", "", "D1", "B6", "", ""],
    cross_keys_0=["C2"],
    cross_keys_1=["D2 S5"],
    last_put=["Xt C3 D3"],
    input=["X1 C4", "gz1 D4", "S6 C5", "gz2 X2"],
    last=["D5", "X3 gz3 dg0", "C6", "X4 dg1", "D6", "dg2", "X5", "dg3"],
    end=["X6"],
)


def block_kernel(names, T, I, D, C, F, CH, *refs):
    r = types.SimpleNamespace(**dict(zip(names, refs, strict=True)))
    NCH = T // CH
    ICH = I // CH
    HL = C // HEAD_DIM
    g = lax.axis_index("group")
    b = lax.axis_index("blk")
    h = lax.axis_index("head")
    is_mid = (h == 1) | (h == 2)
    is_end = jnp.logical_not(is_mid)
    at_pair = (g, b, h ^ 1)
    at_mid = (g, b, 3 - h)
    at_y = (g, 1 - b, h)
    at_x = (g ^ 2, b, h)
    at_core = (g ^ 1, b, h)
    core = g % 2
    xi = g // 2
    gains = r.gains

    def rows(c, n=CH):
        return pl.ds(pl.multiple_of(c * n, n), n)

    def remote(src, dst, send_sem, recv_sem, where):
        return pltpu.make_async_remote_copy(
            src_ref=src, dst_ref=dst, send_sem=send_sem, recv_sem=recv_sem, device_id=where, device_id_type=MESH
        )

    bar = pltpu.get_barrier_semaphore()
    for where in (at_pair, at_y, at_x, at_core):
        pl.semaphore_signal(bar, inc=1, device_id=where, device_id_type=MESH)

    @pl.when(is_mid)
    def _():
        pl.semaphore_signal(bar, inc=1, device_id=at_mid, device_id_type=MESH)

    loads = {}

    def load(src, dst, name):
        cp = pltpu.make_async_copy(src, dst, r.load_sem.at[len(loads)])
        cp.start()
        loads[name] = cp

    load(r.inputs, r.inp, "inp")
    load(r.w_kv_c, r.wkvc, "wkvc")
    load(r.latents, r.lat, "lat")
    load(r.w_q_c, r.wqc, "wqc")
    load(r.w_o_c, r.woc, "woc")
    load(r.w_in_a, r.wina, "wina")
    load(r.w_out_a, r.wouta, "wouta")
    for j in range(3):
        load(r.w_qkv_s.at[j], r.wqkvs.at[:, pl.ds(j * C, C)], "wqkvs%d" % j)
    load(r.w_o_s, r.wos, "wos")
    load(r.w_in_b, r.winb, "winb")
    load(r.w_out_b, r.woutb, "woutb")
    load(r.out_grad, r.r4, "r4")

    lg = r.latent_group[...]
    ic = jnp.where(r.input_valid[...] == 1, r.input_group[...], -1).astype(f32)
    sc = jnp.where(r.latent_valid[...] == 1, lg, -1).astype(f32)
    lgf = lg.astype(f32)
    r.codes[:, 0:I] = jnp.broadcast_to(ic, (8, I))
    r.codes[:, I : I + T] = jnp.broadcast_to(sc, (8, T))
    r.codes[:, I + T : I + 2 * T] = jnp.broadcast_to(lgf, (8, T))

    def make_columns(line, dst):
        for j in range(T // LANES):
            dst[pl.ds(j * LANES, LANES), :] = jnp.transpose(
                jnp.broadcast_to(line[:, j * LANES : (j + 1) * LANES], (LANES, LANES))
            )

    make_columns(lgf, r.qcol)
    r.dg[...] = jnp.zeros_like(r.dg)
    r.gz[...] = jnp.zeros_like(r.gz)

    @pl.when(is_mid)
    def _():
        pl.semaphore_wait(bar, 5)

    @pl.when(is_end)
    def _():
        pl.semaphore_wait(bar, 4)

    def to_y(src, dst, k):
        return remote(src, dst, r.y_snd.at[k], r.y_rcv.at[k], at_y)

    codes_cp = to_y(r.codes, r.codes_o, 0)
    codes_cp.start()

    SUB = 2
    SR = CH // SUB

    def cp_in(p, c):
        rw = rows(c, SR)
        return remote(r.part.at[p, rw], r.rin.at[p, rw], r.ar_snd.at[p, c], r.ar_in.at[p, c], at_pair)

    def cp_mid(p, c):
        rw = rows(c, SR)
        return remote(r.part.at[p, rw], r.rmid.at[p, rw], r.ar_snd.at[p, c], r.ar_mid.at[p, c], at_mid)

    def cp_tot(p, c):
        rw = rows(c, SR)
        return remote(r.rin.at[p, rw], r.rin.at[p, rw], r.ar_tot.at[p, c], r.ar_in.at[p, c], at_pair)

    def subs(c):
        return [c * SUB + k for k in range(SUB)]

    def ar_send(p, c):
        @pl.when(is_end)
        def _():
            for k in subs(c):
                cp_in(p, k).start()

    def ar_put(p, c, value):
        r.part[p, rows(c)] = value.astype(bf16)
        ar_send(p, c)

    def ar_b(p, c):
        @pl.when(is_mid)
        def _():
            for k in subs(c):
                rw = rows(k, SR)
                cp_in(p, k).wait_recv()
                r.part[p, rw] = r.part[p, rw] + r.rin[p, rw]
                cp_mid(p, k).start()

    def ar_c(p, c, prev=None):
        @pl.when(is_mid)
        def _():
            for k in subs(c):
                rw = rows(k, SR)
                cp_mid(p, k).wait_recv()
                cp_mid(p, k).wait_send()
                r.rin[p, rw] = r.part[p, rw] + r.rmid[p, rw]
                if prev is not None:
                    cp_tot(prev, k).wait_send()
                cp_tot(p, k).start()

        @pl.when(is_end)
        def _():
            for k in subs(c):
                cp_in(p, k).wait_send()
                cp_tot(p, k).wait_recv()

    def drain(p, c):
        @pl.when(is_mid)
        def _():
            for k in subs(c):
                cp_tot(p, k).wait_send()

    def total_of(p, c):
        return r.rin[p, rows(c)].astype(f32)

    half, quarter, eighth, piece = D // 2, D // 4, D // 8, D // 16
    own = core * half
    p_own = own + xi * eighth
    p_oth = own + (1 - xi) * eighth
    q_base = own + quarter
    q_own = q_base + b * eighth
    q_oth = q_base + (1 - b) * eighth
    p_fin, p_fin_oth = p_own + b * piece, p_own + (1 - b) * piece
    q_fin, q_fin_oth = q_own + xi * piece, q_own + (1 - xi) * piece

    def span(start, n):
        return pl.ds(pl.multiple_of(start, piece), n)

    class Job:
        def __init__(self, index, w, rc, out, parts):
            self.j, self.w, self.rc, self.out, self.parts = index, w, rc, out, parts
            self.s = index % 3

        def tiles(self):
            loop(0, D // TILE, self.tile)
            self.cp_core().start()

        def tile(self, t):
            col = 0
            rw = rows(t, TILE)
            for lhs, rhs in self.parts:
                n = rhs.shape[1]
                self.w[rw, col : col + n] = dot_tn(lhs[:, rw], rhs[...]).astype(bf16)
                col += n

        def cp(self, k, src, dst, where):
            return remote(src, dst, r.j_snd.at[self.j, k], r.j_rcv.at[self.j, k], where)

        def cp_core(self):
            return self.cp(0, self.w.at[span((1 - core) * half, half)], self.rc, at_core)

        def cp_p1(self):
            return self.cp(1, self.w.at[span(p_oth, eighth)], r.r1p.at[self.s], at_x)

        def cp_q1(self):
            return self.cp(2, self.w.at[span(q_oth, eighth)], r.r1q.at[self.s], at_y)

        def cp_p2(self):
            return self.cp(3, self.w.at[span(p_fin_oth, piece)], r.r2p.at[self.s], at_y)

        def cp_q2(self):
            return self.cp(4, self.w.at[span(q_fin_oth, piece)], r.r2q.at[self.s], at_x)

        def cp_p3(self):
            return self.cp(5, self.w.at[span(p_fin, piece)], self.out.at[span(p_fin, piece)], at_y)

        def cp_q3(self):
            return self.cp(6, self.w.at[span(q_fin, piece)], self.out.at[span(q_fin, piece)], at_x)

        def cp_p4(self):
            return self.cp(7, self.out.at[span(p_own, eighth)], self.out.at[span(p_own, eighth)], at_x)

        def cp_q4(self):
            return self.cp(8, self.out.at[span(q_own, eighth)], self.out.at[span(q_own, eighth)], at_y)

        def cp_all(self):
            return self.cp(9, self.out.at[span(own, half)], self.out.at[span(own, half)], at_core)

        def cp_keep(self):
            return (
                pltpu.make_async_copy(
                    self.w.at[span(p_fin, piece)], self.out.at[span(p_fin, piece)], r.j_own.at[self.j, 0]
                ),
                pltpu.make_async_copy(
                    self.w.at[span(q_fin, piece)], self.out.at[span(q_fin, piece)], r.j_own.at[self.j, 1]
                ),
            )

        def add(self, start, n, other):
            rw = span(start, n)
            self.w[rw] = self.w[rw] + other[...]

        def s1(self):
            self.cp_core().wait_recv()
            self.add(p_oth, eighth, self.rc.at[span(p_oth - own, eighth)])
            self.cp_p1().start()
            self.add(q_oth, eighth, self.rc.at[span(q_oth - own, eighth)])
            self.cp_q1().start()
            self.add(p_own, eighth, self.rc.at[span(p_own - own, eighth)])
            self.add(q_own, eighth, self.rc.at[span(q_own - own, eighth)])

        def s2(self):
            self.cp_p1().wait_recv()
            self.add(p_own, eighth, r.r1p.at[self.s])
            self.cp_q1().wait_recv()
            self.add(q_own, eighth, r.r1q.at[self.s])
            self.cp_p2().start()
            self.cp_q2().start()

        def s3(self):
            self.cp_p2().wait_recv()
            self.add(p_fin, piece, r.r2p.at[self.s])
            self.cp_p3().start()
            self.cp_q2().wait_recv()
            self.add(q_fin, piece, r.r2q.at[self.s])
            self.cp_q3().start()
            for cp in self.cp_keep():
                cp.start()

        def s4(self):
            for cp in self.cp_keep():
                cp.wait()
            self.cp_p3().wait_recv()
            self.cp_p4().start()
            self.cp_q3().wait_recv()
            self.cp_q4().start()
            for cp in (self.cp_core(), self.cp_p1(), self.cp_q1(), self.cp_p2(), self.cp_q2(), self.cp_p3(), self.cp_q3()):
                cp.wait_send()

        def s5(self):
            self.cp_p4().wait_recv()
            self.cp_q4().wait_recv()
            self.cp_all().start()
            self.cp_p4().wait_send()
            self.cp_q4().wait_send()

        def s6(self):
            self.cp_all().wait()

    job_out_b = Job(0, r.woutb, r.rc.at[0], r.g_out_b, [(r.r4, r.z2)])
    job_in_b = Job(1, r.winb, r.rc.at[1], r.g_in_b, [(r.h2, r.du2)])
    job_self = Job(2, r.wj, r.rc.at[2], r.g_self, [(r.cs, r.dqkv), (r.ra, r.o_s)])
    job_out_a = Job(3, r.p_s, r.z2, r.g_out_a, [(r.rb, r.z1)])
    job_in_a = Job(4, r.woutb, r.du2, r.g_in_a, [(r.h1, r.du1)])
    job_cross = Job(5, r.winb, r.h2, r.g_cross, [(r.bn, r.dkv), (r.an, r.dq), (r.ra, r.o_c)])

    def norm_out(x, gain_row, out, rstd_out, rw):
        xhat, rstd = norm_rows(x)
        rstd_out[rw] = jnp.broadcast_to(rstd, (rstd.shape[0], LANES))
        low = (xhat * gains[gain_row : gain_row + 1, :]).astype(bf16)
        out[rw] = low
        return low

    def norm_grad(cot, low_ref, dg_row, gain_row, rstd_ref, rw):
        gain = gains[gain_row : gain_row + 1, :]
        xhat = low_ref[rw].astype(f32) * (1.0 / gain)
        scaled = cot * gain
        mean_one = jnp.mean(scaled, axis=-1, keepdims=True)
        mean_two = jnp.mean(scaled * xhat, axis=-1, keepdims=True)
        if dg_row is not None:
            r.dg[dg_row : dg_row + 1, :] += jnp.sum(cot * xhat, axis=0, keepdims=True)
        return rstd_ref[rw, 0:1] * (scaled - mean_one - xhat * mean_two)

    loads["inp"].wait()
    loads["wkvc"].wait()

    def kv_chunk(k):
        rw = rows(k, LANES)
        low = norm_out(r.inp[rw].astype(f32), 1, r.bn, r.rs1, rw)
        r.kv[rw] = dot_nn(low, r.wkvc[...]).astype(bf16)

    loop(0, I // LANES, kv_chunk)
    kv_cp = to_y(r.kv.at[pl.ds(0, I)], r.kv.at[pl.ds(I, I)], 1)
    kv_cp.start()
    loads["lat"].wait()
    loads["wqc"].wait()

    def q_chunk(k):
        rw = rows(k, LANES)
        low = norm_out(r.lat[rw].astype(f32), 0, r.an, r.rs0, rw)
        r.q[rw] = dot_nn(low, r.wqc[...]).astype(bf16)

    loop(0, T // LANES, q_chunk)
    codes_cp.wait()
    make_columns(r.codes_o[0:1, I + T : I + 2 * T], r.qcol_o)
    kv_cp.wait()
    loads["woc"].wait()

    def attend_chunk(k, q_ref, kv_ref, p_ref, o_ref, start, n):
        rw = rows(k)
        kc = jnp.concatenate([r.codes[0:1, start : start + n], r.codes_o[0:1, start : start + n]], axis=1)
        allowed = r.qcol[rw, 0:1] == kc
        for hd in range(HL):
            cols = slice(hd * HEAD_DIM, (hd + 1) * HEAD_DIM)
            vcols = slice(C + hd * HEAD_DIM, C + (hd + 1) * HEAD_DIM)
            s = jnp.where(allowed, dot_nt(q_ref[rw, cols], kv_ref[:, cols]) * SCALE, masked_fill)
            e = jnp.exp(s - jnp.max(s, axis=-1, keepdims=True))
            p = (e * (1.0 / jnp.sum(e, axis=-1, keepdims=True))).astype(bf16)
            p_ref[rows(k + hd * NCH), :] = p
            o_ref[rw, cols] = dot_nn(p, kv_ref[:, vcols]).astype(bf16)

    def cross_chunk(k):
        attend_chunk(k, r.q, r.kv, r.p_c, r.o_c, 0, I)
        ar_put(0, k, dot_nt(r.o_c[rows(k)], r.woc[...]))

        @pl.when(k >= 4)
        def _():
            ar_b(0, k - 4)

    loop(0, NCH, cross_chunk)

    back_cross = [
        to_y(r.p_c.at[:, pl.ds(I, I)], r.pr_c, 2), to_y(r.q, r.qr_c, 3), to_y(r.o_c, r.or_c, 4),
    ]
    for cp in back_cross:
        cp.start()
    loads["wina"].wait()
    loads["wouta"].wait()

    def first_chunk(m):
        @pl.when((m >= 2) & (m < NCH - 2))
        def _():
            ar_b(0, m + 2)

        ar_c(0, m)
        rw = rows(m)
        x = r.lat[rw].astype(f32) + total_of(0, m)
        r.xs[rw] = x
        low = norm_out(x, 2, r.h1, r.rs2, rw)
        z, slope = gelu_both(dot_nn(low, r.wina[...]))
        z = z.astype(bf16)
        r.z1[rw] = z
        r.s1[rw] = slope.astype(bf16)
        ar_put(1, m, dot_nt(z, r.wouta[...]))

        @pl.when(m >= NCH - 2)
        def _():
            ar_b(1, m + 2 - NCH)

    loop(0, NCH, first_chunk)
    for j in range(3):
        loads["wqkvs%d" % j].wait()
    loads["wos"].wait()

    def kv2_cp(c):
        return remote(r.kv2.at[rows(c)], r.kv2.at[rows(c + NCH)], r.kv_snd.at[c], r.kv_rcv.at[c], at_y)

    def second_chunk(m):
        @pl.when(m < NCH - 2)
        def _():
            ar_b(1, m + 2)

        ar_c(1, m, 0)
        rw = rows(m)
        x = r.xs[rw] + total_of(1, m)
        r.xs[rw] = x
        low = norm_out(x, 3, r.cs, r.rs3, rw)
        qkv = dot_nn(low, r.wqkvs[...]).astype(bf16)
        r.q2[rw] = qkv[:, :C]
        r.kv2[rw] = qkv[:, C:]
        kv2_cp(m).start()

    loop(0, NCH, second_chunk)
    loop(0, NCH, lambda c: kv2_cp(c).wait())

    def p_cp(c):
        return remote(r.p_s.at[rows(c), pl.ds(T, T)], r.pr_s.at[rows(c)], r.p_snd.at[c], r.p_rcv.at[c], at_y)

    q_back = to_y(r.q2, r.qr_s, 6)
    q_back.start()

    def self_chunk(k):
        attend_chunk(k, r.q2, r.kv2, r.p_s, r.o_s, I, T)
        for hd in range(HL):
            p_cp(k + hd * NCH).start()

        ar_put(0, k, dot_nt(r.o_s[rows(k)], r.wos[...]))

        @pl.when(k >= 4)
        def _():
            ar_b(0, k - 4)

    loop(0, NCH, self_chunk)
    o_back = to_y(r.o_s, r.or_s, 7)
    o_back.start()
    loads["winb"].wait()
    loads["woutb"].wait()
    loads["r4"].wait()

    def third_chunk(m):
        @pl.when((m >= 2) & (m < NCH - 2))
        def _():
            ar_b(0, m + 2)

        ar_c(0, m, 1)
        rw = rows(m)
        x = r.xs[rw] + total_of(0, m)
        r.xs[rw] = x
        low = norm_out(x, 4, r.h2, r.rs4, rw)
        z, slope = gelu_both(dot_nn(low, r.winb[...]))
        z = z.astype(bf16)
        r.z2[rw] = z
        du = (dot_nn(r.r4[rw], r.woutb[...]) * slope).astype(bf16)
        r.du2[rw] = du
        ar_put(1, m, dot_nt(du, r.winb[...]))
        r.part[2, rw] = dot_nt(z, r.woutb[...]).astype(bf16)

        @pl.when(m >= NCH - 2)
        def _():
            ar_b(1, m + 2 - NCH)

    loop(0, NCH, third_chunk)

    def d_o_cp(k, c):
        return remote(r.do.at[k, rows(c)], r.do_o.at[k, rows(c)], r.do_snd.at[k, c], r.do_rcv.at[k, c], at_y)

    class Back:
        def __init__(self, k, q, qr, kv, p, pr, o, o_r, n, start, dq, dkv, dkv_col):
            self.k, self.q, self.qr, self.kv, self.p, self.pr, self.o, self.o_r = k, q, qr, kv, p, pr, o, o_r
            self.n, self.first, self.dq, self.dkv, self.dkv_col = n, start, dq, dkv, dkv_col
            self.do, self.do_o = r.do.at[k], r.do_o.at[k]

        def own(self, m):
            rw = rows(m)
            n, a = self.n, self.first
            kc = jnp.concatenate([r.codes[0:1, a : a + n], r.codes_o[0:1, a : a + n]], axis=1)
            allowed = r.qcol[rw, 0:1] == kc
            for hd in range(HL):
                cols = slice(hd * HEAD_DIM, (hd + 1) * HEAD_DIM)
                vcols = slice(C + hd * HEAD_DIM, C + (hd + 1) * HEAD_DIM)
                grad = self.do[rw, cols]
                delta = jnp.sum(grad.astype(f32) * self.o[rw, cols].astype(f32), axis=-1, keepdims=True)
                diff = dot_nt(grad, self.kv[:, vcols]) - delta
                prob = self.p[rows(m + hd * NCH), :].astype(f32)
                ds = jnp.where(allowed, prob * diff, 0.0).astype(bf16)
                r.ds[rows(m + 2 * hd * NCH), 0:n] = ds[:, 0:n]
                self.dq[rw, cols] = (dot_nn(ds, self.kv[:, cols]) * SCALE).astype(bf16)

        def other(self, m):
            d_o_cp(self.k, m).wait()
            rw = rows(m)
            n, a = self.n, self.first
            allowed = r.qcol_o[rw, 0:1] == r.codes[0:1, a : a + n]
            for hd in range(HL):
                cols = slice(hd * HEAD_DIM, (hd + 1) * HEAD_DIM)
                vcols = slice(C + hd * HEAD_DIM, C + (hd + 1) * HEAD_DIM)
                grad = self.do_o[rw, cols]
                delta = jnp.sum(grad.astype(f32) * self.o_r[rw, cols].astype(f32), axis=-1, keepdims=True)
                diff = dot_nt(grad, self.kv[0:n, vcols]) - delta
                prob = self.pr[rows(m + hd * NCH), :].astype(f32)
                ds = jnp.where(allowed, prob * diff, 0.0).astype(bf16)
                r.ds[rows(m + (2 * hd + 1) * NCH), 0:n] = ds

        def some_other(self, m, waits):
            if waits is not None:

                @pl.when(m == NCH // 2)
                def _():
                    for wait in waits:
                        wait()

            @pl.when((m >= NCH // 2) & (m < NCH - 2))
            def _():
                self.other(2 * m - NCH)
                self.other(2 * m + 1 - NCH)

            @pl.when(m == NCH - 2)
            def _():
                self.other(NCH - 4)

            @pl.when(m == NCH - 1)
            def _():
                self.other(NCH - 3)

        def keys(self, hd):
            if hd >= HL:
                return
            n = self.n
            cols = slice(hd * HEAD_DIM, (hd + 1) * HEAD_DIM)
            at = 2 * hd * T
            dk = dot_tn(r.ds[at : at + T, 0:n], self.q[:, cols]) + dot_tn(r.ds[at + T : at + 2 * T, 0:n], self.qr[:, cols])
            col = self.dkv_col + hd * HEAD_DIM
            self.dkv[:, col : col + HEAD_DIM] = (dk * SCALE).astype(bf16)
            at = hd * T
            dv = dot_tn(self.p[at : at + T, 0:n], self.do[:, cols]) + dot_tn(self.pr[at : at + T, :], self.do_o[:, cols])
            col += C
            self.dkv[:, col : col + HEAD_DIM] = dv.astype(bf16)

    back_of_self = Back(0, r.q2, r.qr_s, r.kv2, r.p_s, r.pr_s, r.o_s, r.or_s, T, I, r.dqkv, r.dqkv, C)
    back_of_cross = Back(1, r.q, r.qr_c, r.kv, r.p_c, r.pr_c, r.o_c, r.or_c, I, 0, r.dq, r.dkv, 0)

    jobs = dict(A=job_out_b, B=job_in_b, S=job_self, C=job_out_a, D=job_in_a, X=job_cross)
    extra = {}

    def on(place, m=None):
        for step, words in enumerate(SCHEDULE[place]):
            names = words.split()
            if not names:
                continue

            def run(names=names):
                for name in names:
                    if name in extra:
                        extra[name]()
                    else:
                        getattr(jobs[name[0]], "tiles" if name[1] == "t" else "s" + name[1])()

            if m is None:
                run()
            else:
                pl.when(m == step)(run)

    def fifth_chunk(m):
        @pl.when(m < NCH - 2)
        def _():
            ar_b(1, m + 2)

        ar_c(1, m, 0)
        rw = rows(m)
        dx = r.r4[rw].astype(f32) + norm_grad(total_of(1, m), r.h2, 4, 4, r.rs4, rw)
        r.dxs[rw] = dx
        low = dx.astype(bf16)
        r.ra[rw] = low
        r.do[0, rw] = dot_nn(low, r.wos[...]).astype(bf16)
        d_o_cp(0, m).start()
        back_of_self.own(m)
        back_of_self.some_other(m, [q_back.wait, o_back.wait, lambda: loop(0, HL * NCH, lambda c: p_cp(c).wait())])

        on("fifth", m)

        @pl.when(m >= NCH // 2)
        def _():
            ar_b(2, m - NCH // 2)

    loop(0, NCH // 2, lambda c: ar_send(2, c))
    loop(0, NCH, fifth_chunk)

    def late_out(c):
        ar_c(2, c)
        rw = rows(c)
        r.part[2, rw] = (r.xs[rw] + total_of(2, c)).astype(bf16)

    back_of_self.other(NCH - 2)
    back_of_self.other(NCH - 1)
    back_of_self.keys(0)
    on("self_keys_0")
    loop(0, 2, late_out)
    back_of_self.keys(1)
    on("self_keys_1")
    loop(2, NCH // 2, late_out)
    late_cps = [
        pltpu.make_async_copy(r.part.at[2, rw], r.latents_out.at[rw], r.out_sem.at[2 + 2 * k])
        for k, rw in enumerate([pl.ds(0, T // 2), pl.ds(T // 2, T // 2)])
    ]
    late_cps[0].start()

    def sixth_put(k):
        ar_put(0, k, dot_nt(r.dqkv[rows(k)], r.wqkvs[...]))

    loop(0, NCH, sixth_put)
    on("sixth_put")
    loop(0, 2, lambda c: ar_b(0, c))

    def sixth_chunk(m):
        @pl.when(m < NCH - 2)
        def _():
            ar_b(0, m + 2)

        ar_c(0, m, 1)
        rw = rows(m)
        dx = r.dxs[rw] + norm_grad(total_of(0, m), r.cs, 3, 3, r.rs3, rw)
        r.dxs[rw] = dx
        low = dx.astype(bf16)
        r.rb[rw] = low
        du = (dot_nn(low, r.wouta[...]) * r.s1[rw].astype(f32)).astype(bf16)
        r.du1[rw] = du
        ar_put(1, m, dot_nt(du, r.wina[...]))

        @pl.when(m >= NCH - 2)
        def _():
            ar_b(1, m + 2 - NCH)

        on("sixth", m)

    loop(0, NCH, sixth_chunk)
    def seventh_chunk(m):
        @pl.when(m < NCH - 2)
        def _():
            ar_b(1, m + 2)

        @pl.when(m < NCH // 2)
        def _():
            drain(2, m)

        ar_c(1, m, 0)
        rw = rows(m)
        dx = r.dxs[rw] + norm_grad(total_of(1, m), r.h1, 2, 2, r.rs2, rw)
        r.dxs[rw] = dx
        low = dx.astype(bf16)
        r.ra[rw] = low
        r.do[1, rw] = dot_nn(low, r.woc[...]).astype(bf16)
        d_o_cp(1, m).start()
        back_of_cross.own(m)
        back_of_cross.some_other(m, [cp.wait for cp in back_cross])

        on("seventh", m)

        @pl.when(m >= NCH // 2)
        def _():
            ar_b(2, m)

    loop(NCH // 2, NCH, lambda c: ar_send(2, c))
    loop(0, NCH, seventh_chunk)

    back_of_cross.other(NCH - 2)
    back_of_cross.other(NCH - 1)
    back_of_cross.keys(0)
    on("cross_keys_0")
    back_of_cross.keys(1)
    on("cross_keys_1")
    loop(NCH // 2, NCH // 2 + 2, late_out)

    late_cps[0].wait()

    def put_last(p, k, value, low_ref, gain_row):
        ar_put(p, k, value)
        xhat = low_ref[rows(k)].astype(f32) * (1.0 / gains[gain_row : gain_row + 1, :])
        r.gz[gain_row : gain_row + 1, :] += jnp.sum(value * xhat, axis=0, keepdims=True)

    loop(0, ICH, lambda k: put_last(2, k, dot_nt(r.dkv[rows(k)], r.wkvc[...]), r.bn, 1))
    loop(0, NCH, lambda k: put_last(0, k, dot_nt(r.dq[rows(k)], r.wqc[...]), r.an, 0))

    def gz_cp(k, where):
        return remote(r.gz, r.gzr.at[k], r.gz_snd.at[k], r.gz_rcv.at[k], where)

    @pl.when(is_end)
    def _():
        gz_cp(0, at_pair).start()

    def gz_one():
        @pl.when(is_mid)
        def _():
            gz_cp(0, at_pair).wait_recv()
            r.gz[...] += r.gzr[0]
            gz_cp(1, at_mid).start()

    def gz_two():
        @pl.when(is_mid)
        def _():
            gz_cp(1, at_mid).wait()
            r.gz[...] += r.gzr[1]
            gz_cp(2, at_pair).start()

    def gz_three():
        @pl.when(is_end)
        def _():
            gz_cp(0, at_pair).wait_send()
            gz_cp(2, at_pair).wait_recv()
            r.dg[0:2, :] = r.gzr[2, 0:2, :]

        @pl.when(is_mid)
        def _():
            gz_cp(2, at_pair).wait_send()
            r.dg[0:2, :] = r.gz[0:2, :]

    def dg_cp(k):
        return remote(r.dg, r.dgr.at[k], r.dg_snd.at[k], r.dg_rcv.at[k], (at_core, at_x, at_y)[k])

    def dg_next(k):
        def step():
            dg_cp(k).wait()
            r.dg[...] += r.dgr[k]
            if k < 2:
                dg_cp(k + 1).start()

        return step

    dg_zero, dg_one, dg_two = (dg_next(k) for k in range(3))

    loop(NCH // 2 + 2, NCH, late_out)
    late_cps[1].start()
    on("last_put")
    loop(0, 2, lambda c: ar_b(2, c))

    extra.update(gz1=gz_one, gz2=gz_two, gz3=gz_three, dg0=dg_cp(0).start, dg1=dg_zero, dg2=dg_one, dg3=dg_two)

    def input_chunk(m):
        @pl.when(m < ICH - 2)
        def _():
            ar_b(2, m + 2)

        @pl.when(m >= ICH - 2)
        def _():
            ar_b(0, m + 2 - ICH)

        ar_c(2, m)
        rw = rows(m)
        r.gin[rw] = norm_grad(total_of(2, m), r.bn, None, 1, r.rs1, rw).astype(bf16)

        on("input", m)

    loop(0, ICH, input_chunk)
    out_cps = [
        pltpu.make_async_copy(r.gin, r.input_grad, r.out_sem.at[0]),
        pltpu.make_async_copy(r.rb.at[pl.ds(0, T // 2)], r.latent_grad.at[pl.ds(0, T // 2)], r.out_sem.at[1]),
        pltpu.make_async_copy(r.rb.at[pl.ds(T // 2, T // 2)], r.latent_grad.at[pl.ds(T // 2, T // 2)], r.out_sem.at[3]),
    ]
    out_cps[0].start()

    def last_chunk(m):
        @pl.when(m < NCH - 2)
        def _():
            ar_b(0, m + 2)

        ar_c(0, m, 1)
        rw = rows(m)
        r.rb[rw] = (r.dxs[rw] + norm_grad(total_of(0, m), r.an, None, 0, r.rs0, rw)).astype(bf16)

        @pl.when(m == 4)
        def _():
            out_cps[1].start()

        on("last", m)

    loop(0, NCH, last_chunk)
    out_cps[2].start()
    r.gains_grad[...] = r.dg[...]
    on("end")

    loop(0, NCH, lambda c: drain(2, c))
    loop(0, NCH, lambda c: drain(0, c))

    for cp in [*out_cps, late_cps[1]]:
        cp.wait()


def block_call(latents, inputs, latent_group, latent_valid, input_group, input_valid, gains, weights, out_grad):
    T, D = latents.shape
    I = inputs.shape[0]
    C = weights["w_q_c"].shape[1]
    F = weights["w_in_a"].shape[1]
    CH = 64
    NCH = T // CH
    HL = C // HEAD_DIM
    in_vmem = dict(
        latent_group=latent_group, latent_valid=latent_valid, input_group=input_group,
        input_valid=input_valid, gains=gains,
    )
    in_any = dict(latents=latents, inputs=inputs, **weights, out_grad=out_grad)
    S = jax.ShapeDtypeStruct
    out_any = dict(
        latents_out=S((T, D), bf16), latent_grad=S((T, D), bf16), input_grad=S((I, D), bf16),
        g_out_b=S((D, F), bf16), g_in_b=S((D, F), bf16), g_self=S((D, 4 * C), bf16),
        g_out_a=S((D, F), bf16), g_in_a=S((D, F), bf16), g_cross=S((D, 4 * C), bf16),
    )
    out_vmem = dict(gains_grad=S((8, D), f32))
    V, DMA = pltpu.VMEM, pltpu.SemaphoreType.DMA
    half, eighth, piece = D // 2, D // 8, D // 16
    scratch = dict(
        inp=V((I, D), bf16), lat=V((T, D), bf16), r4=V((T, D), bf16),
        wkvc=V((D, 2 * C), bf16), wqc=V((D, C), bf16), woc=V((D, C), bf16),
        wina=V((D, F), bf16), wouta=V((D, F), bf16), wqkvs=V((D, 3 * C), bf16),
        wos=V((D, C), bf16), winb=V((D, F), bf16), woutb=V((D, F), bf16), wj=V((D, F), bf16),
        codes=V((8, I + 2 * T), f32), codes_o=V((8, I + 2 * T), f32),
        qcol=V((T, LANES), f32), qcol_o=V((T, LANES), f32),
        part=V((3, T, D), bf16), rin=V((3, T, D), bf16), rmid=V((3, T, D), bf16),
        xs=V((T, D), f32), dxs=V((T, D), f32), gin=V((I, D), bf16),
        an=V((T, D), bf16), bn=V((I, D), bf16), h1=V((T, D), bf16), cs=V((T, D), bf16), h2=V((T, D), bf16),
        rs0=V((T, LANES), f32), rs1=V((I, LANES), f32), rs2=V((T, LANES), f32), rs3=V((T, LANES), f32),
        rs4=V((T, LANES), f32),
        z1=V((T, F), bf16), s1=V((T, F), bf16), du1=V((T, F), bf16), z2=V((T, F), bf16), du2=V((T, F), bf16),
        ra=V((T, D), bf16), rb=V((T, D), bf16),
        q=V((T, C), bf16), kv=V((2 * I, 2 * C), bf16), p_c=V((HL * T, 2 * I), bf16), o_c=V((T, C), bf16),
        q2=V((T, C), bf16), kv2=V((2 * T, 2 * C), bf16), p_s=V((HL * T, 2 * T), bf16), o_s=V((T, C), bf16),
        pr_c=V((HL * T, I), bf16), qr_c=V((T, C), bf16), or_c=V((T, C), bf16),
        pr_s=V((HL * T, T), bf16), qr_s=V((T, C), bf16), or_s=V((T, C), bf16),
        do=V((2, T, C), bf16), do_o=V((2, T, C), bf16), ds=V((2 * HL * T, max(T, I)), bf16),
        dqkv=V((T, 3 * C), bf16), dq=V((T, C), bf16), dkv=V((I, 2 * C), bf16),
        rc=V((3, half, F), bf16), r1p=V((3, eighth, F), bf16), r1q=V((3, eighth, F), bf16),
        r2p=V((3, piece, F), bf16), r2q=V((3, piece, F), bf16),
        dg=V((8, D), f32), dgr=V((3, 8, D), f32), gz=V((8, D), f32), gzr=V((3, 8, D), f32),
        load_sem=DMA((16,)), out_sem=DMA((5,)),
        y_snd=DMA((8,)), y_rcv=DMA((8,)),
        p_snd=DMA((HL * NCH,)), p_rcv=DMA((HL * NCH,)), kv_snd=DMA((NCH,)), kv_rcv=DMA((NCH,)), do_snd=DMA((2, NCH)), do_rcv=DMA((2, NCH)),
        ar_snd=DMA((3, 2 * NCH)), ar_tot=DMA((3, 2 * NCH)), ar_in=DMA((3, 2 * NCH)), ar_mid=DMA((3, 2 * NCH)),
        j_snd=DMA((6, 10)), j_rcv=DMA((6, 10)), j_own=DMA((6, 2)), dg_snd=DMA((3,)), dg_rcv=DMA((3,)), gz_snd=DMA((3,)), gz_rcv=DMA((3,)),
    )
    names = [*in_vmem, *in_any, *out_any, *out_vmem, *scratch]
    outs = pl.pallas_call(
        functools.partial(block_kernel, names, T, I, D, C, F, CH),
        out_shape=(*out_any.values(), *out_vmem.values()),
        in_specs=[pl.BlockSpec(memory_space=pltpu.VMEM)] * len(in_vmem)
        + [pl.BlockSpec(memory_space=pl.ANY)] * len(in_any),
        out_specs=tuple(
            [pl.BlockSpec(memory_space=pl.ANY)] * len(out_any)
            + [pl.BlockSpec(memory_space=pltpu.VMEM)] * len(out_vmem)
        ),
        scratch_shapes=list(scratch.values()),
        compiler_params=pltpu.CompilerParams(
            collective_id=0, has_side_effects=True, vmem_limit_bytes=63 * 2**20
        ),
        name="block_kernel",
    )(*in_vmem.values(), *in_any.values())
    return dict(zip([*out_any, *out_vmem], outs, strict=True))


def widen_kernel(C, n_gains, lat_in, lgrad_in, igrad_in, gains_in, cross, own, in_a, out_a, in_b, out_b,
                 lat, lgrad, igrad, gains, q, kv, o_c, w_in_a, w_out_a, qkv, o_s, w_in_b, w_out_b):
    lat[0] = lat_in[...]
    lgrad[0] = lgrad_in[...].astype(f32)
    igrad[0] = igrad_in[...].astype(f32)
    gains[...] = gains_in[0:n_gains, :]
    for j in range(2):
        kv[:, j, :] = cross[:, j * C : (j + 1) * C].astype(f32)
    q[...] = cross[:, 2 * C : 3 * C].astype(f32)
    o_c[...] = cross[:, 3 * C :].astype(f32)
    for j in range(3):
        qkv[j] = own[:, j * C : (j + 1) * C].astype(f32)
    o_s[...] = own[:, 3 * C :].astype(f32)
    w_in_a[...] = in_a[...].astype(f32)
    w_out_a[...] = out_a[...].astype(f32)
    w_in_b[...] = in_b[...].astype(f32)
    w_out_b[...] = out_b[...].astype(f32)


def widen_call(o, C, n_gains):
    T, D = o["latents_out"].shape
    I = o["input_grad"].shape[0]
    F = o["g_in_a"].shape[1]
    steps = 8
    S = jax.ShapeDtypeStruct

    def flat(n, width):
        return pl.BlockSpec((n // steps, width), lambda i: (i, 0))

    def whole(n, width):
        return pl.BlockSpec((n, width), lambda i: (0, 0))

    def lead(n, width):
        return pl.BlockSpec((1, n // steps, width), lambda i: (0, i, 0))

    ins = ["latents_out", "latent_grad", "input_grad", "gains_grad", "g_cross", "g_self", "g_in_a", "g_out_a", "g_in_b", "g_out_b"]
    big = flat(D, F)
    col = flat(D, C)
    outs = pl.pallas_call(
        functools.partial(widen_kernel, C, n_gains),
        grid=(steps,),
        in_specs=[flat(T, D), flat(T, D), flat(I, D), whole(8, D), big, big, big, big, big, big],
        out_specs=(
            lead(T, D), lead(T, D), lead(I, D), whole(n_gains, D), col,
            pl.BlockSpec((D // steps, 2, C), lambda i: (i, 0, 0)), col, big, big,
            pl.BlockSpec((3, D // steps, C), lambda i: (0, i, 0)), col, big, big,
        ),
        out_shape=(
            S((1, T, D), bf16), S((1, T, D), f32), S((1, I, D), f32), S((n_gains, D), f32), S((D, C), f32),
            S((D, 2, C), f32), S((D, C), f32), S((D, F), f32), S((D, F), f32),
            S((3, D, C), f32), S((D, C), f32), S((D, F), f32), S((D, F), f32),
        ),
        compiler_params=pltpu.CompilerParams(vmem_limit_bytes=62 * 2**20),
        name="widen_kernel",
    )(*[o[n] for n in ins])
    outs = list(outs)
    outs[9] = jnp.moveaxis(outs[9], 0, 1)
    return tuple(outs)


def per_device_fast(
    latents, inputs, latent_group, latent_valid, input_group, input_valid, gains,
    w_q_cross, w_kv_cross, w_o_cross, w_in_a, w_out_a, w_qkv_self, w_o_self, w_in_b, w_out_b, out_grad,
):
    D = latents.shape[2]
    C = w_q_cross.shape[1]
    weights = dict(
        w_q_c=w_q_cross, w_kv_c=w_kv_cross.reshape(D, 2 * C), w_o_c=w_o_cross, w_in_a=w_in_a,
        w_out_a=w_out_a, w_qkv_s=jnp.moveaxis(w_qkv_self, 1, 0), w_o_s=w_o_self, w_in_b=w_in_b, w_out_b=w_out_b,
    )
    o = block_call(
        latents[0], inputs[0], latent_group, latent_valid, input_group, input_valid, gains, weights, out_grad[0]
    )
    return widen_call(o, C, gains.shape[0])


def solution(mesh):
    fast = dict(mesh.shape) == {"group": 4, "blk": 2, "head": 4}
    return jax.shard_map(
        per_device_fast if fast else per_device,
        mesh=mesh,
        in_specs=(
            P("group", "blk", None),
            P("group", "blk", None),
            P("group", "blk"),
            P("group", "blk"),
            P("group", "blk"),
            P("group", "blk"),
            P(),
            P(None, "head"),
            P(None, None, "head"),
            P(None, "head"),
            P(None, "head"),
            P(None, "head"),
            P(None, None, "head"),
            P(None, "head"),
            P(None, "head"),
            P(None, "head"),
            P("group", "blk", None),
        ),
        out_specs=(
            P("group", "blk", None),
            P("group", "blk", None),
            P("group", "blk", None),
            P(),
            P(None, "head"),
            P(None, None, "head"),
            P(None, "head"),
            P(None, "head"),
            P(None, "head"),
            P(None, None, "head"),
            P(None, "head"),
            P(None, "head"),
            P(None, "head"),
        ),
        check_vma=False,
    )
```

```python
import functools
import types

import jax
import jax.numpy as jnp
from jax import lax
from jax.experimental import pallas as pl
from jax.experimental.pallas import tpu as pltpu
from jax.sharding import PartitionSpec as P

HEAD_DIM = 128


masked_fill = -1000.0
contract_last = (((1,), (1,)), ((), ()))


def layer_norm(values, gains_row):
    centred = values - jnp.mean(values, axis=-1, keepdims=True)
    variance = jnp.mean(centred * centred, axis=-1, keepdims=True)
    return centred * lax.rsqrt(variance + 1e-05) * gains_row


def norm_back(values, gains_row, cotangent):
    unused, pullback = jax.vjp(layer_norm, values, gains_row)
    return pullback(cotangent)


def out_product(left, right):
    return lax.dot_general(left, right, contract_last, preferred_element_type=jnp.float32)


def block_rows(item_count):
    if item_count > 1024 and item_count % 1024 == 0:
        return 1024
    return item_count


def head_sum(partial_sum):
    return lax.psum(partial_sum, "head")


def head_grad_sum(partial_sum):
    return lax.psum(partial_sum, "head")


def score_block(query_heads, key_heads, query_code, key_code):
    scores = jnp.einsum(
        "qhd,khd->hqk", query_heads, key_heads, preferred_element_type=jnp.float32
    ) * HEAD_DIM ** (-0.5)
    allowed = query_code[:, None] == key_code[None, :]
    return (jnp.where(allowed[None], scores, masked_fill), allowed)


def cycle_attend(queries, query_code, key_rows, value_rows, key_code):
    row_count = queries.shape[0]
    heads_local = queries.shape[1] // HEAD_DIM
    query_heads = queries.reshape(row_count, heads_local, HEAD_DIM)

    def stats_block(state_carry, block_data):
        running, totals = state_carry
        key_block, code_block = block_data
        key_heads = key_block.reshape(key_block.shape[0], heads_local, HEAD_DIM)
        scores, allowed = score_block(query_heads, key_heads, query_code, code_block)
        largest = jnp.maximum(running, jnp.max(scores, axis=-1))
        totals = totals * jnp.exp(running - largest) + jnp.sum(
            jnp.exp(scores - largest[:, :, None]), axis=-1
        )
        return ((largest, totals), None)

    stats_init = (
        jnp.full((heads_local, row_count), -jnp.inf, jnp.float32),
        jnp.zeros((heads_local, row_count), jnp.float32),
    )
    state_carry = stats_init
    key_piece = lax.all_gather(key_rows, "blk", axis=0, tiled=True)
    code_piece = lax.all_gather(key_code, "blk", axis=0, tiled=True)
    item_count = key_piece.shape[0]
    step_rows = block_rows(item_count)
    block_count = item_count // step_rows
    stacked = (
        key_piece.reshape(block_count, step_rows, key_piece.shape[1]),
        code_piece.reshape(block_count, step_rows),
    )
    state_carry, unused = lax.scan(stats_block, state_carry, stacked)
    running, totals = state_carry
    log_sums = running + jnp.log(totals)

    def one_block(accumulated, block_data):
        key_block, value_block, code_block = block_data
        key_heads = key_block.reshape(key_block.shape[0], heads_local, HEAD_DIM)
        value_heads = value_block.reshape(value_block.shape[0], heads_local, HEAD_DIM)
        scores, allowed = score_block(query_heads, key_heads, query_code, code_block)
        prob_rows = jnp.exp(scores - log_sums[:, :, None]).astype(jnp.bfloat16)
        accumulated = accumulated + jnp.einsum(
            "hqk,khd->qhd", prob_rows, value_heads, preferred_element_type=jnp.float32
        )
        return (accumulated, None)

    initial = jnp.zeros((row_count, heads_local, HEAD_DIM), jnp.float32)
    accumulated = initial
    key_piece = lax.all_gather(key_rows, "blk", axis=0, tiled=True)
    value_piece = lax.all_gather(value_rows, "blk", axis=0, tiled=True)
    code_piece = lax.all_gather(key_code, "blk", axis=0, tiled=True)
    item_count = key_piece.shape[0]
    step_rows = block_rows(item_count)
    block_count = item_count // step_rows
    stacked = (
        key_piece.reshape(block_count, step_rows, key_piece.shape[1]),
        value_piece.reshape(block_count, step_rows, value_piece.shape[1]),
        code_piece.reshape(block_count, step_rows),
    )
    accumulated, unused = lax.scan(one_block, accumulated, stacked)
    mixed = accumulated.reshape(row_count, heads_local * HEAD_DIM)
    return (mixed, log_sums)


def grad_parts(query_rows, grad_rows, query_code, log_sums, deltas, key_rows, value_rows, key_code):
    heads_local = query_rows.shape[1] // HEAD_DIM
    query_heads = query_rows.reshape(query_rows.shape[0], heads_local, HEAD_DIM)
    grad_heads = grad_rows.reshape(grad_rows.shape[0], heads_local, HEAD_DIM)
    key_heads = key_rows.reshape(key_rows.shape[0], heads_local, HEAD_DIM)
    value_heads = value_rows.reshape(value_rows.shape[0], heads_local, HEAD_DIM)
    scores, allowed = score_block(query_heads, key_heads, query_code, key_code)
    prob_rows = jnp.exp(scores - log_sums[:, :, None])
    grad_probs = jnp.einsum(
        "qhd,khd->hqk", grad_heads, value_heads, preferred_element_type=jnp.float32
    )
    grad_scores = jnp.where(
        allowed[None], prob_rows * (grad_probs - deltas[:, :, None]), 0.0
    ).astype(jnp.bfloat16)
    return (query_heads, grad_heads, key_heads, grad_scores, prob_rows)


def query_part(grad_scores, key_heads, row_shape):
    grad_query = jnp.einsum(
        "hqk,khd->qhd", grad_scores, key_heads, preferred_element_type=jnp.float32
    ) * HEAD_DIM ** (-0.5)
    return grad_query.reshape(row_shape)


def key_parts(grad_scores, prob_rows, query_heads, grad_heads, row_shape):
    grad_key = jnp.einsum(
        "hqk,qhd->khd", grad_scores, query_heads, preferred_element_type=jnp.float32
    ) * HEAD_DIM ** (-0.5)
    grad_value = jnp.einsum(
        "hqk,qhd->khd",
        prob_rows.astype(jnp.bfloat16),
        grad_heads,
        preferred_element_type=jnp.float32,
    )
    return (grad_key.reshape(row_shape), grad_value.reshape(row_shape))


def row_delta(grad_mixed, mixed):
    row_count = mixed.shape[0]
    heads_local = mixed.shape[1] // HEAD_DIM
    product = (grad_mixed.astype(jnp.float32) * mixed).reshape(row_count, heads_local, HEAD_DIM)
    return jnp.sum(product, axis=-1).T


def attend_back(queries, grad_mixed, query_code, log_sums, deltas, key_rows, value_rows, key_code):
    row_count = queries.shape[0]
    col_width = queries.shape[1]
    heads_local = col_width // HEAD_DIM
    all_keys, all_values, all_kcodes, all_queries, all_grads, all_qcodes = (
        lax.all_gather(key_rows, "blk", axis=0, tiled=True),
        lax.all_gather(value_rows, "blk", axis=0, tiled=True),
        lax.all_gather(key_code, "blk", axis=0, tiled=True),
        lax.all_gather(queries, "blk", axis=0, tiled=True),
        lax.all_gather(grad_mixed, "blk", axis=0, tiled=True),
        lax.all_gather(query_code, "blk", axis=0, tiled=True),
    )
    all_sums, all_deltas = (
        lax.all_gather(log_sums, "blk", axis=1, tiled=True),
        lax.all_gather(deltas, "blk", axis=1, tiled=True),
    )
    key_total = all_keys.shape[0]
    key_step = block_rows(key_total)
    key_blocks = key_total // key_step

    def own_queries(grad_query, block_data):
        key_block_rows, value_block_rows, code_block = block_data
        parts = grad_parts(
            queries,
            grad_mixed,
            query_code,
            log_sums,
            deltas,
            key_block_rows,
            value_block_rows,
            code_block,
        )
        return (grad_query + query_part(parts[3], parts[2], queries.shape), None)

    key_stack = (
        all_keys.reshape(key_blocks, key_step, col_width),
        all_values.reshape(key_blocks, key_step, col_width),
        all_kcodes.reshape(key_blocks, key_step),
    )
    grad_query, unused = lax.scan(
        own_queries, jnp.zeros((row_count, col_width), jnp.float32), key_stack
    )
    query_total = all_queries.shape[0]
    query_step = block_rows(query_total)
    query_blocks = query_total // query_step
    key_count = key_rows.shape[0]

    def own_keys(state_carry, block_data):
        grad_key, grad_value = state_carry
        query_block_rows, grad_block_rows, code_block, sums_block, deltas_block = block_data
        query_heads, grad_heads, key_heads, grad_scores, prob_rows = grad_parts(
            query_block_rows,
            grad_block_rows,
            code_block,
            sums_block,
            deltas_block,
            key_rows,
            value_rows,
            key_code,
        )
        part_key, part_value = key_parts(
            grad_scores, prob_rows, query_heads, grad_heads, key_rows.shape
        )
        return ((grad_key + part_key, grad_value + part_value), None)

    query_stack = (
        all_queries.reshape(query_blocks, query_step, col_width),
        all_grads.reshape(query_blocks, query_step, col_width),
        all_qcodes.reshape(query_blocks, query_step),
        all_sums.reshape(heads_local, query_blocks, query_step).transpose(1, 0, 2),
        all_deltas.reshape(heads_local, query_blocks, query_step).transpose(1, 0, 2),
    )
    zeros_keys = jnp.zeros((key_count, col_width), jnp.float32)
    (grad_key, grad_value), unused = lax.scan(own_keys, (zeros_keys, zeros_keys), query_stack)
    return (grad_query, grad_key, grad_value)


def mlp_forward(stream, gains_row, weight_in, weight_out):
    hidden_in = layer_norm(stream, gains_row).astype(jnp.bfloat16)
    hidden = jnp.dot(hidden_in, weight_in, preferred_element_type=jnp.float32)
    activated = jax.nn.gelu(hidden).astype(jnp.bfloat16)
    branch = head_sum(out_product(activated, weight_out))
    return (stream + branch, (hidden_in, hidden, activated))


def mlp_backward(stream, gains_row, weight_in, weight_out, saved, grad_stream):
    hidden_in, hidden, activated = saved
    grad_low = grad_stream.astype(jnp.bfloat16)
    grad_weight_out = jnp.einsum(
        "td,tf->df", grad_low, activated, preferred_element_type=jnp.float32
    )
    grad_activated = jnp.dot(grad_low, weight_out, preferred_element_type=jnp.float32)
    unused, gelu_back = jax.vjp(jax.nn.gelu, hidden)
    grad_hidden = gelu_back(grad_activated)[0].astype(jnp.bfloat16)
    grad_weight_in = jnp.einsum(
        "td,tf->df", hidden_in, grad_hidden, preferred_element_type=jnp.float32
    )
    grad_normed = head_grad_sum(out_product(grad_hidden, weight_in))
    grad_input, grad_gain = norm_back(stream, gains_row, grad_normed)
    return (grad_stream + grad_input, grad_gain, grad_weight_in, grad_weight_out)


def self_forward(stream, gains_row, weight_triple, weight_out, query_code, key_code):
    normed_low = layer_norm(stream, gains_row).astype(jnp.bfloat16)
    col_width = weight_triple.shape[2]
    triple = jnp.dot(
        normed_low,
        weight_triple.reshape(weight_triple.shape[0], 3 * col_width),
        preferred_element_type=jnp.float32,
    ).astype(jnp.bfloat16)
    queries = triple[:, :col_width]
    key_rows = triple[:, col_width : 2 * col_width]
    value_rows = triple[:, 2 * col_width :]
    mixed, log_sums = cycle_attend(queries, query_code, key_rows, value_rows, key_code)
    mixed_low = mixed.astype(jnp.bfloat16)
    branch = head_sum(out_product(mixed_low, weight_out))
    return (
        stream + branch,
        (normed_low, queries, key_rows, value_rows, mixed, mixed_low, log_sums),
    )


def self_backward(
    stream, gains_row, weight_triple, weight_out, saved, grad_stream, query_code, key_code
):
    normed_low, queries, key_rows, value_rows, mixed, mixed_low, log_sums = saved
    grad_low = grad_stream.astype(jnp.bfloat16)
    grad_weight_out = jnp.einsum(
        "td,ti->di", grad_low, mixed_low, preferred_element_type=jnp.float32
    )
    grad_mixed = jnp.dot(grad_low, weight_out, preferred_element_type=jnp.float32).astype(
        jnp.bfloat16
    )
    deltas = row_delta(grad_mixed, mixed)
    grad_query, grad_key, grad_value = attend_back(
        queries, grad_mixed, query_code, log_sums, deltas, key_rows, value_rows, key_code
    )
    grad_triple = jnp.concatenate([grad_query, grad_key, grad_value], axis=1).astype(jnp.bfloat16)
    grad_weight_triple = jnp.einsum(
        "td,tc->dc", normed_low, grad_triple, preferred_element_type=jnp.float32
    ).reshape(weight_triple.shape)
    grad_normed = head_grad_sum(
        out_product(grad_triple, weight_triple.reshape(weight_triple.shape[0], -1))
    )
    grad_input, grad_gain = norm_back(stream, gains_row, grad_normed)
    return (grad_stream + grad_input, grad_gain, grad_weight_triple, grad_weight_out)


def cross_forward(
    stream, input_rows, gains, weight_query, weight_pairs, weight_out, query_code, key_code
):
    latent_low = layer_norm(stream, gains[0]).astype(jnp.bfloat16)
    input_low = layer_norm(input_rows, gains[1]).astype(jnp.bfloat16)
    col_width = weight_query.shape[1]
    queries = jnp.dot(latent_low, weight_query, preferred_element_type=jnp.float32).astype(
        jnp.bfloat16
    )
    paired = jnp.dot(
        input_low,
        weight_pairs.reshape(weight_pairs.shape[0], 2 * col_width),
        preferred_element_type=jnp.float32,
    ).astype(jnp.bfloat16)
    key_rows = paired[:, :col_width]
    value_rows = paired[:, col_width:]
    mixed, log_sums = cycle_attend(queries, query_code, key_rows, value_rows, key_code)
    mixed_low = mixed.astype(jnp.bfloat16)
    branch = head_sum(out_product(mixed_low, weight_out))
    return (
        stream + branch,
        (latent_low, input_low, queries, key_rows, value_rows, mixed, mixed_low, log_sums),
    )


def cross_backward(
    stream,
    input_rows,
    gains,
    weight_query,
    weight_pairs,
    weight_out,
    saved,
    grad_stream,
    query_code,
    key_code,
):
    latent_low, input_low, queries, key_rows, value_rows, mixed, mixed_low, log_sums = saved
    grad_low = grad_stream.astype(jnp.bfloat16)
    grad_weight_out = jnp.einsum(
        "td,ti->di", grad_low, mixed_low, preferred_element_type=jnp.float32
    )
    grad_mixed = jnp.dot(grad_low, weight_out, preferred_element_type=jnp.float32).astype(
        jnp.bfloat16
    )
    deltas = row_delta(grad_mixed, mixed)
    grad_query, grad_key, grad_value = attend_back(
        queries, grad_mixed, query_code, log_sums, deltas, key_rows, value_rows, key_code
    )
    grad_query_low = grad_query.astype(jnp.bfloat16)
    grad_pairs = jnp.concatenate([grad_key, grad_value], axis=1).astype(jnp.bfloat16)
    grad_weight_query = jnp.einsum(
        "td,tc->dc", latent_low, grad_query_low, preferred_element_type=jnp.float32
    )
    grad_weight_pairs = jnp.einsum(
        "td,tc->dc", input_low, grad_pairs, preferred_element_type=jnp.float32
    ).reshape(weight_pairs.shape)
    latent_part = out_product(grad_query_low, weight_query)
    input_part = out_product(grad_pairs, weight_pairs.reshape(weight_pairs.shape[0], -1))
    latent_normed, input_normed = lax.psum((latent_part, input_part), "head")
    grad_latent, gain_zero = norm_back(stream, gains[0], latent_normed)
    grad_inputs, gain_one = norm_back(input_rows, gains[1], input_normed)
    return (
        grad_stream + grad_latent,
        grad_inputs,
        gain_zero,
        gain_one,
        grad_weight_query,
        grad_weight_pairs,
        grad_weight_out,
    )


def per_device(
    latents,
    inputs,
    latent_group,
    latent_valid,
    input_group,
    input_valid,
    gains,
    w_q_cross,
    w_kv_cross,
    w_o_cross,
    w_in_a,
    w_out_a,
    w_qkv_self,
    w_o_self,
    w_in_b,
    w_out_b,
    out_grad,
):
    start_stream = latents[0].astype(jnp.float32)
    input_rows = inputs[0].astype(jnp.float32)
    query_code = latent_group[0].astype(jnp.bfloat16)
    input_code = jnp.where(input_valid[0] == 1, input_group[0], -1).astype(jnp.bfloat16)
    self_code = jnp.where(latent_valid[0] == 1, latent_group[0], -1).astype(jnp.bfloat16)
    cross_stream, cross_saved = cross_forward(
        start_stream, input_rows, gains, w_q_cross, w_kv_cross, w_o_cross, query_code, input_code
    )
    middle_stream, first_saved = mlp_forward(cross_stream, gains[2], w_in_a, w_out_a)
    self_stream, self_saved = self_forward(
        middle_stream, gains[3], w_qkv_self, w_o_self, query_code, self_code
    )
    final_stream, second_saved = mlp_forward(self_stream, gains[4], w_in_b, w_out_b)
    grad_stream = out_grad[0].astype(jnp.float32)
    grad_stream, gain_four, grad_in_b, grad_out_b = mlp_backward(
        self_stream, gains[4], w_in_b, w_out_b, second_saved, grad_stream
    )
    grad_stream, gain_three, grad_qkv_self, grad_o_self = self_backward(
        middle_stream,
        gains[3],
        w_qkv_self,
        w_o_self,
        self_saved,
        grad_stream,
        query_code,
        self_code,
    )
    grad_stream, gain_two, grad_in_a, grad_out_a = mlp_backward(
        cross_stream, gains[2], w_in_a, w_out_a, first_saved, grad_stream
    )
    grad_stream, grad_inputs, gain_zero, gain_one, grad_q_cross, grad_kv_cross, grad_o_cross = (
        cross_backward(
            start_stream,
            input_rows,
            gains,
            w_q_cross,
            w_kv_cross,
            w_o_cross,
            cross_saved,
            grad_stream,
            query_code,
            input_code,
        )
    )
    gain_terms = jnp.stack([gain_zero, gain_one, gain_two, gain_three, gain_four], axis=1)
    (
        sum_gains,
        sum_q_cross,
        sum_kv_cross,
        sum_o_cross,
        sum_in_a,
        sum_out_a,
        sum_qkv_self,
        sum_o_self,
        sum_in_b,
        sum_out_b,
    ) = (
        lax.psum_scatter(gain_terms, ("group", "blk"), scatter_dimension=0, tiled=True),
        lax.psum_scatter(grad_q_cross, ("group", "blk"), scatter_dimension=0, tiled=True),
        lax.psum_scatter(grad_kv_cross, ("group", "blk"), scatter_dimension=0, tiled=True),
        lax.psum_scatter(grad_o_cross, ("group", "blk"), scatter_dimension=0, tiled=True),
        lax.psum_scatter(grad_in_a, ("group", "blk"), scatter_dimension=0, tiled=True),
        lax.psum_scatter(grad_out_a, ("group", "blk"), scatter_dimension=0, tiled=True),
        lax.psum_scatter(grad_qkv_self, ("group", "blk"), scatter_dimension=0, tiled=True),
        lax.psum_scatter(grad_o_self, ("group", "blk"), scatter_dimension=0, tiled=True),
        lax.psum_scatter(grad_in_b, ("group", "blk"), scatter_dimension=0, tiled=True),
        lax.psum_scatter(grad_out_b, ("group", "blk"), scatter_dimension=0, tiled=True),
    )
    (
        full_gains,
        full_q_cross,
        full_kv_cross,
        full_o_cross,
        full_in_a,
        full_out_a,
        full_qkv_self,
        full_o_self,
        full_in_b,
        full_out_b,
    ) = (
        lax.all_gather(sum_gains, ("group", "blk"), axis=0, tiled=True),
        lax.all_gather(sum_q_cross, ("group", "blk"), axis=0, tiled=True),
        lax.all_gather(sum_kv_cross, ("group", "blk"), axis=0, tiled=True),
        lax.all_gather(sum_o_cross, ("group", "blk"), axis=0, tiled=True),
        lax.all_gather(sum_in_a, ("group", "blk"), axis=0, tiled=True),
        lax.all_gather(sum_out_a, ("group", "blk"), axis=0, tiled=True),
        lax.all_gather(sum_qkv_self, ("group", "blk"), axis=0, tiled=True),
        lax.all_gather(sum_o_self, ("group", "blk"), axis=0, tiled=True),
        lax.all_gather(sum_in_b, ("group", "blk"), axis=0, tiled=True),
        lax.all_gather(sum_out_b, ("group", "blk"), axis=0, tiled=True),
    )
    return (
        final_stream.astype(jnp.bfloat16)[None],
        grad_stream[None],
        grad_inputs[None],
        full_gains.T,
        full_q_cross,
        full_kv_cross,
        full_o_cross,
        full_in_a,
        full_out_a,
        full_qkv_self,
        full_o_self,
        full_in_b,
        full_out_b,
    )


MESH = pl.DeviceIdType.MESH
bf16, f32 = jnp.bfloat16, jnp.float32
LANES = 128
TILE = 256
SCALE = HEAD_DIM**-0.5
GELU_A = 0.7978845608028654
GELU_B = 0.044715


def dot_nn(a, b):
    return jnp.dot(a, b, preferred_element_type=f32)


def dot_nt(a, b):
    return lax.dot_general(a, b, (((1,), (1,)), ((), ())), preferred_element_type=f32)


def dot_tn(a, b):
    return lax.dot_general(a, b, (((0,), (0,)), ((), ())), preferred_element_type=f32)


def norm_rows(x):
    c = x - jnp.mean(x, axis=-1, keepdims=True)
    rstd = lax.rsqrt(jnp.mean(c * c, axis=-1, keepdims=True) + 1e-05)
    return c * rstd, rstd


def gelu_both(u):
    u2 = u * u
    t = jnp.tanh(GELU_A * u * (1.0 + GELU_B * u2))
    half = 0.5 * (1.0 + t)
    slope = half + 0.5 * u * (1.0 - t * t) * (GELU_A * (1.0 + 3.0 * GELU_B * u2))
    return u * half, slope


def loop(start, stop, body):
    def step(k, carry):
        body(k)
        return carry

    lax.fori_loop(start, stop, step, 0)


SCHEDULE = dict(
    fifth=["At", "Bt", "", "A1", "B1", "", "", ""],
    sixth_put=["A2 St B2"],
    sixth=["A3", "S1", "B3", "", "S2 A4", "", "S3 B4", ""],
    seventh_pre=["Ct Dt"],
    seventh=["A5", "S4", "B5", "", "C1", "A6 B6", "S5", "D1"],
    last_put=["C2 Xt"],
    late_end=["C3 D2 S6"],
    input=["X1", "C4", "D3", "X2 gz1"],
    last=["", "gz2 D4", "C5", "X3 gz3 dg0", "dg1", "X4 D5", "dg2", "dg3"],
    end=["X5 C6 X6 D6"],
)


def block_kernel(names, T, I, D, C, F, CH, *refs):
    r = types.SimpleNamespace(**dict(zip(names, refs, strict=True)))
    NCH = T // CH
    ICH = I // CH
    HL = C // HEAD_DIM
    g = lax.axis_index("group")
    b = lax.axis_index("blk")
    h = lax.axis_index("head")
    is_mid = (h == 1) | (h == 2)
    is_end = jnp.logical_not(is_mid)
    at_pair = (g, b, h ^ 1)
    at_mid = (g, b, 3 - h)
    at_y = (g, 1 - b, h)
    at_x = (g ^ 2, b, h)
    at_core = (g ^ 1, b, h)
    core = g % 2
    xi = g // 2
    gains = r.gains

    def rows(c, n=CH):
        return pl.ds(pl.multiple_of(c * n, n), n)

    def remote(src, dst, send_sem, recv_sem, where):
        return pltpu.make_async_remote_copy(
            src_ref=src, dst_ref=dst, send_sem=send_sem, recv_sem=recv_sem, device_id=where, device_id_type=MESH
        )

    bar = pltpu.get_barrier_semaphore()
    for where in (at_pair, at_y, at_x, at_core):
        pl.semaphore_signal(bar, inc=1, device_id=where, device_id_type=MESH)

    @pl.when(is_mid)
    def _():
        pl.semaphore_signal(bar, inc=1, device_id=at_mid, device_id_type=MESH)

    loads = {}

    def load(src, dst, name):
        cp = pltpu.make_async_copy(src, dst, r.load_sem.at[len(loads)])
        cp.start()
        loads[name] = cp

    load(r.inputs, r.inp, "inp")
    load(r.w_kv_c, r.wkvc, "wkvc")
    load(r.latents, r.lat, "lat")
    load(r.w_q_c, r.wqc, "wqc")
    load(r.w_o_c, r.woc, "woc")
    load(r.w_in_a, r.wina, "wina")
    load(r.w_out_a, r.wouta, "wouta")
    for j in range(3):
        load(r.w_qkv_s.at[j], r.wqkvs.at[:, pl.ds(j * C, C)], "wqkvs%d" % j)
    load(r.w_o_s, r.wos, "wos")
    load(r.w_in_b, r.winb, "winb")
    load(r.w_out_b, r.woutb, "woutb")
    load(r.out_grad, r.r4, "r4")

    lg = r.latent_group[...]
    ic = jnp.where(r.input_valid[...] == 1, r.input_group[...], -1).astype(f32)
    sc = jnp.where(r.latent_valid[...] == 1, lg, -1).astype(f32)
    lgf = lg.astype(f32)
    r.codes[:, 0:I] = jnp.broadcast_to(ic, (8, I))
    r.codes[:, I : I + T] = jnp.broadcast_to(sc, (8, T))
    r.codes[:, I + T : I + 2 * T] = jnp.broadcast_to(lgf, (8, T))

    def make_columns(line, dst):
        for j in range(T // LANES):
            dst[pl.ds(j * LANES, LANES), :] = jnp.transpose(
                jnp.broadcast_to(line[:, j * LANES : (j + 1) * LANES], (LANES, LANES))
            )

    make_columns(lgf, r.qcol)
    r.dg[...] = jnp.zeros_like(r.dg)
    r.gz[...] = jnp.zeros_like(r.gz)

    @pl.when(is_mid)
    def _():
        pl.semaphore_wait(bar, 5)

    @pl.when(is_end)
    def _():
        pl.semaphore_wait(bar, 4)

    def to_y(src, dst, k):
        return remote(src, dst, r.y_snd.at[k], r.y_rcv.at[k], at_y)

    codes_cp = to_y(r.codes, r.codes_o, 0)
    codes_cp.start()

    SUB = 2
    SR = CH // SUB

    def cp_in(p, c):
        rw = rows(c, SR)
        return remote(r.part.at[p, rw], r.rin.at[p, rw], r.ar_snd.at[p, c], r.ar_in.at[p, c], at_pair)

    def cp_mid(p, c):
        rw = rows(c, SR)
        return remote(r.part.at[p, rw], r.rmid.at[p, rw], r.ar_snd.at[p, c], r.ar_mid.at[p, c], at_mid)

    def cp_tot(p, c):
        rw = rows(c, SR)
        return remote(r.rin.at[p, rw], r.rin.at[p, rw], r.ar_tot.at[p, c], r.ar_in.at[p, c], at_pair)

    def subs(c):
        return [c * SUB + k for k in range(SUB)]

    def ar_send(p, c):
        @pl.when(is_end)
        def _():
            for k in subs(c):
                cp_in(p, k).start()

    def ar_put(p, c, value):
        r.part[p, rows(c)] = value.astype(bf16)
        ar_send(p, c)

    def ar_put_wide(p, c, value):
        r.part[p, rows(c, 2 * CH)] = value.astype(bf16)
        ar_send(p, 2 * c)
        ar_send(p, 2 * c + 1)

    def ar_b(p, c):
        @pl.when(is_mid)
        def _():
            for k in subs(c):
                rw = rows(k, SR)
                cp_in(p, k).wait_recv()
                r.part[p, rw] = r.part[p, rw] + r.rin[p, rw]
                cp_mid(p, k).start()

    def ar_c(p, c, prev=None):
        ar_c_mid(p, c, prev)
        ar_c_end(p, c)

    def ar_c_mid(p, c, prev=None):
        @pl.when(is_mid)
        def _():
            for k in subs(c):
                rw = rows(k, SR)
                cp_mid(p, k).wait_recv()
                cp_mid(p, k).wait_send()
                r.rin[p, rw] = r.part[p, rw] + r.rmid[p, rw]
                if prev is not None:
                    cp_tot(prev, k).wait_send()
                cp_tot(p, k).start()

    def ar_c_end(p, c):
        @pl.when(is_end)
        def _():
            for k in subs(c):
                cp_in(p, k).wait_send()
                cp_tot(p, k).wait_recv()

    def drain(p, c):
        @pl.when(is_mid)
        def _():
            for k in subs(c):
                cp_tot(p, k).wait_send()

    def total_of(p, c):
        return r.rin[p, rows(c)].astype(f32)

    half, quarter, eighth, piece = D // 2, D // 4, D // 8, D // 16
    own = core * half
    p_own = own + xi * eighth
    p_oth = own + (1 - xi) * eighth
    q_base = own + quarter
    q_own = q_base + b * eighth
    q_oth = q_base + (1 - b) * eighth
    p_fin, p_fin_oth = p_own + b * piece, p_own + (1 - b) * piece
    q_fin, q_fin_oth = q_own + xi * piece, q_own + (1 - xi) * piece

    def span(start, n):
        return pl.ds(pl.multiple_of(start, piece), n)

    class Job:
        def __init__(self, index, w, rc, out, parts):
            self.j, self.w, self.rc, self.out, self.parts = index, w, rc, out, parts
            self.s = index % 3

        def tiles(self):
            loop(0, D // TILE, self.tile)
            self.cp_core().start()

        def tile(self, t):
            col = 0
            rw = rows(t, TILE)
            for lhs, rhs in self.parts:
                n = rhs.shape[1]
                self.w[rw, col : col + n] = dot_tn(lhs[:, rw], rhs[...]).astype(bf16)
                col += n

        def cp(self, k, src, dst, where):
            return remote(src, dst, r.j_snd.at[self.j, k], r.j_rcv.at[self.j, k], where)

        def cp_core(self):
            return self.cp(0, self.w.at[span((1 - core) * half, half)], self.rc, at_core)

        def cp_p1(self):
            return self.cp(1, self.w.at[span(p_oth, eighth)], r.r1p.at[self.s], at_x)

        def cp_q1(self):
            return self.cp(2, self.w.at[span(q_oth, eighth)], r.r1q.at[self.s], at_y)

        def cp_p2(self):
            return self.cp(3, self.w.at[span(p_fin_oth, piece)], r.r2p.at[self.s], at_y)

        def cp_q2(self):
            return self.cp(4, self.w.at[span(q_fin_oth, piece)], r.r2q.at[self.s], at_x)

        def cp_p3(self):
            return self.cp(5, self.w.at[span(p_fin, piece)], self.out.at[span(p_fin, piece)], at_y)

        def cp_q3(self):
            return self.cp(6, self.w.at[span(q_fin, piece)], self.out.at[span(q_fin, piece)], at_x)

        def cp_p4(self):
            return self.cp(7, self.out.at[span(p_own, eighth)], self.out.at[span(p_own, eighth)], at_x)

        def cp_q4(self):
            return self.cp(8, self.out.at[span(q_own, eighth)], self.out.at[span(q_own, eighth)], at_y)

        def cp_all(self):
            return self.cp(9, self.out.at[span(own, half)], self.out.at[span(own, half)], at_core)

        def cp_keep(self):
            return (
                pltpu.make_async_copy(
                    self.w.at[span(p_fin, piece)], self.out.at[span(p_fin, piece)], r.j_own.at[self.j, 0]
                ),
                pltpu.make_async_copy(
                    self.w.at[span(q_fin, piece)], self.out.at[span(q_fin, piece)], r.j_own.at[self.j, 1]
                ),
            )

        def add(self, start, n, other):
            rw = span(start, n)
            self.w[rw] = self.w[rw] + other[...]

        def s1(self):
            self.cp_core().wait_recv()
            self.add(p_oth, eighth, self.rc.at[span(p_oth - own, eighth)])
            self.cp_p1().start()
            self.add(q_oth, eighth, self.rc.at[span(q_oth - own, eighth)])
            self.cp_q1().start()
            self.add(p_own, eighth, self.rc.at[span(p_own - own, eighth)])
            self.add(q_own, eighth, self.rc.at[span(q_own - own, eighth)])

        def s2(self):
            self.cp_p1().wait_recv()
            self.add(p_own, eighth, r.r1p.at[self.s])
            self.cp_q1().wait_recv()
            self.add(q_own, eighth, r.r1q.at[self.s])
            self.cp_p2().start()
            self.cp_q2().start()

        def s3(self):
            self.cp_p2().wait_recv()
            self.add(p_fin, piece, r.r2p.at[self.s])
            self.cp_p3().start()
            self.cp_q2().wait_recv()
            self.add(q_fin, piece, r.r2q.at[self.s])
            self.cp_q3().start()
            for cp in self.cp_keep():
                cp.start()

        def s4(self):
            for cp in self.cp_keep():
                cp.wait()
            self.cp_p3().wait_recv()
            self.cp_p4().start()
            self.cp_q3().wait_recv()
            self.cp_q4().start()
            for cp in (self.cp_core(), self.cp_p1(), self.cp_q1(), self.cp_p2(), self.cp_q2(), self.cp_p3(), self.cp_q3()):
                cp.wait_send()

        def s5(self):
            self.cp_p4().wait_recv()
            self.cp_q4().wait_recv()
            self.cp_all().start()
            self.cp_p4().wait_send()
            self.cp_q4().wait_send()

        def s6(self):
            self.cp_all().wait()

    job_out_b = Job(0, r.wj, r.rc.at[0], r.g_out_b, [(r.r4, r.z2)])
    job_in_b = Job(1, r.winb, r.rc.at[1], r.g_in_b, [(r.h2, r.du2)])
    job_self = Job(2, r.woutb, r.rc.at[2], r.g_self, [(r.cs, r.dqkv), (r.ra, r.o_s)])
    job_out_a = Job(3, r.p_s, r.z2, r.g_out_a, [(r.lat, r.z1)])
    job_in_a = Job(4, r.wj, r.du2, r.g_in_a, [(r.h1, r.du1)])
    job_cross = Job(5, r.winb, r.h2, r.g_cross, [(r.bn, r.dkv), (r.an, r.dq), (r.ra, r.o_c)])

    def norm_out(x, gain_row, out, rstd_out, rw):
        xhat, rstd = norm_rows(x)
        rstd_out[rw] = jnp.broadcast_to(rstd, (rstd.shape[0], LANES))
        low = (xhat * gains[gain_row : gain_row + 1, :]).astype(bf16)
        out[rw] = low
        return low

    def norm_grad(cot, low_ref, dg_row, gain_row, rstd_ref, rw):
        gain = gains[gain_row : gain_row + 1, :]
        xhat = low_ref[rw].astype(f32) * (1.0 / gain)
        scaled = cot * gain
        mean_one = jnp.mean(scaled, axis=-1, keepdims=True)
        mean_two = jnp.mean(scaled * xhat, axis=-1, keepdims=True)
        if dg_row is not None:
            r.dg[dg_row : dg_row + 1, :] += jnp.sum(cot * xhat, axis=0, keepdims=True)
        return rstd_ref[rw, 0:1] * (scaled - mean_one - xhat * mean_two)

    loads["inp"].wait()
    loads["wkvc"].wait()

    def kv_chunk(k):
        rw = rows(k, LANES)
        low = norm_out(r.inp[rw].astype(f32), 1, r.bn, r.rs1, rw)
        r.kv[rw] = dot_nn(low, r.wkvc[...]).astype(bf16)

    loop(0, I // LANES, kv_chunk)
    kv_cp = to_y(r.kv.at[pl.ds(0, I)], r.kv.at[pl.ds(I, I)], 1)
    kv_cp.start()
    loads["lat"].wait()
    loads["wqc"].wait()

    def q_chunk(k):
        rw = rows(k, LANES)
        low = norm_out(r.lat[rw].astype(f32), 0, r.an, r.rs0, rw)
        r.q[rw] = dot_nn(low, r.wqc[...]).astype(bf16)

    loop(0, T // LANES, q_chunk)
    codes_cp.wait()
    make_columns(r.codes_o[0:1, I + T : I + 2 * T], r.qcol_o)
    kv_cp.wait()
    loads["woc"].wait()

    def attend_chunk(k, q_ref, kv_ref, p_ref, o_ref, start, n):
        rw = rows(k)
        kc = jnp.concatenate([r.codes[0:1, start : start + n], r.codes_o[0:1, start : start + n]], axis=1)
        allowed = r.qcol[rw, 0:1] == kc
        for hd in range(HL):
            cols = slice(hd * HEAD_DIM, (hd + 1) * HEAD_DIM)
            vcols = slice(C + hd * HEAD_DIM, C + (hd + 1) * HEAD_DIM)
            s = jnp.where(allowed, dot_nt(q_ref[rw, cols], kv_ref[:, cols]) * SCALE, masked_fill)
            e = jnp.exp(s - jnp.max(s, axis=-1, keepdims=True))
            p = (e * (1.0 / jnp.sum(e, axis=-1, keepdims=True))).astype(bf16)
            p_ref[rows(k + hd * NCH), :] = p
            o_ref[rw, cols] = dot_nn(p, kv_ref[:, vcols]).astype(bf16)

    def cross_chunk(k):
        attend_chunk(k, r.q, r.kv, r.p_c, r.o_c, 0, I)
        ar_put(0, k, dot_nt(r.o_c[rows(k)], r.woc[...]))

        @pl.when(k >= 4)
        def _():
            ar_b(0, k - 4)

    loop(0, NCH, cross_chunk)

    back_cross = [
        to_y(r.p_c.at[:, pl.ds(I, I)], r.pr_c, 2), to_y(r.q, r.qr_c, 3), to_y(r.o_c, r.or_c, 4),
    ]
    for cp in back_cross:
        cp.start()
    loads["wina"].wait()
    loads["wouta"].wait()

    def first_chunk(m):
        @pl.when((m >= 2) & (m < NCH - 2))
        def _():
            ar_b(0, m + 2)

        ar_c(0, m)
        rw = rows(m)
        x = r.lat[rw].astype(f32) + total_of(0, m)
        r.xs[rw] = x
        low = norm_out(x, 2, r.h1, r.rs2, rw)
        z, slope = gelu_both(dot_nn(low, r.wina[...]))
        z = z.astype(bf16)
        r.z1[rw] = z
        r.s1[rw] = slope.astype(bf16)
        ar_put(1, m, dot_nt(z, r.wouta[...]))

        @pl.when(m >= NCH - 2)
        def _():
            ar_b(1, m + 2 - NCH)

    loop(0, NCH, first_chunk)
    for j in range(3):
        loads["wqkvs%d" % j].wait()
    loads["wos"].wait()

    def kv2_cp(c):
        return remote(r.kv2.at[rows(c)], r.kv2.at[rows(c + NCH)], r.kv_snd.at[c], r.kv_rcv.at[c], at_y)

    def second_chunk(m):
        @pl.when(m < NCH - 2)
        def _():
            ar_b(1, m + 2)

        ar_c(1, m, 0)
        rw = rows(m)
        x = r.xs[rw] + total_of(1, m)
        r.xs[rw] = x
        low = norm_out(x, 3, r.cs, r.rs3, rw)
        qkv = dot_nn(low, r.wqkvs[...]).astype(bf16)
        r.q2[rw] = qkv[:, :C]
        r.kv2[rw] = qkv[:, C:]
        kv2_cp(m).start()

    loop(0, NCH, second_chunk)
    loop(0, NCH, lambda c: kv2_cp(c).wait())

    def p_cp(c):
        return remote(r.p_s.at[rows(c), pl.ds(T, T)], r.pr_s.at[rows(c)], r.p_snd.at[c], r.p_rcv.at[c], at_y)

    q_back = to_y(r.q2, r.qr_s, 6)
    q_back.start()

    def self_chunk(k):
        attend_chunk(k, r.q2, r.kv2, r.p_s, r.o_s, I, T)
        for hd in range(HL):
            p_cp(k + hd * NCH).start()

        ar_put(0, k, dot_nt(r.o_s[rows(k)], r.wos[...]))

        @pl.when(k >= 4)
        def _():
            ar_b(0, k - 4)

    loop(0, NCH, self_chunk)
    o_back = to_y(r.o_s, r.or_s, 7)
    o_back.start()
    loads["winb"].wait()
    loads["woutb"].wait()
    loads["r4"].wait()

    def third_chunk(m):
        @pl.when((m >= 2) & (m < NCH - 2))
        def _():
            ar_b(0, m + 2)

        ar_c(0, m, 1)
        rw = rows(m)
        x = r.xs[rw] + total_of(0, m)
        r.xs[rw] = x
        low = norm_out(x, 4, r.h2, r.rs4, rw)
        z, slope = gelu_both(dot_nn(low, r.winb[...]))
        z = z.astype(bf16)
        r.z2[rw] = z
        du = (dot_nn(r.r4[rw], r.woutb[...]) * slope).astype(bf16)
        r.du2[rw] = du
        ar_put(1, m, dot_nt(du, r.winb[...]))

        @pl.when(m >= NCH - 2)
        def _():
            ar_b(1, m + 2 - NCH)

    loop(0, NCH, third_chunk)

    def d_o_cp(k, c):
        return remote(r.do.at[k, rows(c)], r.do_o.at[k, rows(c)], r.do_snd.at[k, c], r.do_rcv.at[k, c], at_y)

    class Back:
        def __init__(self, k, q, qr, kv, p, pr, o, o_r, n, start, dq, dkv, dkv_col):
            self.k, self.q, self.qr, self.kv, self.p, self.pr, self.o, self.o_r = k, q, qr, kv, p, pr, o, o_r
            self.n, self.first, self.dq, self.dkv, self.dkv_col = n, start, dq, dkv, dkv_col
            self.do, self.do_o = r.do.at[k], r.do_o.at[k]

        def own(self, m):
            rw = rows(m)
            n, a = self.n, self.first
            kc = jnp.concatenate([r.codes[0:1, a : a + n], r.codes_o[0:1, a : a + n]], axis=1)
            allowed = r.qcol[rw, 0:1] == kc
            for hd in range(HL):
                cols = slice(hd * HEAD_DIM, (hd + 1) * HEAD_DIM)
                vcols = slice(C + hd * HEAD_DIM, C + (hd + 1) * HEAD_DIM)
                grad = self.do[rw, cols]
                delta = jnp.sum(grad.astype(f32) * self.o[rw, cols].astype(f32), axis=-1, keepdims=True)
                diff = dot_nt(grad, self.kv[:, vcols]) - delta
                prob = self.p[rows(m + hd * NCH), :].astype(f32)
                ds = jnp.where(allowed, prob * diff, 0.0).astype(bf16)
                r.ds[rows(m + 2 * hd * NCH), 0:n] = ds[:, 0:n]
                self.dq[rw, cols] = (dot_nn(ds, self.kv[:, cols]) * SCALE).astype(bf16)

        def other(self, m):
            d_o_cp(self.k, m).wait()
            rw = rows(m)
            n, a = self.n, self.first
            allowed = r.qcol_o[rw, 0:1] == r.codes[0:1, a : a + n]
            for hd in range(HL):
                cols = slice(hd * HEAD_DIM, (hd + 1) * HEAD_DIM)
                vcols = slice(C + hd * HEAD_DIM, C + (hd + 1) * HEAD_DIM)
                grad = self.do_o[rw, cols]
                delta = jnp.sum(grad.astype(f32) * self.o_r[rw, cols].astype(f32), axis=-1, keepdims=True)
                diff = dot_nt(grad, self.kv[0:n, vcols]) - delta
                prob = self.pr[rows(m + hd * NCH), :].astype(f32)
                ds = jnp.where(allowed, prob * diff, 0.0).astype(bf16)
                r.ds[rows(m + (2 * hd + 1) * NCH), 0:n] = ds

        def some_other(self, m, waits):
            if waits is not None:

                @pl.when(m == NCH // 2)
                def _():
                    for wait in waits:
                        wait()

            @pl.when((m >= NCH // 2) & (m < NCH - 2))
            def _():
                self.other(2 * m - NCH)
                self.other(2 * m + 1 - NCH)

            @pl.when(m == NCH - 2)
            def _():
                self.other(NCH - 4)

            @pl.when(m == NCH - 1)
            def _():
                self.other(NCH - 3)

        def keys_own(self):
            n = self.n
            out = []
            for hd in range(HL):
                cols = slice(hd * HEAD_DIM, (hd + 1) * HEAD_DIM)
                at = 2 * hd * T
                dk = dot_tn(r.ds[at : at + T, 0:n], self.q[:, cols])
                dv = dot_tn(self.p[hd * T : (hd + 1) * T, 0:n], self.do[:, cols])
                out.append((dk, dv))
            return out

        def keys(self, own):
            n = self.n
            for hd, (dk, dv) in enumerate(own):
                cols = slice(hd * HEAD_DIM, (hd + 1) * HEAD_DIM)
                at = (2 * hd + 1) * T
                dk = dk + dot_tn(r.ds[at : at + T, 0:n], self.qr[:, cols])
                dv = dv + dot_tn(self.pr[hd * T : (hd + 1) * T, :], self.do_o[:, cols])
                col = self.dkv_col + hd * HEAD_DIM
                self.dkv[:, col : col + HEAD_DIM] = (dk * SCALE).astype(bf16)
                self.dkv[:, col + C : col + C + HEAD_DIM] = dv.astype(bf16)

    back_of_self = Back(0, r.q2, r.qr_s, r.kv2, r.p_s, r.pr_s, r.o_s, r.or_s, T, I, r.dqkv, r.dqkv, C)
    back_of_cross = Back(1, r.q, r.qr_c, r.kv, r.p_c, r.pr_c, r.o_c, r.or_c, I, 0, r.dq, r.dkv, 0)

    jobs = dict(A=job_out_b, B=job_in_b, S=job_self, C=job_out_a, D=job_in_a, X=job_cross)
    extra = {}

    def on(place, m=None):
        for step, words in enumerate(SCHEDULE[place]):
            names = words.split()
            if not names:
                continue

            def run(names=names):
                for name in names:
                    if name in extra:
                        extra[name]()
                    else:
                        getattr(jobs[name[0]], "tiles" if name[1] == "t" else "s" + name[1])()

            if m is None:
                run()
            else:
                pl.when(m == step)(run)

    def fifth_chunk(m):
        @pl.when(m < NCH - 2)
        def _():
            ar_b(1, m + 2)

        ar_c(1, m, 0)
        rw = rows(m)
        dx = r.r4[rw].astype(f32) + norm_grad(total_of(1, m), r.h2, 4, 4, r.rs4, rw)
        r.dxs[rw] = dx
        low = dx.astype(bf16)
        r.ra[rw] = low
        r.do[0, rw] = dot_nn(low, r.wos[...]).astype(bf16)
        d_o_cp(0, m).start()

        @pl.when(m < NCH // 2)
        def _():
            wide = rows(m, 2 * CH)
            r.part[2, wide] = dot_nt(r.z2[wide], r.woutb[...]).astype(bf16)

        @pl.when(m < NCH // 4)
        def _():
            ar_send(2, 2 * m)
            ar_send(2, 2 * m + 1)

        back_of_self.own(m)
        back_of_self.some_other(m, [q_back.wait, o_back.wait, lambda: loop(0, HL * NCH, lambda c: p_cp(c).wait())])

        on("fifth", m)

        @pl.when(m >= NCH // 2)
        def _():
            ar_b(2, m - NCH // 2)

    loop(0, NCH, fifth_chunk)

    def late_out(c):
        ar_c_end(2, c)
        rw = rows(c)
        r.part[2, rw] = (r.xs[rw] + total_of(2, c)).astype(bf16)

    self_keys = back_of_self.keys_own()
    back_of_self.other(NCH - 2)
    back_of_self.other(NCH - 1)
    back_of_self.keys(self_keys)
    def sixth_put(k):
        ar_put_wide(0, k, dot_nt(r.dqkv[rows(k, 2 * CH)], r.wqkvs[...]))

    loop(0, NCH // 2, sixth_put)
    loop(0, NCH // 2, lambda c: ar_c_mid(2, c))
    on("sixth_put")
    loop(0, 2, lambda c: ar_b(0, c))

    def sixth_chunk(m):
        @pl.when(m < NCH - 2)
        def _():
            ar_b(0, m + 2)

        ar_c(0, m, 1)
        rw = rows(m)
        dx = r.dxs[rw] + norm_grad(total_of(0, m), r.cs, 3, 3, r.rs3, rw)
        r.dxs[rw] = dx
        low = dx.astype(bf16)
        r.lat[rw] = low
        du = (dot_nn(low, r.wouta[...]) * r.s1[rw].astype(f32)).astype(bf16)
        r.du1[rw] = du
        ar_put(1, m, dot_nt(du, r.wina[...]))

        @pl.when(m >= NCH - 2)
        def _():
            ar_b(1, m + 2 - NCH)

        @pl.when(m < NCH // 2)
        def _():
            late_out(m)

        on("sixth", m)

    loop(0, NCH, sixth_chunk)
    late_cps = [
        pltpu.make_async_copy(r.part.at[2, rw], r.latents_out.at[rw], r.out_sem.at[2 + 2 * k])
        for k, rw in enumerate([pl.ds(0, T // 2), pl.ds(T // 2, T // 2)])
    ]
    late_cps[0].start()
    def seventh_chunk(m):
        @pl.when(m < NCH - 2)
        def _():
            ar_b(1, m + 2)

        @pl.when(m < NCH // 2)
        def _():
            drain(2, m)

        ar_c(1, m, 0)
        rw = rows(m)
        dx = r.dxs[rw] + norm_grad(total_of(1, m), r.h1, 2, 2, r.rs2, rw)
        r.dxs[rw] = dx
        low = dx.astype(bf16)
        r.ra[rw] = low
        r.do[1, rw] = dot_nn(low, r.woc[...]).astype(bf16)
        d_o_cp(1, m).start()
        back_of_cross.own(m)
        back_of_cross.some_other(m, [cp.wait for cp in back_cross])

        on("seventh", m)

        @pl.when(m >= NCH // 2)
        def _():
            ar_b(2, m)

    on("seventh_pre")
    loop(NCH // 2, NCH, lambda c: ar_send(2, c))
    loop(0, NCH, seventh_chunk)

    cross_keys = back_of_cross.keys_own()
    back_of_cross.other(NCH - 2)
    back_of_cross.other(NCH - 1)
    back_of_cross.keys(cross_keys)

    late_cps[0].wait()

    def put_last(p, k, value, low_ref, gain_row):
        ar_put_wide(p, k, value)
        xhat = low_ref[rows(k, 2 * CH)].astype(f32) * (1.0 / gains[gain_row : gain_row + 1, :])
        r.gz[gain_row : gain_row + 1, :] += jnp.sum(value * xhat, axis=0, keepdims=True)

    loop(0, ICH // 2, lambda k: put_last(2, k, dot_nt(r.dkv[rows(k, 2 * CH)], r.wkvc[...]), r.bn, 1))
    loop(0, NCH // 2, lambda k: put_last(0, k, dot_nt(r.dq[rows(k, 2 * CH)], r.wqc[...]), r.an, 0))

    def gz_cp(k, where):
        return remote(r.gz, r.gzr.at[k], r.gz_snd.at[k], r.gz_rcv.at[k], where)

    @pl.when(is_end)
    def _():
        gz_cp(0, at_pair).start()

    def gz_one():
        @pl.when(is_mid)
        def _():
            gz_cp(0, at_pair).wait_recv()
            r.gz[...] += r.gzr[0]
            gz_cp(1, at_mid).start()

    def gz_two():
        @pl.when(is_mid)
        def _():
            gz_cp(1, at_mid).wait()
            r.gz[...] += r.gzr[1]
            gz_cp(2, at_pair).start()

    def gz_three():
        @pl.when(is_end)
        def _():
            gz_cp(0, at_pair).wait_send()
            gz_cp(2, at_pair).wait_recv()
            r.dg[0:2, :] = r.gzr[2, 0:2, :]

        @pl.when(is_mid)
        def _():
            gz_cp(2, at_pair).wait_send()
            r.dg[0:2, :] = r.gz[0:2, :]

    def dg_cp(k):
        return remote(r.dg, r.dgr.at[k], r.dg_snd.at[k], r.dg_rcv.at[k], (at_core, at_x, at_y)[k])

    def dg_next(k):
        def step():
            dg_cp(k).wait()
            r.dg[...] += r.dgr[k]
            if k < 2:
                dg_cp(k + 1).start()

        return step

    dg_zero, dg_one, dg_two = (dg_next(k) for k in range(3))

    on("last_put")
    loop(NCH // 2, NCH, lambda c: ar_c_mid(2, c))
    on("late_end")
    loop(0, 2, lambda c: ar_b(2, c))

    extra.update(gz1=gz_one, gz2=gz_two, gz3=gz_three, dg0=dg_cp(0).start, dg1=dg_zero, dg2=dg_one, dg3=dg_two)

    def input_chunk(m):
        @pl.when(m < ICH - 2)
        def _():
            ar_b(2, m + 2)

        @pl.when(m >= ICH - 2)
        def _():
            ar_b(0, m + 2 - ICH)

        ar_c(2, m)
        rw = rows(m)
        r.inp[rw] = norm_grad(total_of(2, m), r.bn, None, 1, r.rs1, rw).astype(bf16)

        late_out(m + NCH // 2)
        on("input", m)

    loop(0, ICH, input_chunk)
    out_cps = [
        pltpu.make_async_copy(r.inp, r.input_grad, r.out_sem.at[0]),
        pltpu.make_async_copy(r.lat.at[pl.ds(0, T // 2)], r.latent_grad.at[pl.ds(0, T // 2)], r.out_sem.at[1]),
        pltpu.make_async_copy(r.lat.at[pl.ds(T // 2, T // 2)], r.latent_grad.at[pl.ds(T // 2, T // 2)], r.out_sem.at[3]),
    ]
    out_cps[0].start()
    late_cps[1].start()

    def last_chunk(m):
        @pl.when(m < NCH - 2)
        def _():
            ar_b(0, m + 2)

        ar_c(0, m, 1)
        rw = rows(m)
        r.lat[rw] = (r.dxs[rw] + norm_grad(total_of(0, m), r.an, None, 0, r.rs0, rw)).astype(bf16)

        @pl.when(m == 4)
        def _():
            out_cps[1].start()

        on("last", m)

    loop(0, NCH, last_chunk)
    out_cps[2].start()
    r.gains_grad[...] = r.dg[...]
    on("end")

    loop(0, NCH, lambda c: drain(2, c))
    loop(0, NCH, lambda c: drain(0, c))

    for cp in [*out_cps, late_cps[1]]:
        cp.wait()


def block_call(latents, inputs, latent_group, latent_valid, input_group, input_valid, gains, weights, out_grad):
    T, D = latents.shape
    I = inputs.shape[0]
    C = weights["w_q_c"].shape[1]
    F = weights["w_in_a"].shape[1]
    CH = 64
    NCH = T // CH
    HL = C // HEAD_DIM
    in_vmem = dict(
        latent_group=latent_group, latent_valid=latent_valid, input_group=input_group,
        input_valid=input_valid, gains=gains,
    )
    in_any = dict(latents=latents, inputs=inputs, **weights, out_grad=out_grad)
    S = jax.ShapeDtypeStruct
    out_any = dict(
        latents_out=S((T, D), bf16), latent_grad=S((T, D), bf16), input_grad=S((I, D), bf16),
        g_out_b=S((D, F), bf16), g_in_b=S((D, F), bf16), g_self=S((D, 4 * C), bf16),
        g_out_a=S((D, F), bf16), g_in_a=S((D, F), bf16), g_cross=S((D, 4 * C), bf16),
    )
    out_vmem = dict(gains_grad=S((8, D), f32))
    V, DMA = pltpu.VMEM, pltpu.SemaphoreType.DMA
    half, eighth, piece = D // 2, D // 8, D // 16
    scratch = dict(
        inp=V((I, D), bf16), lat=V((T, D), bf16), r4=V((T, D), bf16),
        wkvc=V((D, 2 * C), bf16), wqc=V((D, C), bf16), woc=V((D, C), bf16),
        wina=V((D, F), bf16), wouta=V((D, F), bf16), wqkvs=V((D, 3 * C), bf16),
        wos=V((D, C), bf16), winb=V((D, F), bf16), woutb=V((D, F), bf16), wj=V((D, F), bf16),
        codes=V((8, I + 2 * T), f32), codes_o=V((8, I + 2 * T), f32),
        qcol=V((T, LANES), f32), qcol_o=V((T, LANES), f32),
        part=V((3, T, D), bf16), rin=V((3, T, D), bf16), rmid=V((3, T, D), bf16),
        xs=V((T, D), f32), dxs=V((T, D), f32),
        an=V((T, D), bf16), bn=V((I, D), bf16), h1=V((T, D), bf16), cs=V((T, D), bf16), h2=V((T, D), bf16),
        rs0=V((T, LANES), f32), rs1=V((I, LANES), f32), rs2=V((T, LANES), f32), rs3=V((T, LANES), f32),
        rs4=V((T, LANES), f32),
        z1=V((T, F), bf16), s1=V((T, F), bf16), du1=V((T, F), bf16), z2=V((T, F), bf16), du2=V((T, F), bf16),
        ra=V((T, D), bf16),
        q=V((T, C), bf16), kv=V((2 * I, 2 * C), bf16), p_c=V((HL * T, 2 * I), bf16), o_c=V((T, C), bf16),
        q2=V((T, C), bf16), kv2=V((2 * T, 2 * C), bf16), p_s=V((HL * T, 2 * T), bf16), o_s=V((T, C), bf16),
        pr_c=V((HL * T, I), bf16), qr_c=V((T, C), bf16), or_c=V((T, C), bf16),
        pr_s=V((HL * T, T), bf16), qr_s=V((T, C), bf16), or_s=V((T, C), bf16),
        do=V((2, T, C), bf16), do_o=V((2, T, C), bf16), ds=V((2 * HL * T, max(T, I)), bf16),
        dqkv=V((T, 3 * C), bf16), dq=V((T, C), bf16), dkv=V((I, 2 * C), bf16),
        rc=V((3, half, F), bf16), r1p=V((3, eighth, F), bf16), r1q=V((3, eighth, F), bf16),
        r2p=V((3, piece, F), bf16), r2q=V((3, piece, F), bf16),
        dg=V((8, D), f32), dgr=V((3, 8, D), f32), gz=V((8, D), f32), gzr=V((3, 8, D), f32),
        load_sem=DMA((16,)), out_sem=DMA((5,)),
        y_snd=DMA((8,)), y_rcv=DMA((8,)),
        p_snd=DMA((HL * NCH,)), p_rcv=DMA((HL * NCH,)), kv_snd=DMA((NCH,)), kv_rcv=DMA((NCH,)), do_snd=DMA((2, NCH)), do_rcv=DMA((2, NCH)),
        ar_snd=DMA((3, 2 * NCH)), ar_tot=DMA((3, 2 * NCH)), ar_in=DMA((3, 2 * NCH)), ar_mid=DMA((3, 2 * NCH)),
        j_snd=DMA((6, 10)), j_rcv=DMA((6, 10)), j_own=DMA((6, 2)), dg_snd=DMA((3,)), dg_rcv=DMA((3,)), gz_snd=DMA((3,)), gz_rcv=DMA((3,)),
    )
    names = [*in_vmem, *in_any, *out_any, *out_vmem, *scratch]
    outs = pl.pallas_call(
        functools.partial(block_kernel, names, T, I, D, C, F, CH),
        out_shape=(*out_any.values(), *out_vmem.values()),
        in_specs=[pl.BlockSpec(memory_space=pltpu.VMEM)] * len(in_vmem)
        + [pl.BlockSpec(memory_space=pl.ANY)] * len(in_any),
        out_specs=tuple(
            [pl.BlockSpec(memory_space=pl.ANY)] * len(out_any)
            + [pl.BlockSpec(memory_space=pltpu.VMEM)] * len(out_vmem)
        ),
        scratch_shapes=list(scratch.values()),
        compiler_params=pltpu.CompilerParams(
            collective_id=0, has_side_effects=True, vmem_limit_bytes=66900000
        ),
        name="block_kernel",
    )(*in_vmem.values(), *in_any.values())
    return dict(zip([*out_any, *out_vmem], outs, strict=True))


def widen_kernel(C, n_gains, lat_in, lgrad_in, igrad_in, gains_in, cross, own, in_a, out_a, in_b, out_b,
                 lat, lgrad, igrad, gains, q, kv, o_c, w_in_a, w_out_a, qkv, o_s, w_in_b, w_out_b):
    lat[0] = lat_in[...]
    lgrad[0] = lgrad_in[...].astype(f32)
    igrad[0] = igrad_in[...].astype(f32)
    gains[...] = gains_in[0:n_gains, :]
    for j in range(2):
        kv[:, j, :] = cross[:, j * C : (j + 1) * C].astype(f32)
    q[...] = cross[:, 2 * C : 3 * C].astype(f32)
    o_c[...] = cross[:, 3 * C :].astype(f32)
    for j in range(3):
        qkv[j] = own[:, j * C : (j + 1) * C].astype(f32)
    o_s[...] = own[:, 3 * C :].astype(f32)
    w_in_a[...] = in_a[...].astype(f32)
    w_out_a[...] = out_a[...].astype(f32)
    w_in_b[...] = in_b[...].astype(f32)
    w_out_b[...] = out_b[...].astype(f32)


def widen_call(o, C, n_gains):
    T, D = o["latents_out"].shape
    I = o["input_grad"].shape[0]
    F = o["g_in_a"].shape[1]
    steps = 4
    S = jax.ShapeDtypeStruct

    def flat(n, width):
        return pl.BlockSpec((n // steps, width), lambda i: (i, 0))

    def whole(n, width):
        return pl.BlockSpec((n, width), lambda i: (0, 0))

    def lead(n, width):
        return pl.BlockSpec((1, n // steps, width), lambda i: (0, i, 0))

    ins = ["latents_out", "latent_grad", "input_grad", "gains_grad", "g_cross", "g_self", "g_in_a", "g_out_a", "g_in_b", "g_out_b"]
    big = flat(D, F)
    col = flat(D, C)
    outs = pl.pallas_call(
        functools.partial(widen_kernel, C, n_gains),
        grid=(steps,),
        in_specs=[flat(T, D), flat(T, D), flat(I, D), whole(8, D), big, big, big, big, big, big],
        out_specs=(
            lead(T, D), lead(T, D), lead(I, D), whole(n_gains, D), col,
            pl.BlockSpec((D // steps, 2, C), lambda i: (i, 0, 0)), col, big, big,
            pl.BlockSpec((3, D // steps, C), lambda i: (0, i, 0)), col, big, big,
        ),
        out_shape=(
            S((1, T, D), bf16), S((1, T, D), f32), S((1, I, D), f32), S((n_gains, D), f32), S((D, C), f32),
            S((D, 2, C), f32), S((D, C), f32), S((D, F), f32), S((D, F), f32),
            S((3, D, C), f32), S((D, C), f32), S((D, F), f32), S((D, F), f32),
        ),
        compiler_params=pltpu.CompilerParams(vmem_limit_bytes=62 * 2**20),
        name="widen_kernel",
    )(*[o[n] for n in ins])
    outs = list(outs)
    outs[9] = jnp.moveaxis(outs[9], 0, 1)
    return tuple(outs)


def per_device_fast(
    latents, inputs, latent_group, latent_valid, input_group, input_valid, gains,
    w_q_cross, w_kv_cross, w_o_cross, w_in_a, w_out_a, w_qkv_self, w_o_self, w_in_b, w_out_b, out_grad,
):
    D = latents.shape[2]
    C = w_q_cross.shape[1]
    weights = dict(
        w_q_c=w_q_cross, w_kv_c=w_kv_cross.reshape(D, 2 * C), w_o_c=w_o_cross, w_in_a=w_in_a,
        w_out_a=w_out_a, w_qkv_s=jnp.moveaxis(w_qkv_self, 1, 0), w_o_s=w_o_self, w_in_b=w_in_b, w_out_b=w_out_b,
    )
    o = block_call(
        latents[0], inputs[0], latent_group, latent_valid, input_group, input_valid, gains, weights, out_grad[0]
    )
    return widen_call(o, C, gains.shape[0])


def solution(mesh):
    fast = dict(mesh.shape) == {"group": 4, "blk": 2, "head": 4}
    return jax.shard_map(
        per_device_fast if fast else per_device,
        mesh=mesh,
        in_specs=(
            P("group", "blk", None),
            P("group", "blk", None),
            P("group", "blk"),
            P("group", "blk"),
            P("group", "blk"),
            P("group", "blk"),
            P(),
            P(None, "head"),
            P(None, None, "head"),
            P(None, "head"),
            P(None, "head"),
            P(None, "head"),
            P(None, None, "head"),
            P(None, "head"),
            P(None, "head"),
            P(None, "head"),
            P("group", "blk", None),
        ),
        out_specs=(
            P("group", "blk", None),
            P("group", "blk", None),
            P("group", "blk", None),
            P(),
            P(None, "head"),
            P(None, None, "head"),
            P(None, "head"),
            P(None, "head"),
            P(None, "head"),
            P(None, None, "head"),
            P(None, "head"),
            P(None, "head"),
            P(None, "head"),
        ),
        check_vma=False,
    )
```

```python
import functools
import types

import jax
import jax.numpy as jnp
from jax import lax
from jax.experimental import pallas as pl
from jax.experimental.pallas import tpu as pltpu
from jax.sharding import PartitionSpec as P

HEAD_DIM = 128


masked_fill = -1000.0
contract_last = (((1,), (1,)), ((), ()))


def layer_norm(values, gains_row):
    centred = values - jnp.mean(values, axis=-1, keepdims=True)
    variance = jnp.mean(centred * centred, axis=-1, keepdims=True)
    return centred * lax.rsqrt(variance + 1e-05) * gains_row


def norm_back(values, gains_row, cotangent):
    unused, pullback = jax.vjp(layer_norm, values, gains_row)
    return pullback(cotangent)


def out_product(left, right):
    return lax.dot_general(left, right, contract_last, preferred_element_type=jnp.float32)


def block_rows(item_count):
    if item_count > 1024 and item_count % 1024 == 0:
        return 1024
    return item_count


def head_sum(partial_sum):
    return lax.psum(partial_sum, "head")


def head_grad_sum(partial_sum):
    return lax.psum(partial_sum, "head")


def score_block(query_heads, key_heads, query_code, key_code):
    scores = jnp.einsum(
        "qhd,khd->hqk", query_heads, key_heads, preferred_element_type=jnp.float32
    ) * HEAD_DIM ** (-0.5)
    allowed = query_code[:, None] == key_code[None, :]
    return (jnp.where(allowed[None], scores, masked_fill), allowed)


def cycle_attend(queries, query_code, key_rows, value_rows, key_code):
    row_count = queries.shape[0]
    heads_local = queries.shape[1] // HEAD_DIM
    query_heads = queries.reshape(row_count, heads_local, HEAD_DIM)

    def stats_block(state_carry, block_data):
        running, totals = state_carry
        key_block, code_block = block_data
        key_heads = key_block.reshape(key_block.shape[0], heads_local, HEAD_DIM)
        scores, allowed = score_block(query_heads, key_heads, query_code, code_block)
        largest = jnp.maximum(running, jnp.max(scores, axis=-1))
        totals = totals * jnp.exp(running - largest) + jnp.sum(
            jnp.exp(scores - largest[:, :, None]), axis=-1
        )
        return ((largest, totals), None)

    stats_init = (
        jnp.full((heads_local, row_count), -jnp.inf, jnp.float32),
        jnp.zeros((heads_local, row_count), jnp.float32),
    )
    state_carry = stats_init
    key_piece = lax.all_gather(key_rows, "blk", axis=0, tiled=True)
    code_piece = lax.all_gather(key_code, "blk", axis=0, tiled=True)
    item_count = key_piece.shape[0]
    step_rows = block_rows(item_count)
    block_count = item_count // step_rows
    stacked = (
        key_piece.reshape(block_count, step_rows, key_piece.shape[1]),
        code_piece.reshape(block_count, step_rows),
    )
    state_carry, unused = lax.scan(stats_block, state_carry, stacked)
    running, totals = state_carry
    log_sums = running + jnp.log(totals)

    def one_block(accumulated, block_data):
        key_block, value_block, code_block = block_data
        key_heads = key_block.reshape(key_block.shape[0], heads_local, HEAD_DIM)
        value_heads = value_block.reshape(value_block.shape[0], heads_local, HEAD_DIM)
        scores, allowed = score_block(query_heads, key_heads, query_code, code_block)
        prob_rows = jnp.exp(scores - log_sums[:, :, None]).astype(jnp.bfloat16)
        accumulated = accumulated + jnp.einsum(
            "hqk,khd->qhd", prob_rows, value_heads, preferred_element_type=jnp.float32
        )
        return (accumulated, None)

    initial = jnp.zeros((row_count, heads_local, HEAD_DIM), jnp.float32)
    accumulated = initial
    key_piece = lax.all_gather(key_rows, "blk", axis=0, tiled=True)
    value_piece = lax.all_gather(value_rows, "blk", axis=0, tiled=True)
    code_piece = lax.all_gather(key_code, "blk", axis=0, tiled=True)
    item_count = key_piece.shape[0]
    step_rows = block_rows(item_count)
    block_count = item_count // step_rows
    stacked = (
        key_piece.reshape(block_count, step_rows, key_piece.shape[1]),
        value_piece.reshape(block_count, step_rows, value_piece.shape[1]),
        code_piece.reshape(block_count, step_rows),
    )
    accumulated, unused = lax.scan(one_block, accumulated, stacked)
    mixed = accumulated.reshape(row_count, heads_local * HEAD_DIM)
    return (mixed, log_sums)


def grad_parts(query_rows, grad_rows, query_code, log_sums, deltas, key_rows, value_rows, key_code):
    heads_local = query_rows.shape[1] // HEAD_DIM
    query_heads = query_rows.reshape(query_rows.shape[0], heads_local, HEAD_DIM)
    grad_heads = grad_rows.reshape(grad_rows.shape[0], heads_local, HEAD_DIM)
    key_heads = key_rows.reshape(key_rows.shape[0], heads_local, HEAD_DIM)
    value_heads = value_rows.reshape(value_rows.shape[0], heads_local, HEAD_DIM)
    scores, allowed = score_block(query_heads, key_heads, query_code, key_code)
    prob_rows = jnp.exp(scores - log_sums[:, :, None])
    grad_probs = jnp.einsum(
        "qhd,khd->hqk", grad_heads, value_heads, preferred_element_type=jnp.float32
    )
    grad_scores = jnp.where(
        allowed[None], prob_rows * (grad_probs - deltas[:, :, None]), 0.0
    ).astype(jnp.bfloat16)
    return (query_heads, grad_heads, key_heads, grad_scores, prob_rows)


def query_part(grad_scores, key_heads, row_shape):
    grad_query = jnp.einsum(
        "hqk,khd->qhd", grad_scores, key_heads, preferred_element_type=jnp.float32
    ) * HEAD_DIM ** (-0.5)
    return grad_query.reshape(row_shape)


def key_parts(grad_scores, prob_rows, query_heads, grad_heads, row_shape):
    grad_key = jnp.einsum(
        "hqk,qhd->khd", grad_scores, query_heads, preferred_element_type=jnp.float32
    ) * HEAD_DIM ** (-0.5)
    grad_value = jnp.einsum(
        "hqk,qhd->khd",
        prob_rows.astype(jnp.bfloat16),
        grad_heads,
        preferred_element_type=jnp.float32,
    )
    return (grad_key.reshape(row_shape), grad_value.reshape(row_shape))


def row_delta(grad_mixed, mixed):
    row_count = mixed.shape[0]
    heads_local = mixed.shape[1] // HEAD_DIM
    product = (grad_mixed.astype(jnp.float32) * mixed).reshape(row_count, heads_local, HEAD_DIM)
    return jnp.sum(product, axis=-1).T


def attend_back(queries, grad_mixed, query_code, log_sums, deltas, key_rows, value_rows, key_code):
    row_count = queries.shape[0]
    col_width = queries.shape[1]
    heads_local = col_width // HEAD_DIM
    all_keys, all_values, all_kcodes, all_queries, all_grads, all_qcodes = (
        lax.all_gather(key_rows, "blk", axis=0, tiled=True),
        lax.all_gather(value_rows, "blk", axis=0, tiled=True),
        lax.all_gather(key_code, "blk", axis=0, tiled=True),
        lax.all_gather(queries, "blk", axis=0, tiled=True),
        lax.all_gather(grad_mixed, "blk", axis=0, tiled=True),
        lax.all_gather(query_code, "blk", axis=0, tiled=True),
    )
    all_sums, all_deltas = (
        lax.all_gather(log_sums, "blk", axis=1, tiled=True),
        lax.all_gather(deltas, "blk", axis=1, tiled=True),
    )
    key_total = all_keys.shape[0]
    key_step = block_rows(key_total)
    key_blocks = key_total // key_step

    def own_queries(grad_query, block_data):
        key_block_rows, value_block_rows, code_block = block_data
        parts = grad_parts(
            queries,
            grad_mixed,
            query_code,
            log_sums,
            deltas,
            key_block_rows,
            value_block_rows,
            code_block,
        )
        return (grad_query + query_part(parts[3], parts[2], queries.shape), None)

    key_stack = (
        all_keys.reshape(key_blocks, key_step, col_width),
        all_values.reshape(key_blocks, key_step, col_width),
        all_kcodes.reshape(key_blocks, key_step),
    )
    grad_query, unused = lax.scan(
        own_queries, jnp.zeros((row_count, col_width), jnp.float32), key_stack
    )
    query_total = all_queries.shape[0]
    query_step = block_rows(query_total)
    query_blocks = query_total // query_step
    key_count = key_rows.shape[0]

    def own_keys(state_carry, block_data):
        grad_key, grad_value = state_carry
        query_block_rows, grad_block_rows, code_block, sums_block, deltas_block = block_data
        query_heads, grad_heads, key_heads, grad_scores, prob_rows = grad_parts(
            query_block_rows,
            grad_block_rows,
            code_block,
            sums_block,
            deltas_block,
            key_rows,
            value_rows,
            key_code,
        )
        part_key, part_value = key_parts(
            grad_scores, prob_rows, query_heads, grad_heads, key_rows.shape
        )
        return ((grad_key + part_key, grad_value + part_value), None)

    query_stack = (
        all_queries.reshape(query_blocks, query_step, col_width),
        all_grads.reshape(query_blocks, query_step, col_width),
        all_qcodes.reshape(query_blocks, query_step),
        all_sums.reshape(heads_local, query_blocks, query_step).transpose(1, 0, 2),
        all_deltas.reshape(heads_local, query_blocks, query_step).transpose(1, 0, 2),
    )
    zeros_keys = jnp.zeros((key_count, col_width), jnp.float32)
    (grad_key, grad_value), unused = lax.scan(own_keys, (zeros_keys, zeros_keys), query_stack)
    return (grad_query, grad_key, grad_value)


def mlp_forward(stream, gains_row, weight_in, weight_out):
    hidden_in = layer_norm(stream, gains_row).astype(jnp.bfloat16)
    hidden = jnp.dot(hidden_in, weight_in, preferred_element_type=jnp.float32)
    activated = jax.nn.gelu(hidden).astype(jnp.bfloat16)
    branch = head_sum(out_product(activated, weight_out))
    return (stream + branch, (hidden_in, hidden, activated))


def mlp_backward(stream, gains_row, weight_in, weight_out, saved, grad_stream):
    hidden_in, hidden, activated = saved
    grad_low = grad_stream.astype(jnp.bfloat16)
    grad_weight_out = jnp.einsum(
        "td,tf->df", grad_low, activated, preferred_element_type=jnp.float32
    )
    grad_activated = jnp.dot(grad_low, weight_out, preferred_element_type=jnp.float32)
    unused, gelu_back = jax.vjp(jax.nn.gelu, hidden)
    grad_hidden = gelu_back(grad_activated)[0].astype(jnp.bfloat16)
    grad_weight_in = jnp.einsum(
        "td,tf->df", hidden_in, grad_hidden, preferred_element_type=jnp.float32
    )
    grad_normed = head_grad_sum(out_product(grad_hidden, weight_in))
    grad_input, grad_gain = norm_back(stream, gains_row, grad_normed)
    return (grad_stream + grad_input, grad_gain, grad_weight_in, grad_weight_out)


def self_forward(stream, gains_row, weight_triple, weight_out, query_code, key_code):
    normed_low = layer_norm(stream, gains_row).astype(jnp.bfloat16)
    col_width = weight_triple.shape[2]
    triple = jnp.dot(
        normed_low,
        weight_triple.reshape(weight_triple.shape[0], 3 * col_width),
        preferred_element_type=jnp.float32,
    ).astype(jnp.bfloat16)
    queries = triple[:, :col_width]
    key_rows = triple[:, col_width : 2 * col_width]
    value_rows = triple[:, 2 * col_width :]
    mixed, log_sums = cycle_attend(queries, query_code, key_rows, value_rows, key_code)
    mixed_low = mixed.astype(jnp.bfloat16)
    branch = head_sum(out_product(mixed_low, weight_out))
    return (
        stream + branch,
        (normed_low, queries, key_rows, value_rows, mixed, mixed_low, log_sums),
    )


def self_backward(
    stream, gains_row, weight_triple, weight_out, saved, grad_stream, query_code, key_code
):
    normed_low, queries, key_rows, value_rows, mixed, mixed_low, log_sums = saved
    grad_low = grad_stream.astype(jnp.bfloat16)
    grad_weight_out = jnp.einsum(
        "td,ti->di", grad_low, mixed_low, preferred_element_type=jnp.float32
    )
    grad_mixed = jnp.dot(grad_low, weight_out, preferred_element_type=jnp.float32).astype(
        jnp.bfloat16
    )
    deltas = row_delta(grad_mixed, mixed)
    grad_query, grad_key, grad_value = attend_back(
        queries, grad_mixed, query_code, log_sums, deltas, key_rows, value_rows, key_code
    )
    grad_triple = jnp.concatenate([grad_query, grad_key, grad_value], axis=1).astype(jnp.bfloat16)
    grad_weight_triple = jnp.einsum(
        "td,tc->dc", normed_low, grad_triple, preferred_element_type=jnp.float32
    ).reshape(weight_triple.shape)
    grad_normed = head_grad_sum(
        out_product(grad_triple, weight_triple.reshape(weight_triple.shape[0], -1))
    )
    grad_input, grad_gain = norm_back(stream, gains_row, grad_normed)
    return (grad_stream + grad_input, grad_gain, grad_weight_triple, grad_weight_out)


def cross_forward(
    stream, input_rows, gains, weight_query, weight_pairs, weight_out, query_code, key_code
):
    latent_low = layer_norm(stream, gains[0]).astype(jnp.bfloat16)
    input_low = layer_norm(input_rows, gains[1]).astype(jnp.bfloat16)
    col_width = weight_query.shape[1]
    queries = jnp.dot(latent_low, weight_query, preferred_element_type=jnp.float32).astype(
        jnp.bfloat16
    )
    paired = jnp.dot(
        input_low,
        weight_pairs.reshape(weight_pairs.shape[0], 2 * col_width),
        preferred_element_type=jnp.float32,
    ).astype(jnp.bfloat16)
    key_rows = paired[:, :col_width]
    value_rows = paired[:, col_width:]
    mixed, log_sums = cycle_attend(queries, query_code, key_rows, value_rows, key_code)
    mixed_low = mixed.astype(jnp.bfloat16)
    branch = head_sum(out_product(mixed_low, weight_out))
    return (
        stream + branch,
        (latent_low, input_low, queries, key_rows, value_rows, mixed, mixed_low, log_sums),
    )


def cross_backward(
    stream,
    input_rows,
    gains,
    weight_query,
    weight_pairs,
    weight_out,
    saved,
    grad_stream,
    query_code,
    key_code,
):
    latent_low, input_low, queries, key_rows, value_rows, mixed, mixed_low, log_sums = saved
    grad_low = grad_stream.astype(jnp.bfloat16)
    grad_weight_out = jnp.einsum(
        "td,ti->di", grad_low, mixed_low, preferred_element_type=jnp.float32
    )
    grad_mixed = jnp.dot(grad_low, weight_out, preferred_element_type=jnp.float32).astype(
        jnp.bfloat16
    )
    deltas = row_delta(grad_mixed, mixed)
    grad_query, grad_key, grad_value = attend_back(
        queries, grad_mixed, query_code, log_sums, deltas, key_rows, value_rows, key_code
    )
    grad_query_low = grad_query.astype(jnp.bfloat16)
    grad_pairs = jnp.concatenate([grad_key, grad_value], axis=1).astype(jnp.bfloat16)
    grad_weight_query = jnp.einsum(
        "td,tc->dc", latent_low, grad_query_low, preferred_element_type=jnp.float32
    )
    grad_weight_pairs = jnp.einsum(
        "td,tc->dc", input_low, grad_pairs, preferred_element_type=jnp.float32
    ).reshape(weight_pairs.shape)
    latent_part = out_product(grad_query_low, weight_query)
    input_part = out_product(grad_pairs, weight_pairs.reshape(weight_pairs.shape[0], -1))
    latent_normed, input_normed = lax.psum((latent_part, input_part), "head")
    grad_latent, gain_zero = norm_back(stream, gains[0], latent_normed)
    grad_inputs, gain_one = norm_back(input_rows, gains[1], input_normed)
    return (
        grad_stream + grad_latent,
        grad_inputs,
        gain_zero,
        gain_one,
        grad_weight_query,
        grad_weight_pairs,
        grad_weight_out,
    )


def per_device(
    latents,
    inputs,
    latent_group,
    latent_valid,
    input_group,
    input_valid,
    gains,
    w_q_cross,
    w_kv_cross,
    w_o_cross,
    w_in_a,
    w_out_a,
    w_qkv_self,
    w_o_self,
    w_in_b,
    w_out_b,
    out_grad,
):
    start_stream = latents[0].astype(jnp.float32)
    input_rows = inputs[0].astype(jnp.float32)
    query_code = latent_group[0].astype(jnp.bfloat16)
    input_code = jnp.where(input_valid[0] == 1, input_group[0], -1).astype(jnp.bfloat16)
    self_code = jnp.where(latent_valid[0] == 1, latent_group[0], -1).astype(jnp.bfloat16)
    cross_stream, cross_saved = cross_forward(
        start_stream, input_rows, gains, w_q_cross, w_kv_cross, w_o_cross, query_code, input_code
    )
    middle_stream, first_saved = mlp_forward(cross_stream, gains[2], w_in_a, w_out_a)
    self_stream, self_saved = self_forward(
        middle_stream, gains[3], w_qkv_self, w_o_self, query_code, self_code
    )
    final_stream, second_saved = mlp_forward(self_stream, gains[4], w_in_b, w_out_b)
    grad_stream = out_grad[0].astype(jnp.float32)
    grad_stream, gain_four, grad_in_b, grad_out_b = mlp_backward(
        self_stream, gains[4], w_in_b, w_out_b, second_saved, grad_stream
    )
    grad_stream, gain_three, grad_qkv_self, grad_o_self = self_backward(
        middle_stream,
        gains[3],
        w_qkv_self,
        w_o_self,
        self_saved,
        grad_stream,
        query_code,
        self_code,
    )
    grad_stream, gain_two, grad_in_a, grad_out_a = mlp_backward(
        cross_stream, gains[2], w_in_a, w_out_a, first_saved, grad_stream
    )
    grad_stream, grad_inputs, gain_zero, gain_one, grad_q_cross, grad_kv_cross, grad_o_cross = (
        cross_backward(
            start_stream,
            input_rows,
            gains,
            w_q_cross,
            w_kv_cross,
            w_o_cross,
            cross_saved,
            grad_stream,
            query_code,
            input_code,
        )
    )
    gain_terms = jnp.stack([gain_zero, gain_one, gain_two, gain_three, gain_four], axis=1)
    (
        sum_gains,
        sum_q_cross,
        sum_kv_cross,
        sum_o_cross,
        sum_in_a,
        sum_out_a,
        sum_qkv_self,
        sum_o_self,
        sum_in_b,
        sum_out_b,
    ) = (
        lax.psum_scatter(gain_terms, ("group", "blk"), scatter_dimension=0, tiled=True),
        lax.psum_scatter(grad_q_cross, ("group", "blk"), scatter_dimension=0, tiled=True),
        lax.psum_scatter(grad_kv_cross, ("group", "blk"), scatter_dimension=0, tiled=True),
        lax.psum_scatter(grad_o_cross, ("group", "blk"), scatter_dimension=0, tiled=True),
        lax.psum_scatter(grad_in_a, ("group", "blk"), scatter_dimension=0, tiled=True),
        lax.psum_scatter(grad_out_a, ("group", "blk"), scatter_dimension=0, tiled=True),
        lax.psum_scatter(grad_qkv_self, ("group", "blk"), scatter_dimension=0, tiled=True),
        lax.psum_scatter(grad_o_self, ("group", "blk"), scatter_dimension=0, tiled=True),
        lax.psum_scatter(grad_in_b, ("group", "blk"), scatter_dimension=0, tiled=True),
        lax.psum_scatter(grad_out_b, ("group", "blk"), scatter_dimension=0, tiled=True),
    )
    (
        full_gains,
        full_q_cross,
        full_kv_cross,
        full_o_cross,
        full_in_a,
        full_out_a,
        full_qkv_self,
        full_o_self,
        full_in_b,
        full_out_b,
    ) = (
        lax.all_gather(sum_gains, ("group", "blk"), axis=0, tiled=True),
        lax.all_gather(sum_q_cross, ("group", "blk"), axis=0, tiled=True),
        lax.all_gather(sum_kv_cross, ("group", "blk"), axis=0, tiled=True),
        lax.all_gather(sum_o_cross, ("group", "blk"), axis=0, tiled=True),
        lax.all_gather(sum_in_a, ("group", "blk"), axis=0, tiled=True),
        lax.all_gather(sum_out_a, ("group", "blk"), axis=0, tiled=True),
        lax.all_gather(sum_qkv_self, ("group", "blk"), axis=0, tiled=True),
        lax.all_gather(sum_o_self, ("group", "blk"), axis=0, tiled=True),
        lax.all_gather(sum_in_b, ("group", "blk"), axis=0, tiled=True),
        lax.all_gather(sum_out_b, ("group", "blk"), axis=0, tiled=True),
    )
    return (
        final_stream.astype(jnp.bfloat16)[None],
        grad_stream[None],
        grad_inputs[None],
        full_gains.T,
        full_q_cross,
        full_kv_cross,
        full_o_cross,
        full_in_a,
        full_out_a,
        full_qkv_self,
        full_o_self,
        full_in_b,
        full_out_b,
    )


MESH = pl.DeviceIdType.MESH
bf16, f32 = jnp.bfloat16, jnp.float32
LANES = 128
TILE = 256
SCALE = HEAD_DIM**-0.5
GELU_A = 0.7978845608028654
GELU_B = 0.044715


def dot_nn(a, b):
    return jnp.dot(a, b, preferred_element_type=f32)


def dot_nt(a, b):
    return lax.dot_general(a, b, (((1,), (1,)), ((), ())), preferred_element_type=f32)


def dot_tn(a, b):
    return lax.dot_general(a, b, (((0,), (0,)), ((), ())), preferred_element_type=f32)


def norm_rows(x):
    c = x - jnp.mean(x, axis=-1, keepdims=True)
    rstd = lax.rsqrt(jnp.mean(c * c, axis=-1, keepdims=True) + 1e-05)
    return c * rstd, rstd


def gelu_both(u):
    u2 = u * u
    t = jnp.tanh(GELU_A * u * (1.0 + GELU_B * u2))
    half = 0.5 * (1.0 + t)
    slope = half + 0.5 * u * (1.0 - t * t) * (GELU_A * (1.0 + 3.0 * GELU_B * u2))
    return u * half, slope


def loop(start, stop, body):
    def step(k, carry):
        body(k)
        return carry

    lax.fori_loop(start, stop, step, 0)


SCHEDULE = dict(
    fifth=["At", "Bt", "", "A1", "B1", "", "", ""],
    sixth_put=["St A2 B2"],
    sixth=["A3", "S1", "B3", "", "S2 A4", "", "S3 B4", ""],
    seventh_pre=["Ct Dt"],
    seventh=["A5", "S4", "B5", "", "", "C1 A6 B6", "S5", "D1"],
    last_put=["Xt C2"],
    late_end=["C3 D2 S6"],
    input=["X1", "C4", "D3", "X2 gz1"],
    last=["", "gz2", "X3 D4", "C5 gz3 dg0", "X4 dg1", "", "D5 dg2", "X5 dg3"],
    end=["C6 X6 D6"],
)


def block_kernel(names, T, I, D, C, F, CH, *refs):
    r = types.SimpleNamespace(**dict(zip(names, refs, strict=True)))
    NCH = T // CH
    ICH = I // CH
    HL = C // HEAD_DIM
    g = lax.axis_index("group")
    b = lax.axis_index("blk")
    h = lax.axis_index("head")
    is_mid = (h == 1) | (h == 2)
    is_end = jnp.logical_not(is_mid)
    at_pair = (g, b, h ^ 1)
    at_mid = (g, b, 3 - h)
    at_y = (g, 1 - b, h)
    at_x = (g ^ 2, b, h)
    at_core = (g ^ 1, b, h)
    core = g % 2
    xi = g // 2
    gains = r.gains

    def rows(c, n=CH):
        return pl.ds(pl.multiple_of(c * n, n), n)

    def remote(src, dst, send_sem, recv_sem, where):
        return pltpu.make_async_remote_copy(
            src_ref=src, dst_ref=dst, send_sem=send_sem, recv_sem=recv_sem, device_id=where, device_id_type=MESH
        )

    bar = pltpu.get_barrier_semaphore()
    for where in (at_pair, at_y, at_x, at_core):
        pl.semaphore_signal(bar, inc=1, device_id=where, device_id_type=MESH)

    @pl.when(is_mid)
    def _():
        pl.semaphore_signal(bar, inc=1, device_id=at_mid, device_id_type=MESH)

    loads = {}

    def load(src, dst, name):
        cp = pltpu.make_async_copy(src, dst, r.load_sem.at[len(loads)])
        cp.start()
        loads[name] = cp

    load(r.inputs, r.inp, "inp")
    load(r.w_kv_c, r.wkvc, "wkvc")
    load(r.latents, r.lat, "lat")
    load(r.w_q_c, r.wqc, "wqc")
    load(r.w_o_c, r.woc, "woc")
    load(r.w_in_a, r.wina, "wina")
    load(r.w_out_a, r.wouta, "wouta")
    for j in range(3):
        load(r.w_qkv_s.at[j], r.wqkvs.at[:, pl.ds(j * C, C)], "wqkvs%d" % j)
    load(r.w_o_s, r.wos, "wos")
    load(r.w_in_b, r.winb, "winb")
    load(r.w_out_b, r.woutb, "woutb")
    load(r.out_grad, r.r4, "r4")

    lg = r.latent_group[...]
    ic = jnp.where(r.input_valid[...] == 1, r.input_group[...], -1).astype(f32)
    sc = jnp.where(r.latent_valid[...] == 1, lg, -1).astype(f32)
    lgf = lg.astype(f32)
    r.codes[:, 0:I] = jnp.broadcast_to(ic, (8, I))
    r.codes[:, I : I + T] = jnp.broadcast_to(sc, (8, T))
    r.codes[:, I + T : I + 2 * T] = jnp.broadcast_to(lgf, (8, T))

    def make_columns(line, dst):
        for j in range(T // LANES):
            dst[pl.ds(j * LANES, LANES), :] = jnp.transpose(
                jnp.broadcast_to(line[:, j * LANES : (j + 1) * LANES], (LANES, LANES))
            )

    make_columns(lgf, r.qcol)
    r.dg[...] = jnp.zeros_like(r.dg)
    r.gz[...] = jnp.zeros_like(r.gz)

    @pl.when(is_mid)
    def _():
        pl.semaphore_wait(bar, 5)

    @pl.when(is_end)
    def _():
        pl.semaphore_wait(bar, 4)

    def to_y(src, dst, k):
        return remote(src, dst, r.y_snd.at[k], r.y_rcv.at[k], at_y)

    codes_cp = to_y(r.codes, r.codes_o, 0)
    codes_cp.start()

    SUB = 4
    SR = CH // SUB

    def cp_in(p, c):
        rw = rows(c, SR)
        return remote(r.part.at[p, rw], r.rin.at[p, rw], r.ar_snd.at[p, c], r.ar_in.at[p, c], at_pair)

    def cp_mid(p, c):
        rw = rows(c, SR)
        return remote(r.part.at[p, rw], r.rmid.at[p, rw], r.ar_snd.at[p, c], r.ar_mid.at[p, c], at_mid)

    def cp_tot(p, c):
        rw = rows(c, SR)
        return remote(r.rin.at[p, rw], r.rin.at[p, rw], r.ar_tot.at[p, c], r.ar_in.at[p, c], at_pair)

    def subs(c):
        return [c * SUB + k for k in range(SUB)]

    def ar_send(p, c):
        @pl.when(is_end)
        def _():
            for k in subs(c):
                cp_in(p, k).start()

    def ar_put(p, c, value):
        r.part[p, rows(c)] = value.astype(bf16)
        ar_send(p, c)

    def ar_put_wide(p, c, value):
        r.part[p, rows(c, 2 * CH)] = value.astype(bf16)
        ar_send(p, 2 * c)
        ar_send(p, 2 * c + 1)

    def ar_b(p, c):
        @pl.when(is_mid)
        def _():
            for k in subs(c):
                rw = rows(k, SR)
                cp_in(p, k).wait_recv()
                r.part[p, rw] = r.part[p, rw] + r.rin[p, rw]
                cp_mid(p, k).start()

    def ar_c(p, c, prev=None):
        ar_c_mid(p, c, prev)
        ar_c_end(p, c)

    def ar_c_mid(p, c, prev=None):
        @pl.when(is_mid)
        def _():
            for k in subs(c):
                rw = rows(k, SR)
                cp_mid(p, k).wait_recv()
                cp_mid(p, k).wait_send()
                r.rin[p, rw] = r.part[p, rw] + r.rmid[p, rw]
                if prev is not None:
                    cp_tot(prev, k).wait_send()
                cp_tot(p, k).start()

    def ar_c_end(p, c):
        @pl.when(is_end)
        def _():
            for k in subs(c):
                cp_in(p, k).wait_send()
                cp_tot(p, k).wait_recv()

    def drain(p, c):
        @pl.when(is_mid)
        def _():
            for k in subs(c):
                cp_tot(p, k).wait_send()

    def total_of(p, c):
        return r.rin[p, rows(c)].astype(f32)

    half, quarter, eighth, piece = D // 2, D // 4, D // 8, D // 16
    own = core * half
    p_own = own + xi * eighth
    p_oth = own + (1 - xi) * eighth
    q_base = own + quarter
    q_own = q_base + b * eighth
    q_oth = q_base + (1 - b) * eighth
    p_fin, p_fin_oth = p_own + b * piece, p_own + (1 - b) * piece
    q_fin, q_fin_oth = q_own + xi * piece, q_own + (1 - xi) * piece

    def span(start, n):
        return pl.ds(pl.multiple_of(start, piece), n)

    class Job:
        def __init__(self, index, w, rc, out, parts):
            self.j, self.w, self.rc, self.out, self.parts = index, w, rc, out, parts
            self.s = index % 3

        def tiles(self):
            loop(0, D // TILE, self.tile)
            self.cp_core().start()

        def tile(self, t):
            col = 0
            rw = rows(t, TILE)
            for lhs, rhs in self.parts:
                n = rhs.shape[1]
                self.w[rw, col : col + n] = dot_tn(lhs[:, rw], rhs[...]).astype(bf16)
                col += n

        def cp(self, k, src, dst, where):
            return remote(src, dst, r.j_snd.at[self.j, k], r.j_rcv.at[self.j, k], where)

        def cp_core(self):
            return self.cp(0, self.w.at[span((1 - core) * half, half)], self.rc, at_core)

        def cp_p1(self):
            return self.cp(1, self.w.at[span(p_oth, eighth)], r.r1p.at[self.s], at_x)

        def cp_q1(self):
            return self.cp(2, self.w.at[span(q_oth, eighth)], r.r1q.at[self.s], at_y)

        def cp_p2(self):
            return self.cp(3, self.w.at[span(p_fin_oth, piece)], r.r2p.at[self.s], at_y)

        def cp_q2(self):
            return self.cp(4, self.w.at[span(q_fin_oth, piece)], r.r2q.at[self.s], at_x)

        def cp_p3(self):
            return self.cp(5, self.w.at[span(p_fin, piece)], self.out.at[span(p_fin, piece)], at_y)

        def cp_q3(self):
            return self.cp(6, self.w.at[span(q_fin, piece)], self.out.at[span(q_fin, piece)], at_x)

        def cp_p4(self):
            return self.cp(7, self.out.at[span(p_own, eighth)], self.out.at[span(p_own, eighth)], at_x)

        def cp_q4(self):
            return self.cp(8, self.out.at[span(q_own, eighth)], self.out.at[span(q_own, eighth)], at_y)

        def cp_all(self):
            return self.cp(9, self.out.at[span(own, half)], self.out.at[span(own, half)], at_core)

        def cp_keep(self):
            return (
                pltpu.make_async_copy(
                    self.w.at[span(p_fin, piece)], self.out.at[span(p_fin, piece)], r.j_own.at[self.j, 0]
                ),
                pltpu.make_async_copy(
                    self.w.at[span(q_fin, piece)], self.out.at[span(q_fin, piece)], r.j_own.at[self.j, 1]
                ),
            )

        def add(self, start, n, other):
            rw = span(start, n)
            self.w[rw] = self.w[rw] + other[...]

        def s1(self):
            self.cp_core().wait_recv()
            self.add(p_oth, eighth, self.rc.at[span(p_oth - own, eighth)])
            self.cp_p1().start()
            self.add(q_oth, eighth, self.rc.at[span(q_oth - own, eighth)])
            self.cp_q1().start()
            self.add(p_own, eighth, self.rc.at[span(p_own - own, eighth)])
            self.add(q_own, eighth, self.rc.at[span(q_own - own, eighth)])

        def s2(self):
            self.cp_p1().wait_recv()
            self.add(p_own, eighth, r.r1p.at[self.s])
            self.cp_q1().wait_recv()
            self.add(q_own, eighth, r.r1q.at[self.s])
            self.cp_p2().start()
            self.cp_q2().start()

        def s3(self):
            self.cp_p2().wait_recv()
            self.add(p_fin, piece, r.r2p.at[self.s])
            self.cp_p3().start()
            self.cp_q2().wait_recv()
            self.add(q_fin, piece, r.r2q.at[self.s])
            self.cp_q3().start()
            for cp in self.cp_keep():
                cp.start()

        def s4(self):
            for cp in self.cp_keep():
                cp.wait()
            self.cp_p3().wait_recv()
            self.cp_p4().start()
            self.cp_q3().wait_recv()
            self.cp_q4().start()
            for cp in (self.cp_core(), self.cp_p1(), self.cp_q1(), self.cp_p2(), self.cp_q2(), self.cp_p3(), self.cp_q3()):
                cp.wait_send()

        def s5(self):
            self.cp_p4().wait_recv()
            self.cp_q4().wait_recv()
            self.cp_all().start()
            self.cp_p4().wait_send()
            self.cp_q4().wait_send()

        def s6(self):
            self.cp_all().wait()

    job_out_b = Job(0, r.wj, r.rc.at[0], r.g_out_b, [(r.r4, r.z2)])
    job_in_b = Job(1, r.winb, r.rc.at[1], r.g_in_b, [(r.h2, r.du2)])
    job_self = Job(2, r.woutb, r.rc.at[2], r.g_self, [(r.cs, r.dqkv), (r.ra, r.o_s)])
    job_out_a = Job(3, r.p_s, r.z2, r.g_out_a, [(r.lat, r.z1)])
    job_in_a = Job(4, r.wj, r.du2, r.g_in_a, [(r.h1, r.du1)])
    job_cross = Job(5, r.winb, r.h2, r.g_cross, [(r.bn, r.dkv), (r.an, r.dq), (r.ra, r.o_c)])

    def norm_out(x, gain_row, out, rstd_out, rw):
        xhat, rstd = norm_rows(x)
        rstd_out[rw] = jnp.broadcast_to(rstd, (rstd.shape[0], LANES))
        low = (xhat * gains[gain_row : gain_row + 1, :]).astype(bf16)
        out[rw] = low
        return low

    def norm_grad(cot, low_ref, dg_row, gain_row, rstd_ref, rw):
        gain = gains[gain_row : gain_row + 1, :]
        xhat = low_ref[rw].astype(f32) * (1.0 / gain)
        scaled = cot * gain
        mean_one = jnp.mean(scaled, axis=-1, keepdims=True)
        mean_two = jnp.mean(scaled * xhat, axis=-1, keepdims=True)
        if dg_row is not None:
            r.dg[dg_row : dg_row + 1, :] += jnp.sum(cot * xhat, axis=0, keepdims=True)
        return rstd_ref[rw, 0:1] * (scaled - mean_one - xhat * mean_two)

    loads["inp"].wait()
    loads["wkvc"].wait()

    def kv_chunk(k):
        rw = rows(k, LANES)
        low = norm_out(r.inp[rw].astype(f32), 1, r.bn, r.rs1, rw)
        r.kv[rw] = dot_nn(low, r.wkvc[...]).astype(bf16)

    kv_cps = [to_y(r.kv.at[pl.ds(k * I // 2, I // 2)], r.kv.at[pl.ds(I + k * I // 2, I // 2)], (1, 5)[k]) for k in range(2)]
    for k in range(2):
        loop(k * (I // LANES // 2), (k + 1) * (I // LANES // 2), kv_chunk)
        kv_cps[k].start()

    loads["lat"].wait()
    loads["wqc"].wait()

    def q_chunk(k):
        rw = rows(k, LANES)
        low = norm_out(r.lat[rw].astype(f32), 0, r.an, r.rs0, rw)
        r.q[rw] = dot_nn(low, r.wqc[...]).astype(bf16)

    loop(0, T // LANES, q_chunk)
    codes_cp.wait()
    make_columns(r.codes_o[0:1, I + T : I + 2 * T], r.qcol_o)
    for cp in kv_cps:
        cp.wait()
    loads["woc"].wait()

    def attend_chunk(k, q_ref, kv_ref, p_ref, o_ref, start, n):
        rw = rows(k)
        kc = jnp.concatenate([r.codes[0:1, start : start + n], r.codes_o[0:1, start : start + n]], axis=1)
        allowed = r.qcol[rw, 0:1] == kc
        for hd in range(HL):
            cols = slice(hd * HEAD_DIM, (hd + 1) * HEAD_DIM)
            vcols = slice(C + hd * HEAD_DIM, C + (hd + 1) * HEAD_DIM)
            s = jnp.where(allowed, dot_nt(q_ref[rw, cols], kv_ref[:, cols]) * SCALE, masked_fill)
            e = jnp.exp(s - jnp.max(s, axis=-1, keepdims=True))
            p = (e * (1.0 / jnp.sum(e, axis=-1, keepdims=True))).astype(bf16)
            p_ref[rows(k + hd * NCH), :] = p
            o_ref[rw, cols] = dot_nn(p, kv_ref[:, vcols]).astype(bf16)

    def cross_chunk(k):
        attend_chunk(k, r.q, r.kv, r.p_c, r.o_c, 0, I)
        ar_put(0, k, dot_nt(r.o_c[rows(k)], r.woc[...]))

        @pl.when(k >= 4)
        def _():
            ar_b(0, k - 4)

    loop(0, NCH, cross_chunk)

    back_cross = [
        to_y(r.p_c.at[:, pl.ds(I, I)], r.pr_c, 2), to_y(r.q, r.qr_c, 3), to_y(r.o_c, r.or_c, 4),
    ]
    for cp in back_cross:
        cp.start()
    loads["wina"].wait()
    loads["wouta"].wait()

    def first_chunk(m):
        @pl.when((m >= 2) & (m < NCH - 2))
        def _():
            ar_b(0, m + 2)

        ar_c(0, m)
        rw = rows(m)
        x = r.lat[rw].astype(f32) + total_of(0, m)
        r.xs[rw] = x
        low = norm_out(x, 2, r.h1, r.rs2, rw)
        z, slope = gelu_both(dot_nn(low, r.wina[...]))
        z = z.astype(bf16)
        r.z1[rw] = z
        r.s1[rw] = slope.astype(bf16)
        ar_put(1, m, dot_nt(z, r.wouta[...]))

        @pl.when(m >= NCH - 2)
        def _():
            ar_b(1, m + 2 - NCH)

    loop(0, NCH, first_chunk)
    for j in range(3):
        loads["wqkvs%d" % j].wait()
    loads["wos"].wait()

    def kv2_cp(c):
        return remote(r.kv2.at[rows(c)], r.kv2.at[rows(c + NCH)], r.kv_snd.at[c], r.kv_rcv.at[c], at_y)

    def second_chunk(m):
        @pl.when(m < NCH - 2)
        def _():
            ar_b(1, m + 2)

        ar_c(1, m, 0)
        rw = rows(m)
        x = r.xs[rw] + total_of(1, m)
        r.xs[rw] = x
        low = norm_out(x, 3, r.cs, r.rs3, rw)
        qkv = dot_nn(low, r.wqkvs[...]).astype(bf16)
        r.q2[rw] = qkv[:, :C]
        r.kv2[rw] = qkv[:, C:]
        kv2_cp(m).start()

    loop(0, NCH, second_chunk)
    loop(0, NCH, lambda c: kv2_cp(c).wait())

    def p_cp(c):
        return remote(r.p_s.at[rows(c), pl.ds(T, T)], r.pr_s.at[rows(c)], r.p_snd.at[c], r.p_rcv.at[c], at_y)

    q_back = to_y(r.q2, r.qr_s, 6)
    q_back.start()

    def self_chunk(k):
        attend_chunk(k, r.q2, r.kv2, r.p_s, r.o_s, I, T)
        for hd in range(HL):
            p_cp(k + hd * NCH).start()

        ar_put(0, k, dot_nt(r.o_s[rows(k)], r.wos[...]))

        @pl.when(k >= 4)
        def _():
            ar_b(0, k - 4)

    loop(0, NCH, self_chunk)
    o_back = to_y(r.o_s, r.or_s, 7)
    o_back.start()
    loads["winb"].wait()
    loads["woutb"].wait()
    loads["r4"].wait()

    def third_chunk(m):
        @pl.when((m >= 2) & (m < NCH - 2))
        def _():
            ar_b(0, m + 2)

        ar_c(0, m, 1)
        rw = rows(m)
        x = r.xs[rw] + total_of(0, m)
        r.xs[rw] = x
        low = norm_out(x, 4, r.h2, r.rs4, rw)
        z, slope = gelu_both(dot_nn(low, r.winb[...]))
        z = z.astype(bf16)
        r.z2[rw] = z
        du = (dot_nn(r.r4[rw], r.woutb[...]) * slope).astype(bf16)
        r.du2[rw] = du
        ar_put(1, m, dot_nt(du, r.winb[...]))

        @pl.when(m >= NCH - 2)
        def _():
            ar_b(1, m + 2 - NCH)

    loop(0, NCH, third_chunk)

    def d_o_cp(k, c):
        return remote(r.do.at[k, rows(c)], r.do_o.at[k, rows(c)], r.do_snd.at[k, c], r.do_rcv.at[k, c], at_y)

    class Back:
        def __init__(self, k, q, qr, kv, p, pr, o, o_r, n, start, dq, dkv, dkv_col):
            self.k, self.q, self.qr, self.kv, self.p, self.pr, self.o, self.o_r = k, q, qr, kv, p, pr, o, o_r
            self.n, self.first, self.dq, self.dkv, self.dkv_col = n, start, dq, dkv, dkv_col
            self.do, self.do_o = r.do.at[k], r.do_o.at[k]

        def own(self, m):
            rw = rows(m)
            n, a = self.n, self.first
            kc = jnp.concatenate([r.codes[0:1, a : a + n], r.codes_o[0:1, a : a + n]], axis=1)
            allowed = r.qcol[rw, 0:1] == kc
            for hd in range(HL):
                cols = slice(hd * HEAD_DIM, (hd + 1) * HEAD_DIM)
                vcols = slice(C + hd * HEAD_DIM, C + (hd + 1) * HEAD_DIM)
                grad = self.do[rw, cols]
                delta = jnp.sum(grad.astype(f32) * self.o[rw, cols].astype(f32), axis=-1, keepdims=True)
                diff = dot_nt(grad, self.kv[:, vcols]) - delta
                prob = self.p[rows(m + hd * NCH), :].astype(f32)
                ds = jnp.where(allowed, prob * diff, 0.0).astype(bf16)
                r.ds[rows(m + 2 * hd * NCH), 0:n] = ds[:, 0:n]
                self.dq[rw, cols] = (dot_nn(ds, self.kv[:, cols]) * SCALE).astype(bf16)

        def other(self, m):
            d_o_cp(self.k, m).wait()
            rw = rows(m)
            n, a = self.n, self.first
            allowed = r.qcol_o[rw, 0:1] == r.codes[0:1, a : a + n]
            for hd in range(HL):
                cols = slice(hd * HEAD_DIM, (hd + 1) * HEAD_DIM)
                vcols = slice(C + hd * HEAD_DIM, C + (hd + 1) * HEAD_DIM)
                grad = self.do_o[rw, cols]
                delta = jnp.sum(grad.astype(f32) * self.o_r[rw, cols].astype(f32), axis=-1, keepdims=True)
                diff = dot_nt(grad, self.kv[0:n, vcols]) - delta
                prob = self.pr[rows(m + hd * NCH), :].astype(f32)
                ds = jnp.where(allowed, prob * diff, 0.0).astype(bf16)
                r.ds[rows(m + (2 * hd + 1) * NCH), 0:n] = ds

        def some_other(self, m, waits):
            if waits is not None:

                @pl.when(m == NCH // 2)
                def _():
                    for wait in waits:
                        wait()

            @pl.when((m >= NCH // 2) & (m < NCH - 2))
            def _():
                self.other(2 * m - NCH)
                self.other(2 * m + 1 - NCH)

            @pl.when(m == NCH - 2)
            def _():
                self.other(NCH - 4)

            @pl.when(m == NCH - 1)
            def _():
                self.other(NCH - 3)

        def keys_own(self):
            n = self.n
            out = []
            for hd in range(HL):
                cols = slice(hd * HEAD_DIM, (hd + 1) * HEAD_DIM)
                at = 2 * hd * T
                dk = dot_tn(r.ds[at : at + T, 0:n], self.q[:, cols])
                dv = dot_tn(self.p[hd * T : (hd + 1) * T, 0:n], self.do[:, cols])
                out.append((dk, dv))
            return out

        def keys(self, own):
            n = self.n
            for hd, (dk, dv) in enumerate(own):
                cols = slice(hd * HEAD_DIM, (hd + 1) * HEAD_DIM)
                at = (2 * hd + 1) * T
                dk = dk + dot_tn(r.ds[at : at + T, 0:n], self.qr[:, cols])
                dv = dv + dot_tn(self.pr[hd * T : (hd + 1) * T, :], self.do_o[:, cols])
                col = self.dkv_col + hd * HEAD_DIM
                self.dkv[:, col : col + HEAD_DIM] = (dk * SCALE).astype(bf16)
                self.dkv[:, col + C : col + C + HEAD_DIM] = dv.astype(bf16)

    back_of_self = Back(0, r.q2, r.qr_s, r.kv2, r.p_s, r.pr_s, r.o_s, r.or_s, T, I, r.dqkv, r.dqkv, C)
    back_of_cross = Back(1, r.q, r.qr_c, r.kv, r.p_c, r.pr_c, r.o_c, r.or_c, I, 0, r.dq, r.dkv, 0)

    jobs = dict(A=job_out_b, B=job_in_b, S=job_self, C=job_out_a, D=job_in_a, X=job_cross)
    extra = {}

    def on(place, m=None):
        for step, words in enumerate(SCHEDULE[place]):
            names = words.split()
            if not names:
                continue

            def run(names=names):
                for name in names:
                    if name in extra:
                        extra[name]()
                    else:
                        getattr(jobs[name[0]], "tiles" if name[1] == "t" else "s" + name[1])()

            if m is None:
                run()
            else:
                pl.when(m == step)(run)

    def fifth_chunk(m):
        @pl.when(m < NCH - 2)
        def _():
            ar_b(1, m + 2)

        ar_c(1, m, 0)
        rw = rows(m)
        dx = r.r4[rw].astype(f32) + norm_grad(total_of(1, m), r.h2, 4, 4, r.rs4, rw)
        r.dxs[rw] = dx
        low = dx.astype(bf16)
        r.ra[rw] = low
        r.do[0, rw] = dot_nn(low, r.wos[...]).astype(bf16)
        d_o_cp(0, m).start()

        @pl.when(m < NCH // 2)
        def _():
            wide = rows(m, 2 * CH)
            r.part[2, wide] = dot_nt(r.z2[wide], r.woutb[...]).astype(bf16)

        @pl.when(m < NCH // 4)
        def _():
            ar_send(2, 2 * m)
            ar_send(2, 2 * m + 1)

        back_of_self.own(m)
        back_of_self.some_other(m, [q_back.wait, o_back.wait, lambda: loop(0, HL * NCH, lambda c: p_cp(c).wait())])

        on("fifth", m)

        @pl.when(m >= NCH // 2)
        def _():
            ar_b(2, m - NCH // 2)

    loop(0, NCH, fifth_chunk)

    def late_out(c):
        ar_c_end(2, c)
        rw = rows(c)
        r.part[2, rw] = (r.xs[rw] + total_of(2, c)).astype(bf16)

    self_keys = back_of_self.keys_own()
    back_of_self.other(NCH - 2)
    back_of_self.other(NCH - 1)
    back_of_self.keys(self_keys)
    def sixth_put(k):
        ar_put_wide(0, k, dot_nt(r.dqkv[rows(k, 2 * CH)], r.wqkvs[...]))

    loop(0, NCH // 2, sixth_put)
    loop(0, NCH // 2, lambda c: ar_c_mid(2, c))
    on("sixth_put")
    loop(0, 2, lambda c: ar_b(0, c))

    def sixth_chunk(m):
        @pl.when(m < NCH - 2)
        def _():
            ar_b(0, m + 2)

        ar_c(0, m, 1)
        rw = rows(m)
        dx = r.dxs[rw] + norm_grad(total_of(0, m), r.cs, 3, 3, r.rs3, rw)
        r.dxs[rw] = dx
        low = dx.astype(bf16)
        r.lat[rw] = low
        du = (dot_nn(low, r.wouta[...]) * r.s1[rw].astype(f32)).astype(bf16)
        r.du1[rw] = du
        ar_put(1, m, dot_nt(du, r.wina[...]))

        @pl.when(m >= NCH - 2)
        def _():
            ar_b(1, m + 2 - NCH)

        @pl.when(m < NCH // 2)
        def _():
            late_out(m)

        on("sixth", m)

    loop(0, NCH, sixth_chunk)
    late_cps = [
        pltpu.make_async_copy(r.part.at[2, rw], r.latents_out.at[rw], r.out_sem.at[2 + 2 * k])
        for k, rw in enumerate([pl.ds(0, T // 2), pl.ds(T // 2, T // 2)])
    ]
    late_cps[0].start()
    def seventh_chunk(m):
        @pl.when(m < NCH - 2)
        def _():
            ar_b(1, m + 2)

        @pl.when(m < NCH // 2)
        def _():
            drain(2, m)

        ar_c(1, m, 0)
        rw = rows(m)
        dx = r.dxs[rw] + norm_grad(total_of(1, m), r.h1, 2, 2, r.rs2, rw)
        r.dxs[rw] = dx
        low = dx.astype(bf16)
        r.ra[rw] = low
        r.do[1, rw] = dot_nn(low, r.woc[...]).astype(bf16)
        d_o_cp(1, m).start()
        back_of_cross.own(m)
        back_of_cross.some_other(m, [cp.wait for cp in back_cross])

        on("seventh", m)

        @pl.when(m >= NCH // 2)
        def _():
            ar_b(2, m)

    on("seventh_pre")
    loop(NCH // 2, NCH, lambda c: ar_send(2, c))
    loop(0, NCH, seventh_chunk)

    cross_keys = back_of_cross.keys_own()
    back_of_cross.other(NCH - 2)
    back_of_cross.other(NCH - 1)
    back_of_cross.keys(cross_keys)

    late_cps[0].wait()

    def put_last(p, k, value, low_ref, gain_row):
        ar_put_wide(p, k, value)
        xhat = low_ref[rows(k, 2 * CH)].astype(f32) * (1.0 / gains[gain_row : gain_row + 1, :])
        r.gz[gain_row : gain_row + 1, :] += jnp.sum(value * xhat, axis=0, keepdims=True)

    loop(0, ICH // 2, lambda k: put_last(2, k, dot_nt(r.dkv[rows(k, 2 * CH)], r.wkvc[...]), r.bn, 1))
    loop(0, NCH // 2, lambda k: put_last(0, k, dot_nt(r.dq[rows(k, 2 * CH)], r.wqc[...]), r.an, 0))

    def gz_cp(k, where):
        return remote(r.gz, r.gzr.at[k], r.gz_snd.at[k], r.gz_rcv.at[k], where)

    @pl.when(is_end)
    def _():
        gz_cp(0, at_pair).start()

    def gz_one():
        @pl.when(is_mid)
        def _():
            gz_cp(0, at_pair).wait_recv()
            r.gz[...] += r.gzr[0]
            gz_cp(1, at_mid).start()

    def gz_two():
        @pl.when(is_mid)
        def _():
            gz_cp(1, at_mid).wait()
            r.gz[...] += r.gzr[1]
            gz_cp(2, at_pair).start()

    def gz_three():
        @pl.when(is_end)
        def _():
            gz_cp(0, at_pair).wait_send()
            gz_cp(2, at_pair).wait_recv()
            r.dg[0:2, :] = r.gzr[2, 0:2, :]

        @pl.when(is_mid)
        def _():
            gz_cp(2, at_pair).wait_send()
            r.dg[0:2, :] = r.gz[0:2, :]

    def dg_cp(k):
        return remote(r.dg, r.dgr.at[k], r.dg_snd.at[k], r.dg_rcv.at[k], (at_core, at_x, at_y)[k])

    def dg_next(k):
        def step():
            dg_cp(k).wait()
            r.dg[...] += r.dgr[k]
            if k < 2:
                dg_cp(k + 1).start()

        return step

    dg_zero, dg_one, dg_two = (dg_next(k) for k in range(3))

    on("last_put")
    loop(NCH // 2, NCH, lambda c: ar_c_mid(2, c))
    on("late_end")
    loop(0, 2, lambda c: ar_b(2, c))

    extra.update(gz1=gz_one, gz2=gz_two, gz3=gz_three, dg0=dg_cp(0).start, dg1=dg_zero, dg2=dg_one, dg3=dg_two)

    def input_chunk(m):
        @pl.when(m < ICH - 2)
        def _():
            ar_b(2, m + 2)

        @pl.when(m >= ICH - 2)
        def _():
            ar_b(0, m + 2 - ICH)

        ar_c(2, m)
        rw = rows(m)
        r.inp[rw] = norm_grad(total_of(2, m), r.bn, None, 1, r.rs1, rw).astype(bf16)

        late_out(m + NCH // 2)
        on("input", m)

    loop(0, ICH, input_chunk)
    out_cps = [
        pltpu.make_async_copy(r.inp, r.input_grad, r.out_sem.at[0]),
        pltpu.make_async_copy(r.lat.at[pl.ds(0, T // 2)], r.latent_grad.at[pl.ds(0, T // 2)], r.out_sem.at[1]),
        pltpu.make_async_copy(r.lat.at[pl.ds(T // 2, T // 2)], r.latent_grad.at[pl.ds(T // 2, T // 2)], r.out_sem.at[3]),
    ]
    out_cps[0].start()
    late_cps[1].start()

    def last_chunk(m):
        @pl.when(m < NCH - 2)
        def _():
            ar_b(0, m + 2)

        ar_c(0, m, 1)
        rw = rows(m)
        r.lat[rw] = (r.dxs[rw] + norm_grad(total_of(0, m), r.an, None, 0, r.rs0, rw)).astype(bf16)

        @pl.when(m == 4)
        def _():
            out_cps[1].start()

        on("last", m)

    loop(0, NCH, last_chunk)
    out_cps[2].start()
    r.gains_grad[...] = r.dg[...]
    on("end")

    loop(0, NCH, lambda c: drain(2, c))
    loop(0, NCH, lambda c: drain(0, c))

    for cp in [*out_cps, late_cps[1]]:
        cp.wait()


def block_call(latents, inputs, latent_group, latent_valid, input_group, input_valid, gains, weights, out_grad):
    T, D = latents.shape
    I = inputs.shape[0]
    C = weights["w_q_c"].shape[1]
    F = weights["w_in_a"].shape[1]
    CH = 64
    NCH = T // CH
    HL = C // HEAD_DIM
    in_vmem = dict(
        latent_group=latent_group, latent_valid=latent_valid, input_group=input_group,
        input_valid=input_valid, gains=gains,
    )
    in_any = dict(latents=latents, inputs=inputs, **weights, out_grad=out_grad)
    S = jax.ShapeDtypeStruct
    out_any = dict(
        latents_out=S((T, D), bf16), latent_grad=S((T, D), bf16), input_grad=S((I, D), bf16),
        g_out_b=S((D, F), bf16), g_in_b=S((D, F), bf16), g_self=S((D, 4 * C), bf16),
        g_out_a=S((D, F), bf16), g_in_a=S((D, F), bf16), g_cross=S((D, 4 * C), bf16),
    )
    out_vmem = dict(gains_grad=S((8, D), f32))
    V, DMA = pltpu.VMEM, pltpu.SemaphoreType.DMA
    half, eighth, piece = D // 2, D // 8, D // 16
    scratch = dict(
        inp=V((I, D), bf16), lat=V((T, D), bf16), r4=V((T, D), bf16),
        wkvc=V((D, 2 * C), bf16), wqc=V((D, C), bf16), woc=V((D, C), bf16),
        wina=V((D, F), bf16), wouta=V((D, F), bf16), wqkvs=V((D, 3 * C), bf16),
        wos=V((D, C), bf16), winb=V((D, F), bf16), woutb=V((D, F), bf16), wj=V((D, F), bf16),
        codes=V((8, I + 2 * T), f32), codes_o=V((8, I + 2 * T), f32),
        qcol=V((T, LANES), f32), qcol_o=V((T, LANES), f32),
        part=V((3, T, D), bf16), rin=V((3, T, D), bf16), rmid=V((3, T, D), bf16),
        xs=V((T, D), f32), dxs=V((T, D), f32),
        an=V((T, D), bf16), bn=V((I, D), bf16), h1=V((T, D), bf16), cs=V((T, D), bf16), h2=V((T, D), bf16),
        rs0=V((T, LANES), f32), rs1=V((I, LANES), f32), rs2=V((T, LANES), f32), rs3=V((T, LANES), f32),
        rs4=V((T, LANES), f32),
        z1=V((T, F), bf16), s1=V((T, F), bf16), du1=V((T, F), bf16), z2=V((T, F), bf16), du2=V((T, F), bf16),
        ra=V((T, D), bf16),
        q=V((T, C), bf16), kv=V((2 * I, 2 * C), bf16), p_c=V((HL * T, 2 * I), bf16), o_c=V((T, C), bf16),
        q2=V((T, C), bf16), kv2=V((2 * T, 2 * C), bf16), p_s=V((HL * T, 2 * T), bf16), o_s=V((T, C), bf16),
        pr_c=V((HL * T, I), bf16), qr_c=V((T, C), bf16), or_c=V((T, C), bf16),
        pr_s=V((HL * T, T), bf16), qr_s=V((T, C), bf16), or_s=V((T, C), bf16),
        do=V((2, T, C), bf16), do_o=V((2, T, C), bf16), ds=V((2 * HL * T, max(T, I)), bf16),
        dqkv=V((T, 3 * C), bf16), dq=V((T, C), bf16), dkv=V((I, 2 * C), bf16),
        rc=V((3, half, F), bf16), r1p=V((3, eighth, F), bf16), r1q=V((3, eighth, F), bf16),
        r2p=V((3, piece, F), bf16), r2q=V((3, piece, F), bf16),
        dg=V((8, D), f32), dgr=V((3, 8, D), f32), gz=V((8, D), f32), gzr=V((3, 8, D), f32),
        load_sem=DMA((16,)), out_sem=DMA((5,)),
        y_snd=DMA((8,)), y_rcv=DMA((8,)),
        p_snd=DMA((HL * NCH,)), p_rcv=DMA((HL * NCH,)), kv_snd=DMA((NCH,)), kv_rcv=DMA((NCH,)), do_snd=DMA((2, NCH)), do_rcv=DMA((2, NCH)),
        ar_snd=DMA((3, 4 * NCH)), ar_tot=DMA((3, 4 * NCH)), ar_in=DMA((3, 4 * NCH)), ar_mid=DMA((3, 4 * NCH)),
        j_snd=DMA((6, 10)), j_rcv=DMA((6, 10)), j_own=DMA((6, 2)), dg_snd=DMA((3,)), dg_rcv=DMA((3,)), gz_snd=DMA((3,)), gz_rcv=DMA((3,)),
    )
    names = [*in_vmem, *in_any, *out_any, *out_vmem, *scratch]
    outs = pl.pallas_call(
        functools.partial(block_kernel, names, T, I, D, C, F, CH),
        out_shape=(*out_any.values(), *out_vmem.values()),
        in_specs=[pl.BlockSpec(memory_space=pltpu.VMEM)] * len(in_vmem)
        + [pl.BlockSpec(memory_space=pl.ANY)] * len(in_any),
        out_specs=tuple(
            [pl.BlockSpec(memory_space=pl.ANY)] * len(out_any)
            + [pl.BlockSpec(memory_space=pltpu.VMEM)] * len(out_vmem)
        ),
        scratch_shapes=list(scratch.values()),
        compiler_params=pltpu.CompilerParams(
            collective_id=0, has_side_effects=True, vmem_limit_bytes=66900000
        ),
        name="block_kernel",
    )(*in_vmem.values(), *in_any.values())
    return dict(zip([*out_any, *out_vmem], outs, strict=True))


def widen_kernel(C, n_gains, lat_in, lgrad_in, igrad_in, gains_in, cross, own, in_a, out_a, in_b, out_b,
                 lat, lgrad, igrad, gains, q, kv, o_c, w_in_a, w_out_a, qkv, o_s, w_in_b, w_out_b):
    lat[0] = lat_in[...]
    lgrad[0] = lgrad_in[...].astype(f32)
    igrad[0] = igrad_in[...].astype(f32)
    gains[...] = gains_in[0:n_gains, :]
    for j in range(2):
        kv[:, j, :] = cross[:, j * C : (j + 1) * C].astype(f32)
    q[...] = cross[:, 2 * C : 3 * C].astype(f32)
    o_c[...] = cross[:, 3 * C :].astype(f32)
    for j in range(3):
        qkv[j] = own[:, j * C : (j + 1) * C].astype(f32)
    o_s[...] = own[:, 3 * C :].astype(f32)
    w_in_a[...] = in_a[...].astype(f32)
    w_out_a[...] = out_a[...].astype(f32)
    w_in_b[...] = in_b[...].astype(f32)
    w_out_b[...] = out_b[...].astype(f32)


def widen_call(o, C, n_gains):
    T, D = o["latents_out"].shape
    I = o["input_grad"].shape[0]
    F = o["g_in_a"].shape[1]
    steps = 4
    S = jax.ShapeDtypeStruct

    def flat(n, width):
        return pl.BlockSpec((n // steps, width), lambda i: (i, 0))

    def whole(n, width):
        return pl.BlockSpec((n, width), lambda i: (0, 0))

    def lead(n, width):
        return pl.BlockSpec((1, n // steps, width), lambda i: (0, i, 0))

    ins = ["latents_out", "latent_grad", "input_grad", "gains_grad", "g_cross", "g_self", "g_in_a", "g_out_a", "g_in_b", "g_out_b"]
    big = flat(D, F)
    col = flat(D, C)
    outs = pl.pallas_call(
        functools.partial(widen_kernel, C, n_gains),
        grid=(steps,),
        in_specs=[flat(T, D), flat(T, D), flat(I, D), whole(8, D), big, big, big, big, big, big],
        out_specs=(
            lead(T, D), lead(T, D), lead(I, D), whole(n_gains, D), col,
            pl.BlockSpec((D // steps, 2, C), lambda i: (i, 0, 0)), col, big, big,
            pl.BlockSpec((3, D // steps, C), lambda i: (0, i, 0)), col, big, big,
        ),
        out_shape=(
            S((1, T, D), bf16), S((1, T, D), f32), S((1, I, D), f32), S((n_gains, D), f32), S((D, C), f32),
            S((D, 2, C), f32), S((D, C), f32), S((D, F), f32), S((D, F), f32),
            S((3, D, C), f32), S((D, C), f32), S((D, F), f32), S((D, F), f32),
        ),
        compiler_params=pltpu.CompilerParams(vmem_limit_bytes=62 * 2**20),
        name="widen_kernel",
    )(*[o[n] for n in ins])
    outs = list(outs)
    outs[9] = jnp.moveaxis(outs[9], 0, 1)
    return tuple(outs)


def per_device_fast(
    latents, inputs, latent_group, latent_valid, input_group, input_valid, gains,
    w_q_cross, w_kv_cross, w_o_cross, w_in_a, w_out_a, w_qkv_self, w_o_self, w_in_b, w_out_b, out_grad,
):
    D = latents.shape[2]
    C = w_q_cross.shape[1]
    weights = dict(
        w_q_c=w_q_cross, w_kv_c=w_kv_cross.reshape(D, 2 * C), w_o_c=w_o_cross, w_in_a=w_in_a,
        w_out_a=w_out_a, w_qkv_s=jnp.moveaxis(w_qkv_self, 1, 0), w_o_s=w_o_self, w_in_b=w_in_b, w_out_b=w_out_b,
    )
    o = block_call(
        latents[0], inputs[0], latent_group, latent_valid, input_group, input_valid, gains, weights, out_grad[0]
    )
    return widen_call(o, C, gains.shape[0])


def solution(mesh):
    fast = dict(mesh.shape) == {"group": 4, "blk": 2, "head": 4}
    return jax.shard_map(
        per_device_fast if fast else per_device,
        mesh=mesh,
        in_specs=(
            P("group", "blk", None),
            P("group", "blk", None),
            P("group", "blk"),
            P("group", "blk"),
            P("group", "blk"),
            P("group", "blk"),
            P(),
            P(None, "head"),
            P(None, None, "head"),
            P(None, "head"),
            P(None, "head"),
            P(None, "head"),
            P(None, None, "head"),
            P(None, "head"),
            P(None, "head"),
            P(None, "head"),
            P("group", "blk", None),
        ),
        out_specs=(
            P("group", "blk", None),
            P("group", "blk", None),
            P("group", "blk", None),
            P(),
            P(None, "head"),
            P(None, None, "head"),
            P(None, "head"),
            P(None, "head"),
            P(None, "head"),
            P(None, None, "head"),
            P(None, "head"),
            P(None, "head"),
            P(None, "head"),
        ),
        check_vma=False,
    )
```

```python
import functools
import types

import jax
import jax.numpy as jnp
from jax import lax
from jax.experimental import pallas as pl
from jax.experimental.pallas import tpu as pltpu
from jax.sharding import PartitionSpec as P

HEAD_DIM = 128


masked_fill = -1000.0
contract_last = (((1,), (1,)), ((), ()))


def layer_norm(values, gains_row):
    centred = values - jnp.mean(values, axis=-1, keepdims=True)
    variance = jnp.mean(centred * centred, axis=-1, keepdims=True)
    return centred * lax.rsqrt(variance + 1e-05) * gains_row


def norm_back(values, gains_row, cotangent):
    unused, pullback = jax.vjp(layer_norm, values, gains_row)
    return pullback(cotangent)


def out_product(left, right):
    return lax.dot_general(left, right, contract_last, preferred_element_type=jnp.float32)


def block_rows(item_count):
    if item_count > 1024 and item_count % 1024 == 0:
        return 1024
    return item_count


def head_sum(partial_sum):
    return lax.psum(partial_sum, "head")


def head_grad_sum(partial_sum):
    return lax.psum(partial_sum, "head")


def score_block(query_heads, key_heads, query_code, key_code):
    scores = jnp.einsum(
        "qhd,khd->hqk", query_heads, key_heads, preferred_element_type=jnp.float32
    ) * HEAD_DIM ** (-0.5)
    allowed = query_code[:, None] == key_code[None, :]
    return (jnp.where(allowed[None], scores, masked_fill), allowed)


def cycle_attend(queries, query_code, key_rows, value_rows, key_code):
    row_count = queries.shape[0]
    heads_local = queries.shape[1] // HEAD_DIM
    query_heads = queries.reshape(row_count, heads_local, HEAD_DIM)

    def stats_block(state_carry, block_data):
        running, totals = state_carry
        key_block, code_block = block_data
        key_heads = key_block.reshape(key_block.shape[0], heads_local, HEAD_DIM)
        scores, allowed = score_block(query_heads, key_heads, query_code, code_block)
        largest = jnp.maximum(running, jnp.max(scores, axis=-1))
        totals = totals * jnp.exp(running - largest) + jnp.sum(
            jnp.exp(scores - largest[:, :, None]), axis=-1
        )
        return ((largest, totals), None)

    stats_init = (
        jnp.full((heads_local, row_count), -jnp.inf, jnp.float32),
        jnp.zeros((heads_local, row_count), jnp.float32),
    )
    state_carry = stats_init
    key_piece = lax.all_gather(key_rows, "blk", axis=0, tiled=True)
    code_piece = lax.all_gather(key_code, "blk", axis=0, tiled=True)
    item_count = key_piece.shape[0]
    step_rows = block_rows(item_count)
    block_count = item_count // step_rows
    stacked = (
        key_piece.reshape(block_count, step_rows, key_piece.shape[1]),
        code_piece.reshape(block_count, step_rows),
    )
    state_carry, unused = lax.scan(stats_block, state_carry, stacked)
    running, totals = state_carry
    log_sums = running + jnp.log(totals)

    def one_block(accumulated, block_data):
        key_block, value_block, code_block = block_data
        key_heads = key_block.reshape(key_block.shape[0], heads_local, HEAD_DIM)
        value_heads = value_block.reshape(value_block.shape[0], heads_local, HEAD_DIM)
        scores, allowed = score_block(query_heads, key_heads, query_code, code_block)
        prob_rows = jnp.exp(scores - log_sums[:, :, None]).astype(jnp.bfloat16)
        accumulated = accumulated + jnp.einsum(
            "hqk,khd->qhd", prob_rows, value_heads, preferred_element_type=jnp.float32
        )
        return (accumulated, None)

    initial = jnp.zeros((row_count, heads_local, HEAD_DIM), jnp.float32)
    accumulated = initial
    key_piece = lax.all_gather(key_rows, "blk", axis=0, tiled=True)
    value_piece = lax.all_gather(value_rows, "blk", axis=0, tiled=True)
    code_piece = lax.all_gather(key_code, "blk", axis=0, tiled=True)
    item_count = key_piece.shape[0]
    step_rows = block_rows(item_count)
    block_count = item_count // step_rows
    stacked = (
        key_piece.reshape(block_count, step_rows, key_piece.shape[1]),
        value_piece.reshape(block_count, step_rows, value_piece.shape[1]),
        code_piece.reshape(block_count, step_rows),
    )
    accumulated, unused = lax.scan(one_block, accumulated, stacked)
    mixed = accumulated.reshape(row_count, heads_local * HEAD_DIM)
    return (mixed, log_sums)


def grad_parts(query_rows, grad_rows, query_code, log_sums, deltas, key_rows, value_rows, key_code):
    heads_local = query_rows.shape[1] // HEAD_DIM
    query_heads = query_rows.reshape(query_rows.shape[0], heads_local, HEAD_DIM)
    grad_heads = grad_rows.reshape(grad_rows.shape[0], heads_local, HEAD_DIM)
    key_heads = key_rows.reshape(key_rows.shape[0], heads_local, HEAD_DIM)
    value_heads = value_rows.reshape(value_rows.shape[0], heads_local, HEAD_DIM)
    scores, allowed = score_block(query_heads, key_heads, query_code, key_code)
    prob_rows = jnp.exp(scores - log_sums[:, :, None])
    grad_probs = jnp.einsum(
        "qhd,khd->hqk", grad_heads, value_heads, preferred_element_type=jnp.float32
    )
    grad_scores = jnp.where(
        allowed[None], prob_rows * (grad_probs - deltas[:, :, None]), 0.0
    ).astype(jnp.bfloat16)
    return (query_heads, grad_heads, key_heads, grad_scores, prob_rows)


def query_part(grad_scores, key_heads, row_shape):
    grad_query = jnp.einsum(
        "hqk,khd->qhd", grad_scores, key_heads, preferred_element_type=jnp.float32
    ) * HEAD_DIM ** (-0.5)
    return grad_query.reshape(row_shape)


def key_parts(grad_scores, prob_rows, query_heads, grad_heads, row_shape):
    grad_key = jnp.einsum(
        "hqk,qhd->khd", grad_scores, query_heads, preferred_element_type=jnp.float32
    ) * HEAD_DIM ** (-0.5)
    grad_value = jnp.einsum(
        "hqk,qhd->khd",
        prob_rows.astype(jnp.bfloat16),
        grad_heads,
        preferred_element_type=jnp.float32,
    )
    return (grad_key.reshape(row_shape), grad_value.reshape(row_shape))


def row_delta(grad_mixed, mixed):
    row_count = mixed.shape[0]
    heads_local = mixed.shape[1] // HEAD_DIM
    product = (grad_mixed.astype(jnp.float32) * mixed).reshape(row_count, heads_local, HEAD_DIM)
    return jnp.sum(product, axis=-1).T


def attend_back(queries, grad_mixed, query_code, log_sums, deltas, key_rows, value_rows, key_code):
    row_count = queries.shape[0]
    col_width = queries.shape[1]
    heads_local = col_width // HEAD_DIM
    all_keys, all_values, all_kcodes, all_queries, all_grads, all_qcodes = (
        lax.all_gather(key_rows, "blk", axis=0, tiled=True),
        lax.all_gather(value_rows, "blk", axis=0, tiled=True),
        lax.all_gather(key_code, "blk", axis=0, tiled=True),
        lax.all_gather(queries, "blk", axis=0, tiled=True),
        lax.all_gather(grad_mixed, "blk", axis=0, tiled=True),
        lax.all_gather(query_code, "blk", axis=0, tiled=True),
    )
    all_sums, all_deltas = (
        lax.all_gather(log_sums, "blk", axis=1, tiled=True),
        lax.all_gather(deltas, "blk", axis=1, tiled=True),
    )
    key_total = all_keys.shape[0]
    key_step = block_rows(key_total)
    key_blocks = key_total // key_step

    def own_queries(grad_query, block_data):
        key_block_rows, value_block_rows, code_block = block_data
        parts = grad_parts(
            queries,
            grad_mixed,
            query_code,
            log_sums,
            deltas,
            key_block_rows,
            value_block_rows,
            code_block,
        )
        return (grad_query + query_part(parts[3], parts[2], queries.shape), None)

    key_stack = (
        all_keys.reshape(key_blocks, key_step, col_width),
        all_values.reshape(key_blocks, key_step, col_width),
        all_kcodes.reshape(key_blocks, key_step),
    )
    grad_query, unused = lax.scan(
        own_queries, jnp.zeros((row_count, col_width), jnp.float32), key_stack
    )
    query_total = all_queries.shape[0]
    query_step = block_rows(query_total)
    query_blocks = query_total // query_step
    key_count = key_rows.shape[0]

    def own_keys(state_carry, block_data):
        grad_key, grad_value = state_carry
        query_block_rows, grad_block_rows, code_block, sums_block, deltas_block = block_data
        query_heads, grad_heads, key_heads, grad_scores, prob_rows = grad_parts(
            query_block_rows,
            grad_block_rows,
            code_block,
            sums_block,
            deltas_block,
            key_rows,
            value_rows,
            key_code,
        )
        part_key, part_value = key_parts(
            grad_scores, prob_rows, query_heads, grad_heads, key_rows.shape
        )
        return ((grad_key + part_key, grad_value + part_value), None)

    query_stack = (
        all_queries.reshape(query_blocks, query_step, col_width),
        all_grads.reshape(query_blocks, query_step, col_width),
        all_qcodes.reshape(query_blocks, query_step),
        all_sums.reshape(heads_local, query_blocks, query_step).transpose(1, 0, 2),
        all_deltas.reshape(heads_local, query_blocks, query_step).transpose(1, 0, 2),
    )
    zeros_keys = jnp.zeros((key_count, col_width), jnp.float32)
    (grad_key, grad_value), unused = lax.scan(own_keys, (zeros_keys, zeros_keys), query_stack)
    return (grad_query, grad_key, grad_value)


def mlp_forward(stream, gains_row, weight_in, weight_out):
    hidden_in = layer_norm(stream, gains_row).astype(jnp.bfloat16)
    hidden = jnp.dot(hidden_in, weight_in, preferred_element_type=jnp.float32)
    activated = jax.nn.gelu(hidden).astype(jnp.bfloat16)
    branch = head_sum(out_product(activated, weight_out))
    return (stream + branch, (hidden_in, hidden, activated))


def mlp_backward(stream, gains_row, weight_in, weight_out, saved, grad_stream):
    hidden_in, hidden, activated = saved
    grad_low = grad_stream.astype(jnp.bfloat16)
    grad_weight_out = jnp.einsum(
        "td,tf->df", grad_low, activated, preferred_element_type=jnp.float32
    )
    grad_activated = jnp.dot(grad_low, weight_out, preferred_element_type=jnp.float32)
    unused, gelu_back = jax.vjp(jax.nn.gelu, hidden)
    grad_hidden = gelu_back(grad_activated)[0].astype(jnp.bfloat16)
    grad_weight_in = jnp.einsum(
        "td,tf->df", hidden_in, grad_hidden, preferred_element_type=jnp.float32
    )
    grad_normed = head_grad_sum(out_product(grad_hidden, weight_in))
    grad_input, grad_gain = norm_back(stream, gains_row, grad_normed)
    return (grad_stream + grad_input, grad_gain, grad_weight_in, grad_weight_out)


def self_forward(stream, gains_row, weight_triple, weight_out, query_code, key_code):
    normed_low = layer_norm(stream, gains_row).astype(jnp.bfloat16)
    col_width = weight_triple.shape[2]
    triple = jnp.dot(
        normed_low,
        weight_triple.reshape(weight_triple.shape[0], 3 * col_width),
        preferred_element_type=jnp.float32,
    ).astype(jnp.bfloat16)
    queries = triple[:, :col_width]
    key_rows = triple[:, col_width : 2 * col_width]
    value_rows = triple[:, 2 * col_width :]
    mixed, log_sums = cycle_attend(queries, query_code, key_rows, value_rows, key_code)
    mixed_low = mixed.astype(jnp.bfloat16)
    branch = head_sum(out_product(mixed_low, weight_out))
    return (
        stream + branch,
        (normed_low, queries, key_rows, value_rows, mixed, mixed_low, log_sums),
    )


def self_backward(
    stream, gains_row, weight_triple, weight_out, saved, grad_stream, query_code, key_code
):
    normed_low, queries, key_rows, value_rows, mixed, mixed_low, log_sums = saved
    grad_low = grad_stream.astype(jnp.bfloat16)
    grad_weight_out = jnp.einsum(
        "td,ti->di", grad_low, mixed_low, preferred_element_type=jnp.float32
    )
    grad_mixed = jnp.dot(grad_low, weight_out, preferred_element_type=jnp.float32).astype(
        jnp.bfloat16
    )
    deltas = row_delta(grad_mixed, mixed)
    grad_query, grad_key, grad_value = attend_back(
        queries, grad_mixed, query_code, log_sums, deltas, key_rows, value_rows, key_code
    )
    grad_triple = jnp.concatenate([grad_query, grad_key, grad_value], axis=1).astype(jnp.bfloat16)
    grad_weight_triple = jnp.einsum(
        "td,tc->dc", normed_low, grad_triple, preferred_element_type=jnp.float32
    ).reshape(weight_triple.shape)
    grad_normed = head_grad_sum(
        out_product(grad_triple, weight_triple.reshape(weight_triple.shape[0], -1))
    )
    grad_input, grad_gain = norm_back(stream, gains_row, grad_normed)
    return (grad_stream + grad_input, grad_gain, grad_weight_triple, grad_weight_out)


def cross_forward(
    stream, input_rows, gains, weight_query, weight_pairs, weight_out, query_code, key_code
):
    latent_low = layer_norm(stream, gains[0]).astype(jnp.bfloat16)
    input_low = layer_norm(input_rows, gains[1]).astype(jnp.bfloat16)
    col_width = weight_query.shape[1]
    queries = jnp.dot(latent_low, weight_query, preferred_element_type=jnp.float32).astype(
        jnp.bfloat16
    )
    paired = jnp.dot(
        input_low,
        weight_pairs.reshape(weight_pairs.shape[0], 2 * col_width),
        preferred_element_type=jnp.float32,
    ).astype(jnp.bfloat16)
    key_rows = paired[:, :col_width]
    value_rows = paired[:, col_width:]
    mixed, log_sums = cycle_attend(queries, query_code, key_rows, value_rows, key_code)
    mixed_low = mixed.astype(jnp.bfloat16)
    branch = head_sum(out_product(mixed_low, weight_out))
    return (
        stream + branch,
        (latent_low, input_low, queries, key_rows, value_rows, mixed, mixed_low, log_sums),
    )


def cross_backward(
    stream,
    input_rows,
    gains,
    weight_query,
    weight_pairs,
    weight_out,
    saved,
    grad_stream,
    query_code,
    key_code,
):
    latent_low, input_low, queries, key_rows, value_rows, mixed, mixed_low, log_sums = saved
    grad_low = grad_stream.astype(jnp.bfloat16)
    grad_weight_out = jnp.einsum(
        "td,ti->di", grad_low, mixed_low, preferred_element_type=jnp.float32
    )
    grad_mixed = jnp.dot(grad_low, weight_out, preferred_element_type=jnp.float32).astype(
        jnp.bfloat16
    )
    deltas = row_delta(grad_mixed, mixed)
    grad_query, grad_key, grad_value = attend_back(
        queries, grad_mixed, query_code, log_sums, deltas, key_rows, value_rows, key_code
    )
    grad_query_low = grad_query.astype(jnp.bfloat16)
    grad_pairs = jnp.concatenate([grad_key, grad_value], axis=1).astype(jnp.bfloat16)
    grad_weight_query = jnp.einsum(
        "td,tc->dc", latent_low, grad_query_low, preferred_element_type=jnp.float32
    )
    grad_weight_pairs = jnp.einsum(
        "td,tc->dc", input_low, grad_pairs, preferred_element_type=jnp.float32
    ).reshape(weight_pairs.shape)
    latent_part = out_product(grad_query_low, weight_query)
    input_part = out_product(grad_pairs, weight_pairs.reshape(weight_pairs.shape[0], -1))
    latent_normed, input_normed = lax.psum((latent_part, input_part), "head")
    grad_latent, gain_zero = norm_back(stream, gains[0], latent_normed)
    grad_inputs, gain_one = norm_back(input_rows, gains[1], input_normed)
    return (
        grad_stream + grad_latent,
        grad_inputs,
        gain_zero,
        gain_one,
        grad_weight_query,
        grad_weight_pairs,
        grad_weight_out,
    )


def per_device(
    latents,
    inputs,
    latent_group,
    latent_valid,
    input_group,
    input_valid,
    gains,
    w_q_cross,
    w_kv_cross,
    w_o_cross,
    w_in_a,
    w_out_a,
    w_qkv_self,
    w_o_self,
    w_in_b,
    w_out_b,
    out_grad,
):
    start_stream = latents[0].astype(jnp.float32)
    input_rows = inputs[0].astype(jnp.float32)
    query_code = latent_group[0].astype(jnp.bfloat16)
    input_code = jnp.where(input_valid[0] == 1, input_group[0], -1).astype(jnp.bfloat16)
    self_code = jnp.where(latent_valid[0] == 1, latent_group[0], -1).astype(jnp.bfloat16)
    cross_stream, cross_saved = cross_forward(
        start_stream, input_rows, gains, w_q_cross, w_kv_cross, w_o_cross, query_code, input_code
    )
    middle_stream, first_saved = mlp_forward(cross_stream, gains[2], w_in_a, w_out_a)
    self_stream, self_saved = self_forward(
        middle_stream, gains[3], w_qkv_self, w_o_self, query_code, self_code
    )
    final_stream, second_saved = mlp_forward(self_stream, gains[4], w_in_b, w_out_b)
    grad_stream = out_grad[0].astype(jnp.float32)
    grad_stream, gain_four, grad_in_b, grad_out_b = mlp_backward(
        self_stream, gains[4], w_in_b, w_out_b, second_saved, grad_stream
    )
    grad_stream, gain_three, grad_qkv_self, grad_o_self = self_backward(
        middle_stream,
        gains[3],
        w_qkv_self,
        w_o_self,
        self_saved,
        grad_stream,
        query_code,
        self_code,
    )
    grad_stream, gain_two, grad_in_a, grad_out_a = mlp_backward(
        cross_stream, gains[2], w_in_a, w_out_a, first_saved, grad_stream
    )
    grad_stream, grad_inputs, gain_zero, gain_one, grad_q_cross, grad_kv_cross, grad_o_cross = (
        cross_backward(
            start_stream,
            input_rows,
            gains,
            w_q_cross,
            w_kv_cross,
            w_o_cross,
            cross_saved,
            grad_stream,
            query_code,
            input_code,
        )
    )
    gain_terms = jnp.stack([gain_zero, gain_one, gain_two, gain_three, gain_four], axis=1)
    (
        sum_gains,
        sum_q_cross,
        sum_kv_cross,
        sum_o_cross,
        sum_in_a,
        sum_out_a,
        sum_qkv_self,
        sum_o_self,
        sum_in_b,
        sum_out_b,
    ) = (
        lax.psum_scatter(gain_terms, ("group", "blk"), scatter_dimension=0, tiled=True),
        lax.psum_scatter(grad_q_cross, ("group", "blk"), scatter_dimension=0, tiled=True),
        lax.psum_scatter(grad_kv_cross, ("group", "blk"), scatter_dimension=0, tiled=True),
        lax.psum_scatter(grad_o_cross, ("group", "blk"), scatter_dimension=0, tiled=True),
        lax.psum_scatter(grad_in_a, ("group", "blk"), scatter_dimension=0, tiled=True),
        lax.psum_scatter(grad_out_a, ("group", "blk"), scatter_dimension=0, tiled=True),
        lax.psum_scatter(grad_qkv_self, ("group", "blk"), scatter_dimension=0, tiled=True),
        lax.psum_scatter(grad_o_self, ("group", "blk"), scatter_dimension=0, tiled=True),
        lax.psum_scatter(grad_in_b, ("group", "blk"), scatter_dimension=0, tiled=True),
        lax.psum_scatter(grad_out_b, ("group", "blk"), scatter_dimension=0, tiled=True),
    )
    (
        full_gains,
        full_q_cross,
        full_kv_cross,
        full_o_cross,
        full_in_a,
        full_out_a,
        full_qkv_self,
        full_o_self,
        full_in_b,
        full_out_b,
    ) = (
        lax.all_gather(sum_gains, ("group", "blk"), axis=0, tiled=True),
        lax.all_gather(sum_q_cross, ("group", "blk"), axis=0, tiled=True),
        lax.all_gather(sum_kv_cross, ("group", "blk"), axis=0, tiled=True),
        lax.all_gather(sum_o_cross, ("group", "blk"), axis=0, tiled=True),
        lax.all_gather(sum_in_a, ("group", "blk"), axis=0, tiled=True),
        lax.all_gather(sum_out_a, ("group", "blk"), axis=0, tiled=True),
        lax.all_gather(sum_qkv_self, ("group", "blk"), axis=0, tiled=True),
        lax.all_gather(sum_o_self, ("group", "blk"), axis=0, tiled=True),
        lax.all_gather(sum_in_b, ("group", "blk"), axis=0, tiled=True),
        lax.all_gather(sum_out_b, ("group", "blk"), axis=0, tiled=True),
    )
    return (
        final_stream.astype(jnp.bfloat16)[None],
        grad_stream[None],
        grad_inputs[None],
        full_gains.T,
        full_q_cross,
        full_kv_cross,
        full_o_cross,
        full_in_a,
        full_out_a,
        full_qkv_self,
        full_o_self,
        full_in_b,
        full_out_b,
    )


MESH = pl.DeviceIdType.MESH
bf16, f32 = jnp.bfloat16, jnp.float32
LANES = 128
TILE = 256
SCALE = HEAD_DIM**-0.5
GELU_A = 0.7978845608028654
GELU_B = 0.044715


def dot_nn(a, b):
    return jnp.dot(a, b, preferred_element_type=f32)


def dot_nt(a, b):
    return lax.dot_general(a, b, (((1,), (1,)), ((), ())), preferred_element_type=f32)


def dot_tn(a, b):
    return lax.dot_general(a, b, (((0,), (0,)), ((), ())), preferred_element_type=f32)


def norm_rows(x):
    c = x - jnp.mean(x, axis=-1, keepdims=True)
    rstd = lax.rsqrt(jnp.mean(c * c, axis=-1, keepdims=True) + 1e-05)
    return c * rstd, rstd


def gelu_both(u):
    u2 = u * u
    t = jnp.tanh(GELU_A * u * (1.0 + GELU_B * u2))
    half = 0.5 * (1.0 + t)
    slope = half + 0.5 * u * (1.0 - t * t) * (GELU_A * (1.0 + 3.0 * GELU_B * u2))
    return u * half, slope


def loop(start, stop, body):
    def step(k, carry):
        body(k)
        return carry

    lax.fori_loop(start, stop, step, 0)


SCHEDULE = dict(
    fifth=["At", "Bt", "", "A1", "B1", "", "", ""],
    sixth_put=["St A2 B2"],
    sixth=["A3", "S1", "B3", "", "S2 A4", "", "S3 B4", ""],
    seventh_pre=["Ct Dt"],
    seventh=["A5", "S4", "B5", "", "", "C1 A6 B6", "S5", "D1"],
    last_put=["Xt C2"],
    late_end=["C3 D2 S6"],
    input=["X1", "C4", "D3", "X2 gz1"],
    last=["", "gz2", "X3 D4", "C5 gz3 dg0", "X4 dg1", "", "D5 dg2", "X5 dg3"],
    end=["C6 X6 D6"],
)


def block_kernel(names, T, I, D, C, F, CH, *refs):
    r = types.SimpleNamespace(**dict(zip(names, refs, strict=True)))
    NCH = T // CH
    ICH = I // CH
    HL = C // HEAD_DIM
    g = lax.axis_index("group")
    b = lax.axis_index("blk")
    h = lax.axis_index("head")
    is_mid = (h == 1) | (h == 2)
    is_end = jnp.logical_not(is_mid)
    at_pair = (g, b, h ^ 1)
    at_mid = (g, b, 3 - h)
    at_y = (g, 1 - b, h)
    at_x = (g ^ 2, b, h)
    at_core = (g ^ 1, b, h)
    core = g % 2
    xi = g // 2
    gains = r.gains

    def rows(c, n=CH):
        return pl.ds(pl.multiple_of(c * n, n), n)

    def remote(src, dst, send_sem, recv_sem, where):
        return pltpu.make_async_remote_copy(
            src_ref=src, dst_ref=dst, send_sem=send_sem, recv_sem=recv_sem, device_id=where, device_id_type=MESH
        )

    bar = pltpu.get_barrier_semaphore()
    for where in (at_pair, at_y, at_x, at_core):
        pl.semaphore_signal(bar, inc=1, device_id=where, device_id_type=MESH)

    @pl.when(is_mid)
    def _():
        pl.semaphore_signal(bar, inc=1, device_id=at_mid, device_id_type=MESH)

    loads = {}

    def load(src, dst, name):
        cp = pltpu.make_async_copy(src, dst, r.load_sem.at[len(loads)])
        cp.start()
        loads[name] = cp

    load(r.inputs, r.inp, "inp")
    load(r.w_kv_c, r.wkvc, "wkvc")
    load(r.latents, r.lat, "lat")
    load(r.w_q_c, r.wqc, "wqc")
    load(r.w_o_c, r.woc, "woc")
    load(r.w_in_a, r.wina, "wina")
    load(r.w_out_a, r.wouta, "wouta")
    for j in range(3):
        load(r.w_qkv_s.at[j], r.wqkvs.at[:, pl.ds(j * C, C)], "wqkvs%d" % j)
    load(r.w_o_s, r.wos, "wos")
    load(r.w_in_b, r.winb, "winb")
    load(r.w_out_b, r.woutb, "woutb")
    load(r.out_grad, r.r4, "r4")

    lg = r.latent_group[...]
    ic = jnp.where(r.input_valid[...] == 1, r.input_group[...], -1).astype(f32)
    sc = jnp.where(r.latent_valid[...] == 1, lg, -1).astype(f32)
    lgf = lg.astype(f32)
    r.codes[:, 0:I] = jnp.broadcast_to(ic, (8, I))
    r.codes[:, I : I + T] = jnp.broadcast_to(sc, (8, T))
    r.codes[:, I + T : I + 2 * T] = jnp.broadcast_to(lgf, (8, T))

    def make_columns(line, dst):
        for j in range(T // LANES):
            dst[pl.ds(j * LANES, LANES), :] = jnp.transpose(
                jnp.broadcast_to(line[:, j * LANES : (j + 1) * LANES], (LANES, LANES))
            )

    make_columns(lgf, r.qcol)
    r.dg[...] = jnp.zeros_like(r.dg)
    r.gz[...] = jnp.zeros_like(r.gz)

    @pl.when(is_mid)
    def _():
        pl.semaphore_wait(bar, 5)

    @pl.when(is_end)
    def _():
        pl.semaphore_wait(bar, 4)

    def to_y(src, dst, k):
        return remote(src, dst, r.y_snd.at[k], r.y_rcv.at[k], at_y)

    codes_cp = to_y(r.codes, r.codes_o, 0)
    codes_cp.start()

    SUB = 4
    SR = CH // SUB

    def cp_in(p, c):
        rw = rows(c, SR)
        return remote(r.part.at[p, rw], r.rin.at[p, rw], r.ar_snd.at[p, c], r.ar_in.at[p, c], at_pair)

    def cp_mid(p, c):
        rw = rows(c, SR)
        return remote(r.part.at[p, rw], r.rmid.at[p, rw], r.ar_snd.at[p, c], r.ar_mid.at[p, c], at_mid)

    def cp_tot(p, c):
        rw = rows(c, SR)
        return remote(r.rin.at[p, rw], r.rin.at[p, rw], r.ar_tot.at[p, c], r.ar_in.at[p, c], at_pair)

    def subs(c):
        return [c * SUB + k for k in range(SUB)]

    def ar_send(p, c):
        @pl.when(is_end)
        def _():
            for k in subs(c):
                cp_in(p, k).start()

    def ar_put(p, c, value):
        r.part[p, rows(c)] = value.astype(bf16)
        ar_send(p, c)

    def ar_put_wide(p, c, value):
        r.part[p, rows(c, 2 * CH)] = value.astype(bf16)
        ar_send(p, 2 * c)
        ar_send(p, 2 * c + 1)

    def ar_b(p, c):
        @pl.when(is_mid)
        def _():
            for k in subs(c):
                rw = rows(k, SR)
                cp_in(p, k).wait_recv()
                r.part[p, rw] = r.part[p, rw] + r.rin[p, rw]
                cp_mid(p, k).start()

    def ar_c(p, c, prev=None):
        ar_c_mid(p, c, prev)
        ar_c_end(p, c)

    def ar_c_mid(p, c, prev=None):
        @pl.when(is_mid)
        def _():
            for k in subs(c):
                rw = rows(k, SR)
                cp_mid(p, k).wait_recv()
                cp_mid(p, k).wait_send()
                r.rin[p, rw] = r.part[p, rw] + r.rmid[p, rw]
                if prev is not None:
                    cp_tot(prev, k).wait_send()
                cp_tot(p, k).start()

    def ar_c_end(p, c):
        @pl.when(is_end)
        def _():
            for k in subs(c):
                cp_in(p, k).wait_send()
                cp_tot(p, k).wait_recv()

    def drain(p, c):
        @pl.when(is_mid)
        def _():
            for k in subs(c):
                cp_tot(p, k).wait_send()

    def total_of(p, c):
        return r.rin[p, rows(c)].astype(f32)

    half, quarter, eighth, piece = D // 2, D // 4, D // 8, D // 16
    own = core * half
    p_own = own + xi * eighth
    p_oth = own + (1 - xi) * eighth
    q_base = own + quarter
    q_own = q_base + b * eighth
    q_oth = q_base + (1 - b) * eighth
    p_fin, p_fin_oth = p_own + b * piece, p_own + (1 - b) * piece
    q_fin, q_fin_oth = q_own + xi * piece, q_own + (1 - xi) * piece

    def span(start, n):
        return pl.ds(pl.multiple_of(start, piece), n)

    class Job:
        def __init__(self, index, w, rc, out, parts):
            self.j, self.w, self.rc, self.out, self.parts = index, w, rc, out, parts
            self.s = index % 3

        def tiles(self):
            loop(0, D // TILE, self.tile)
            self.cp_core().start()

        def tile(self, t):
            col = 0
            rw = rows(t, TILE)
            for lhs, rhs in self.parts:
                n = rhs.shape[1]
                self.w[rw, col : col + n] = dot_tn(lhs[:, rw], rhs[...]).astype(bf16)
                col += n

        def cp(self, k, src, dst, where):
            return remote(src, dst, r.j_snd.at[self.j, k], r.j_rcv.at[self.j, k], where)

        def cp_core(self):
            return self.cp(0, self.w.at[span((1 - core) * half, half)], self.rc, at_core)

        def cp_p1(self):
            return self.cp(1, self.w.at[span(p_oth, eighth)], r.r1p.at[self.s], at_x)

        def cp_q1(self):
            return self.cp(2, self.w.at[span(q_oth, eighth)], r.r1q.at[self.s], at_y)

        def cp_p2(self):
            return self.cp(3, self.w.at[span(p_fin_oth, piece)], r.r2p.at[self.s], at_y)

        def cp_q2(self):
            return self.cp(4, self.w.at[span(q_fin_oth, piece)], r.r2q.at[self.s], at_x)

        def cp_p3(self):
            return self.cp(5, self.w.at[span(p_fin, piece)], self.out.at[span(p_fin, piece)], at_y)

        def cp_q3(self):
            return self.cp(6, self.w.at[span(q_fin, piece)], self.out.at[span(q_fin, piece)], at_x)

        def cp_p4(self):
            return self.cp(7, self.out.at[span(p_own, eighth)], self.out.at[span(p_own, eighth)], at_x)

        def cp_q4(self):
            return self.cp(8, self.out.at[span(q_own, eighth)], self.out.at[span(q_own, eighth)], at_y)

        def cp_all(self):
            return self.cp(9, self.out.at[span(own, half)], self.out.at[span(own, half)], at_core)

        def cp_keep(self):
            return (
                pltpu.make_async_copy(
                    self.w.at[span(p_fin, piece)], self.out.at[span(p_fin, piece)], r.j_own.at[self.j, 0]
                ),
                pltpu.make_async_copy(
                    self.w.at[span(q_fin, piece)], self.out.at[span(q_fin, piece)], r.j_own.at[self.j, 1]
                ),
            )

        def add(self, start, n, other):
            rw = span(start, n)
            self.w[rw] = self.w[rw] + other[...]

        def s1(self):
            self.cp_core().wait_recv()
            self.add(p_oth, eighth, self.rc.at[span(p_oth - own, eighth)])
            self.cp_p1().start()
            self.add(q_oth, eighth, self.rc.at[span(q_oth - own, eighth)])
            self.cp_q1().start()
            self.add(p_own, eighth, self.rc.at[span(p_own - own, eighth)])
            self.add(q_own, eighth, self.rc.at[span(q_own - own, eighth)])

        def s2(self):
            self.cp_p1().wait_recv()
            self.add(p_own, eighth, r.r1p.at[self.s])
            self.cp_q1().wait_recv()
            self.add(q_own, eighth, r.r1q.at[self.s])
            self.cp_p2().start()
            self.cp_q2().start()

        def s3(self):
            self.cp_p2().wait_recv()
            self.add(p_fin, piece, r.r2p.at[self.s])
            self.cp_p3().start()
            self.cp_q2().wait_recv()
            self.add(q_fin, piece, r.r2q.at[self.s])
            self.cp_q3().start()
            for cp in self.cp_keep():
                cp.start()

        def s4(self):
            for cp in self.cp_keep():
                cp.wait()
            self.cp_p3().wait_recv()
            self.cp_p4().start()
            self.cp_q3().wait_recv()
            self.cp_q4().start()
            for cp in (self.cp_core(), self.cp_p1(), self.cp_q1(), self.cp_p2(), self.cp_q2(), self.cp_p3(), self.cp_q3()):
                cp.wait_send()

        def s5(self):
            self.cp_p4().wait_recv()
            self.cp_q4().wait_recv()
            self.cp_all().start()
            self.cp_p4().wait_send()
            self.cp_q4().wait_send()

        def s6(self):
            self.cp_all().wait()

    job_out_b = Job(0, r.wj, r.rc.at[0], r.g_out_b, [(r.r4, r.z2)])
    job_in_b = Job(1, r.winb, r.rc.at[1], r.g_in_b, [(r.h2, r.du2)])
    job_self = Job(2, r.woutb, r.rc.at[2], r.g_self, [(r.cs, r.dqkv), (r.ra, r.o_s)])
    job_out_a = Job(3, r.p_s, r.z2, r.g_out_a, [(r.lat, r.z1)])
    job_in_a = Job(4, r.wj, r.du2, r.g_in_a, [(r.h1, r.du1)])
    job_cross = Job(5, r.winb, r.h2, r.g_cross, [(r.bn, r.dkv), (r.an, r.dq), (r.ra, r.o_c)])

    def norm_out(x, gain_row, out, rstd_out, rw):
        xhat, rstd = norm_rows(x)
        rstd_out[rw] = jnp.broadcast_to(rstd, (rstd.shape[0], LANES))
        low = (xhat * gains[gain_row : gain_row + 1, :]).astype(bf16)
        out[rw] = low
        return low

    def norm_grad(cot, low_ref, dg_row, gain_row, rstd_ref, rw):
        gain = gains[gain_row : gain_row + 1, :]
        xhat = low_ref[rw].astype(f32) * (1.0 / gain)
        scaled = cot * gain
        mean_one = jnp.mean(scaled, axis=-1, keepdims=True)
        mean_two = jnp.mean(scaled * xhat, axis=-1, keepdims=True)
        if dg_row is not None:
            r.dg[dg_row : dg_row + 1, :] += jnp.sum(cot * xhat, axis=0, keepdims=True)
        return rstd_ref[rw, 0:1] * (scaled - mean_one - xhat * mean_two)

    loads["inp"].wait()
    loads["wkvc"].wait()

    def kv_chunk(k):
        rw = rows(k, LANES)
        low = norm_out(r.inp[rw].astype(f32), 1, r.bn, r.rs1, rw)
        r.kv[rw] = dot_nn(low, r.wkvc[...]).astype(bf16)

    kv_cps = [to_y(r.kv.at[pl.ds(k * I // 2, I // 2)], r.kv.at[pl.ds(I + k * I // 2, I // 2)], (1, 5)[k]) for k in range(2)]
    for k in range(2):
        loop(k * (I // LANES // 2), (k + 1) * (I // LANES // 2), kv_chunk)
        kv_cps[k].start()

    loads["lat"].wait()
    loads["wqc"].wait()

    def q_chunk(k):
        rw = rows(k, LANES)
        low = norm_out(r.lat[rw].astype(f32), 0, r.an, r.rs0, rw)
        r.q[rw] = dot_nn(low, r.wqc[...]).astype(bf16)

    loop(0, T // LANES, q_chunk)
    codes_cp.wait()
    make_columns(r.codes_o[0:1, I + T : I + 2 * T], r.qcol_o)
    for cp in kv_cps:
        cp.wait()
    loads["woc"].wait()

    def attend_chunk(k, q_ref, kv_ref, p_ref, o_ref, start, n):
        rw = rows(k)
        kc = jnp.concatenate([r.codes[0:1, start : start + n], r.codes_o[0:1, start : start + n]], axis=1)
        allowed = r.qcol[rw, 0:1] == kc
        for hd in range(HL):
            cols = slice(hd * HEAD_DIM, (hd + 1) * HEAD_DIM)
            vcols = slice(C + hd * HEAD_DIM, C + (hd + 1) * HEAD_DIM)
            s = jnp.where(allowed, dot_nt(q_ref[rw, cols], kv_ref[:, cols]) * SCALE, masked_fill)
            e = jnp.exp(s - jnp.max(s, axis=-1, keepdims=True))
            p = (e * (1.0 / jnp.sum(e, axis=-1, keepdims=True))).astype(bf16)
            p_ref[rows(k + hd * NCH), :] = p
            o_ref[rw, cols] = dot_nn(p, kv_ref[:, vcols]).astype(bf16)

    def cross_chunk(k):
        attend_chunk(k, r.q, r.kv, r.p_c, r.o_c, 0, I)
        ar_put(0, k, dot_nt(r.o_c[rows(k)], r.woc[...]))

        @pl.when(k >= 4)
        def _():
            ar_b(0, k - 4)

    loop(0, NCH, cross_chunk)

    back_cross = [
        to_y(r.p_c.at[:, pl.ds(I, I)], r.pr_c, 2), to_y(r.q, r.qr_c, 3), to_y(r.o_c, r.or_c, 4),
    ]
    for cp in back_cross:
        cp.start()
    loads["wina"].wait()
    loads["wouta"].wait()

    def first_chunk(m):
        @pl.when((m >= 2) & (m < NCH - 2))
        def _():
            ar_b(0, m + 2)

        ar_c(0, m)
        rw = rows(m)
        x = r.lat[rw].astype(f32) + total_of(0, m)
        r.xs[rw] = x
        low = norm_out(x, 2, r.h1, r.rs2, rw)
        z, slope = gelu_both(dot_nn(low, r.wina[...]))
        z = z.astype(bf16)
        r.z1[rw] = z
        r.s1[rw] = slope.astype(bf16)
        ar_put(1, m, dot_nt(z, r.wouta[...]))

        @pl.when(m >= NCH - 2)
        def _():
            ar_b(1, m + 2 - NCH)

    loop(0, NCH, first_chunk)
    for j in range(3):
        loads["wqkvs%d" % j].wait()
    loads["wos"].wait()

    def kv2_cp(c):
        return remote(r.kv2.at[rows(c)], r.kv2.at[rows(c + NCH)], r.kv_snd.at[c], r.kv_rcv.at[c], at_y)

    def second_chunk(m):
        @pl.when(m < NCH - 2)
        def _():
            ar_b(1, m + 2)

        ar_c(1, m, 0)
        rw = rows(m)
        x = r.xs[rw] + total_of(1, m)
        r.xs[rw] = x
        low = norm_out(x, 3, r.cs, r.rs3, rw)
        qkv = dot_nn(low, r.wqkvs[...]).astype(bf16)
        r.q2[rw] = qkv[:, :C]
        r.kv2[rw] = qkv[:, C:]
        kv2_cp(m).start()

    loop(0, NCH, second_chunk)
    loads["woutb"].wait()
    loads["r4"].wait()

    def hidden_grad(k):
        rw = rows(k, TILE)
        r.du2[rw] = dot_nn(r.r4[rw], r.woutb[...]).astype(bf16)

    loop(0, T // TILE, hidden_grad)
    loop(0, NCH, lambda c: kv2_cp(c).wait())

    def p_cp(c):
        return remote(r.p_s.at[rows(c), pl.ds(T, T)], r.pr_s.at[rows(c)], r.p_snd.at[c], r.p_rcv.at[c], at_y)

    q_back = to_y(r.q2, r.qr_s, 6)
    q_back.start()

    def self_chunk(k):
        attend_chunk(k, r.q2, r.kv2, r.p_s, r.o_s, I, T)
        for hd in range(HL):
            p_cp(k + hd * NCH).start()

        ar_put(0, k, dot_nt(r.o_s[rows(k)], r.wos[...]))

        @pl.when(k >= 4)
        def _():
            ar_b(0, k - 4)

    loop(0, NCH, self_chunk)
    o_back = to_y(r.o_s, r.or_s, 7)
    o_back.start()
    loads["winb"].wait()

    def third_chunk(m):
        @pl.when((m >= 2) & (m < NCH - 2))
        def _():
            ar_b(0, m + 2)

        ar_c(0, m, 1)
        rw = rows(m)
        x = r.xs[rw] + total_of(0, m)
        r.xs[rw] = x
        low = norm_out(x, 4, r.h2, r.rs4, rw)
        z, slope = gelu_both(dot_nn(low, r.winb[...]))
        z = z.astype(bf16)
        r.z2[rw] = z
        du = (r.du2[rw].astype(f32) * slope).astype(bf16)
        r.du2[rw] = du
        ar_put(1, m, dot_nt(du, r.winb[...]))

        @pl.when((m == 3) | (m == 5))
        def _():
            wide = rows((m - 3) // 2, 2 * CH)
            r.part[2, wide] = dot_nt(r.z2[wide], r.woutb[...]).astype(bf16)

        @pl.when(m >= NCH - 2)
        def _():
            ar_b(1, m + 2 - NCH)

    loop(0, NCH, third_chunk)

    def d_o_cp(k, c):
        return remote(r.do.at[k, rows(c)], r.do_o.at[k, rows(c)], r.do_snd.at[k, c], r.do_rcv.at[k, c], at_y)

    class Back:
        def __init__(self, k, q, qr, kv, p, pr, o, o_r, n, start, dq, dkv, dkv_col):
            self.k, self.q, self.qr, self.kv, self.p, self.pr, self.o, self.o_r = k, q, qr, kv, p, pr, o, o_r
            self.n, self.first, self.dq, self.dkv, self.dkv_col = n, start, dq, dkv, dkv_col
            self.do, self.do_o = r.do.at[k], r.do_o.at[k]

        def own(self, m):
            rw = rows(m)
            n, a = self.n, self.first
            kc = jnp.concatenate([r.codes[0:1, a : a + n], r.codes_o[0:1, a : a + n]], axis=1)
            allowed = r.qcol[rw, 0:1] == kc
            for hd in range(HL):
                cols = slice(hd * HEAD_DIM, (hd + 1) * HEAD_DIM)
                vcols = slice(C + hd * HEAD_DIM, C + (hd + 1) * HEAD_DIM)
                grad = self.do[rw, cols]
                delta = jnp.sum(grad.astype(f32) * self.o[rw, cols].astype(f32), axis=-1, keepdims=True)
                diff = dot_nt(grad, self.kv[:, vcols]) - delta
                prob = self.p[rows(m + hd * NCH), :].astype(f32)
                ds = jnp.where(allowed, prob * diff, 0.0).astype(bf16)
                r.ds[rows(m + 2 * hd * NCH), 0:n] = ds[:, 0:n]
                self.dq[rw, cols] = (dot_nn(ds, self.kv[:, cols]) * SCALE).astype(bf16)

        def other(self, m):
            d_o_cp(self.k, m).wait()
            rw = rows(m)
            n, a = self.n, self.first
            allowed = r.qcol_o[rw, 0:1] == r.codes[0:1, a : a + n]
            for hd in range(HL):
                cols = slice(hd * HEAD_DIM, (hd + 1) * HEAD_DIM)
                vcols = slice(C + hd * HEAD_DIM, C + (hd + 1) * HEAD_DIM)
                grad = self.do_o[rw, cols]
                delta = jnp.sum(grad.astype(f32) * self.o_r[rw, cols].astype(f32), axis=-1, keepdims=True)
                diff = dot_nt(grad, self.kv[0:n, vcols]) - delta
                prob = self.pr[rows(m + hd * NCH), :].astype(f32)
                ds = jnp.where(allowed, prob * diff, 0.0).astype(bf16)
                r.ds[rows(m + (2 * hd + 1) * NCH), 0:n] = ds

        def some_other(self, m, waits):
            if waits is not None:

                @pl.when(m == NCH // 2)
                def _():
                    for wait in waits:
                        wait()

            @pl.when((m >= NCH // 2) & (m < NCH - 2))
            def _():
                self.other(2 * m - NCH)
                self.other(2 * m + 1 - NCH)

            @pl.when(m == NCH - 2)
            def _():
                self.other(NCH - 4)

            @pl.when(m == NCH - 1)
            def _():
                self.other(NCH - 3)

        def keys_own(self):
            n = self.n
            out = []
            for hd in range(HL):
                cols = slice(hd * HEAD_DIM, (hd + 1) * HEAD_DIM)
                at = 2 * hd * T
                dk = dot_tn(r.ds[at : at + T, 0:n], self.q[:, cols])
                dv = dot_tn(self.p[hd * T : (hd + 1) * T, 0:n], self.do[:, cols])
                out.append((dk, dv))
            return out

        def keys(self, own):
            n = self.n
            for hd, (dk, dv) in enumerate(own):
                cols = slice(hd * HEAD_DIM, (hd + 1) * HEAD_DIM)
                at = (2 * hd + 1) * T
                dk = dk + dot_tn(r.ds[at : at + T, 0:n], self.qr[:, cols])
                dv = dv + dot_tn(self.pr[hd * T : (hd + 1) * T, :], self.do_o[:, cols])
                col = self.dkv_col + hd * HEAD_DIM
                self.dkv[:, col : col + HEAD_DIM] = (dk * SCALE).astype(bf16)
                self.dkv[:, col + C : col + C + HEAD_DIM] = dv.astype(bf16)

    back_of_self = Back(0, r.q2, r.qr_s, r.kv2, r.p_s, r.pr_s, r.o_s, r.or_s, T, I, r.dqkv, r.dqkv, C)
    back_of_cross = Back(1, r.q, r.qr_c, r.kv, r.p_c, r.pr_c, r.o_c, r.or_c, I, 0, r.dq, r.dkv, 0)

    jobs = dict(A=job_out_b, B=job_in_b, S=job_self, C=job_out_a, D=job_in_a, X=job_cross)
    extra = {}

    def on(place, m=None):
        for step, words in enumerate(SCHEDULE[place]):
            names = words.split()
            if not names:
                continue

            def run(names=names):
                for name in names:
                    if name in extra:
                        extra[name]()
                    else:
                        getattr(jobs[name[0]], "tiles" if name[1] == "t" else "s" + name[1])()

            if m is None:
                run()
            else:
                pl.when(m == step)(run)

    def fifth_chunk(m):
        @pl.when(m < NCH - 2)
        def _():
            ar_b(1, m + 2)

        ar_c(1, m, 0)
        rw = rows(m)
        dx = r.r4[rw].astype(f32) + norm_grad(total_of(1, m), r.h2, 4, 4, r.rs4, rw)
        r.dxs[rw] = dx
        low = dx.astype(bf16)
        r.ra[rw] = low
        r.do[0, rw] = dot_nn(low, r.wos[...]).astype(bf16)
        d_o_cp(0, m).start()

        @pl.when((m >= NCH // 4) & (m < NCH // 2))
        def _():
            wide = rows(m, 2 * CH)
            r.part[2, wide] = dot_nt(r.z2[wide], r.woutb[...]).astype(bf16)

        @pl.when(m < NCH // 4)
        def _():
            ar_send(2, 2 * m)
            ar_send(2, 2 * m + 1)

        back_of_self.own(m)
        back_of_self.some_other(m, [q_back.wait, o_back.wait, lambda: loop(0, HL * NCH, lambda c: p_cp(c).wait())])

        on("fifth", m)

        @pl.when(m >= NCH // 2)
        def _():
            ar_b(2, m - NCH // 2)

    loop(0, NCH, fifth_chunk)

    def late_out(c):
        ar_c_end(2, c)
        rw = rows(c)
        r.part[2, rw] = (r.xs[rw] + total_of(2, c)).astype(bf16)

    self_keys = back_of_self.keys_own()
    back_of_self.other(NCH - 2)
    back_of_self.other(NCH - 1)
    back_of_self.keys(self_keys)
    def sixth_put(k):
        ar_put_wide(0, k, dot_nt(r.dqkv[rows(k, 2 * CH)], r.wqkvs[...]))

    loop(0, NCH // 2, sixth_put)
    loop(0, NCH // 2, lambda c: ar_c_mid(2, c))
    on("sixth_put")
    loop(0, 2, lambda c: ar_b(0, c))

    def sixth_chunk(m):
        @pl.when(m < NCH - 2)
        def _():
            ar_b(0, m + 2)

        ar_c(0, m, 1)
        rw = rows(m)
        dx = r.dxs[rw] + norm_grad(total_of(0, m), r.cs, 3, 3, r.rs3, rw)
        r.dxs[rw] = dx
        low = dx.astype(bf16)
        r.lat[rw] = low
        du = (dot_nn(low, r.wouta[...]) * r.s1[rw].astype(f32)).astype(bf16)
        r.du1[rw] = du
        ar_put(1, m, dot_nt(du, r.wina[...]))

        @pl.when(m >= NCH - 2)
        def _():
            ar_b(1, m + 2 - NCH)

        @pl.when(m < NCH // 2)
        def _():
            late_out(m)

        on("sixth", m)

    loop(0, NCH, sixth_chunk)
    late_cps = [
        pltpu.make_async_copy(r.part.at[2, rw], r.latents_out.at[rw], r.out_sem.at[2 + 2 * k])
        for k, rw in enumerate([pl.ds(0, T // 2), pl.ds(T // 2, T // 2)])
    ]
    late_cps[0].start()
    def seventh_chunk(m):
        @pl.when(m < NCH - 2)
        def _():
            ar_b(1, m + 2)

        @pl.when(m < NCH // 2)
        def _():
            drain(2, m)

        ar_c(1, m, 0)
        rw = rows(m)
        dx = r.dxs[rw] + norm_grad(total_of(1, m), r.h1, 2, 2, r.rs2, rw)
        r.dxs[rw] = dx
        low = dx.astype(bf16)
        r.ra[rw] = low
        r.do[1, rw] = dot_nn(low, r.woc[...]).astype(bf16)
        d_o_cp(1, m).start()
        back_of_cross.own(m)
        back_of_cross.some_other(m, [cp.wait for cp in back_cross])

        on("seventh", m)

        @pl.when(m >= NCH // 2)
        def _():
            ar_b(2, m)

    on("seventh_pre")
    loop(NCH // 2, NCH, lambda c: ar_send(2, c))
    loop(0, NCH, seventh_chunk)

    cross_keys = back_of_cross.keys_own()
    back_of_cross.other(NCH - 2)
    back_of_cross.other(NCH - 1)
    back_of_cross.keys(cross_keys)

    late_cps[0].wait()

    def put_last(p, k, value, low_ref, gain_row):
        ar_put_wide(p, k, value)
        xhat = low_ref[rows(k, 2 * CH)].astype(f32) * (1.0 / gains[gain_row : gain_row + 1, :])
        r.gz[gain_row : gain_row + 1, :] += jnp.sum(value * xhat, axis=0, keepdims=True)

    loop(0, ICH // 2, lambda k: put_last(2, k, dot_nt(r.dkv[rows(k, 2 * CH)], r.wkvc[...]), r.bn, 1))
    loop(0, NCH // 2, lambda k: put_last(0, k, dot_nt(r.dq[rows(k, 2 * CH)], r.wqc[...]), r.an, 0))

    def gz_cp(k, where):
        return remote(r.gz, r.gzr.at[k], r.gz_snd.at[k], r.gz_rcv.at[k], where)

    @pl.when(is_end)
    def _():
        gz_cp(0, at_pair).start()

    def gz_one():
        @pl.when(is_mid)
        def _():
            gz_cp(0, at_pair).wait_recv()
            r.gz[...] += r.gzr[0]
            gz_cp(1, at_mid).start()

    def gz_two():
        @pl.when(is_mid)
        def _():
            gz_cp(1, at_mid).wait()
            r.gz[...] += r.gzr[1]
            gz_cp(2, at_pair).start()

    def gz_three():
        @pl.when(is_end)
        def _():
            gz_cp(0, at_pair).wait_send()
            gz_cp(2, at_pair).wait_recv()
            r.dg[0:2, :] = r.gzr[2, 0:2, :]

        @pl.when(is_mid)
        def _():
            gz_cp(2, at_pair).wait_send()
            r.dg[0:2, :] = r.gz[0:2, :]

    def dg_cp(k):
        return remote(r.dg, r.dgr.at[k], r.dg_snd.at[k], r.dg_rcv.at[k], (at_core, at_x, at_y)[k])

    def dg_next(k):
        def step():
            dg_cp(k).wait()
            r.dg[...] += r.dgr[k]
            if k < 2:
                dg_cp(k + 1).start()

        return step

    dg_zero, dg_one, dg_two = (dg_next(k) for k in range(3))

    on("last_put")
    loop(NCH // 2, NCH, lambda c: ar_c_mid(2, c))
    on("late_end")
    loop(0, 2, lambda c: ar_b(2, c))

    extra.update(gz1=gz_one, gz2=gz_two, gz3=gz_three, dg0=dg_cp(0).start, dg1=dg_zero, dg2=dg_one, dg3=dg_two)

    def input_chunk(m):
        @pl.when(m < ICH - 2)
        def _():
            ar_b(2, m + 2)

        @pl.when(m >= ICH - 2)
        def _():
            ar_b(0, m + 2 - ICH)

        ar_c(2, m)
        rw = rows(m)
        r.inp[rw] = norm_grad(total_of(2, m), r.bn, None, 1, r.rs1, rw).astype(bf16)

        late_out(m + NCH // 2)
        on("input", m)

    loop(0, ICH, input_chunk)
    out_cps = [
        pltpu.make_async_copy(r.inp, r.input_grad, r.out_sem.at[0]),
        pltpu.make_async_copy(r.lat.at[pl.ds(0, T // 2)], r.latent_grad.at[pl.ds(0, T // 2)], r.out_sem.at[1]),
        pltpu.make_async_copy(r.lat.at[pl.ds(T // 2, T // 2)], r.latent_grad.at[pl.ds(T // 2, T // 2)], r.out_sem.at[3]),
    ]
    out_cps[0].start()
    late_cps[1].start()

    def last_chunk(m):
        @pl.when(m < NCH - 2)
        def _():
            ar_b(0, m + 2)

        ar_c(0, m, 1)
        rw = rows(m)
        r.lat[rw] = (r.dxs[rw] + norm_grad(total_of(0, m), r.an, None, 0, r.rs0, rw)).astype(bf16)

        @pl.when(m == 4)
        def _():
            out_cps[1].start()

        on("last", m)

    loop(0, NCH, last_chunk)
    out_cps[2].start()
    r.gains_grad[...] = r.dg[...]
    on("end")

    loop(0, NCH, lambda c: drain(2, c))
    loop(0, NCH, lambda c: drain(0, c))

    for cp in [*out_cps, late_cps[1]]:
        cp.wait()


def block_call(latents, inputs, latent_group, latent_valid, input_group, input_valid, gains, weights, out_grad):
    T, D = latents.shape
    I = inputs.shape[0]
    C = weights["w_q_c"].shape[1]
    F = weights["w_in_a"].shape[1]
    CH = 64
    NCH = T // CH
    HL = C // HEAD_DIM
    in_vmem = dict(
        latent_group=latent_group, latent_valid=latent_valid, input_group=input_group,
        input_valid=input_valid, gains=gains,
    )
    in_any = dict(latents=latents, inputs=inputs, **weights, out_grad=out_grad)
    S = jax.ShapeDtypeStruct
    out_any = dict(
        latents_out=S((T, D), bf16), latent_grad=S((T, D), bf16), input_grad=S((I, D), bf16),
        g_out_b=S((D, F), bf16), g_in_b=S((D, F), bf16), g_self=S((D, 4 * C), bf16),
        g_out_a=S((D, F), bf16), g_in_a=S((D, F), bf16), g_cross=S((D, 4 * C), bf16),
    )
    out_vmem = dict(gains_grad=S((8, D), f32))
    V, DMA = pltpu.VMEM, pltpu.SemaphoreType.DMA
    half, eighth, piece = D // 2, D // 8, D // 16
    scratch = dict(
        inp=V((I, D), bf16), lat=V((T, D), bf16), r4=V((T, D), bf16),
        wkvc=V((D, 2 * C), bf16), wqc=V((D, C), bf16), woc=V((D, C), bf16),
        wina=V((D, F), bf16), wouta=V((D, F), bf16), wqkvs=V((D, 3 * C), bf16),
        wos=V((D, C), bf16), winb=V((D, F), bf16), woutb=V((D, F), bf16), wj=V((D, F), bf16),
        codes=V((8, I + 2 * T), f32), codes_o=V((8, I + 2 * T), f32),
        qcol=V((T, LANES), f32), qcol_o=V((T, LANES), f32),
        part=V((3, T, D), bf16), rin=V((3, T, D), bf16), rmid=V((3, T, D), bf16),
        xs=V((T, D), f32), dxs=V((T, D), f32),
        an=V((T, D), bf16), bn=V((I, D), bf16), h1=V((T, D), bf16), cs=V((T, D), bf16), h2=V((T, D), bf16),
        rs0=V((T, LANES), f32), rs1=V((I, LANES), f32), rs2=V((T, LANES), f32), rs3=V((T, LANES), f32),
        rs4=V((T, LANES), f32),
        z1=V((T, F), bf16), s1=V((T, F), bf16), du1=V((T, F), bf16), z2=V((T, F), bf16), du2=V((T, F), bf16),
        ra=V((T, D), bf16),
        q=V((T, C), bf16), kv=V((2 * I, 2 * C), bf16), p_c=V((HL * T, 2 * I), bf16), o_c=V((T, C), bf16),
        q2=V((T, C), bf16), kv2=V((2 * T, 2 * C), bf16), p_s=V((HL * T, 2 * T), bf16), o_s=V((T, C), bf16),
        pr_c=V((HL * T, I), bf16), qr_c=V((T, C), bf16), or_c=V((T, C), bf16),
        pr_s=V((HL * T, T), bf16), qr_s=V((T, C), bf16), or_s=V((T, C), bf16),
        do=V((2, T, C), bf16), do_o=V((2, T, C), bf16), ds=V((2 * HL * T, max(T, I)), bf16),
        dqkv=V((T, 3 * C), bf16), dq=V((T, C), bf16), dkv=V((I, 2 * C), bf16),
        rc=V((3, half, F), bf16), r1p=V((3, eighth, F), bf16), r1q=V((3, eighth, F), bf16),
        r2p=V((3, piece, F), bf16), r2q=V((3, piece, F), bf16),
        dg=V((8, D), f32), dgr=V((3, 8, D), f32), gz=V((8, D), f32), gzr=V((3, 8, D), f32),
        load_sem=DMA((16,)), out_sem=DMA((5,)),
        y_snd=DMA((8,)), y_rcv=DMA((8,)),
        p_snd=DMA((HL * NCH,)), p_rcv=DMA((HL * NCH,)), kv_snd=DMA((NCH,)), kv_rcv=DMA((NCH,)), do_snd=DMA((2, NCH)), do_rcv=DMA((2, NCH)),
        ar_snd=DMA((3, 4 * NCH)), ar_tot=DMA((3, 4 * NCH)), ar_in=DMA((3, 4 * NCH)), ar_mid=DMA((3, 4 * NCH)),
        j_snd=DMA((6, 10)), j_rcv=DMA((6, 10)), j_own=DMA((6, 2)), dg_snd=DMA((3,)), dg_rcv=DMA((3,)), gz_snd=DMA((3,)), gz_rcv=DMA((3,)),
    )
    names = [*in_vmem, *in_any, *out_any, *out_vmem, *scratch]
    outs = pl.pallas_call(
        functools.partial(block_kernel, names, T, I, D, C, F, CH),
        out_shape=(*out_any.values(), *out_vmem.values()),
        in_specs=[pl.BlockSpec(memory_space=pltpu.VMEM)] * len(in_vmem)
        + [pl.BlockSpec(memory_space=pl.ANY)] * len(in_any),
        out_specs=tuple(
            [pl.BlockSpec(memory_space=pl.ANY)] * len(out_any)
            + [pl.BlockSpec(memory_space=pltpu.VMEM)] * len(out_vmem)
        ),
        scratch_shapes=list(scratch.values()),
        compiler_params=pltpu.CompilerParams(
            collective_id=0, has_side_effects=True, vmem_limit_bytes=66900000
        ),
        name="block_kernel",
    )(*in_vmem.values(), *in_any.values())
    return dict(zip([*out_any, *out_vmem], outs, strict=True))


def widen_kernel(C, n_gains, lat_in, lgrad_in, igrad_in, gains_in, cross, own, in_a, out_a, in_b, out_b,
                 lat, lgrad, igrad, gains, q, kv, o_c, w_in_a, w_out_a, qkv, o_s, w_in_b, w_out_b):
    lat[0] = lat_in[...]
    lgrad[0] = lgrad_in[...].astype(f32)
    igrad[0] = igrad_in[...].astype(f32)
    gains[...] = gains_in[0:n_gains, :]
    for j in range(2):
        kv[:, j, :] = cross[:, j * C : (j + 1) * C].astype(f32)
    q[...] = cross[:, 2 * C : 3 * C].astype(f32)
    o_c[...] = cross[:, 3 * C :].astype(f32)
    for j in range(3):
        qkv[j] = own[:, j * C : (j + 1) * C].astype(f32)
    o_s[...] = own[:, 3 * C :].astype(f32)
    w_in_a[...] = in_a[...].astype(f32)
    w_out_a[...] = out_a[...].astype(f32)
    w_in_b[...] = in_b[...].astype(f32)
    w_out_b[...] = out_b[...].astype(f32)


def widen_call(o, C, n_gains):
    T, D = o["latents_out"].shape
    I = o["input_grad"].shape[0]
    F = o["g_in_a"].shape[1]
    steps = 2
    S = jax.ShapeDtypeStruct

    def flat(n, width):
        return pl.BlockSpec((n // steps, width), lambda i: (i, 0))

    def whole(n, width):
        return pl.BlockSpec((n, width), lambda i: (0, 0))

    def lead(n, width):
        return pl.BlockSpec((1, n // steps, width), lambda i: (0, i, 0))

    ins = ["latents_out", "latent_grad", "input_grad", "gains_grad", "g_cross", "g_self", "g_in_a", "g_out_a", "g_in_b", "g_out_b"]
    big = flat(D, F)
    col = flat(D, C)
    outs = pl.pallas_call(
        functools.partial(widen_kernel, C, n_gains),
        grid=(steps,),
        in_specs=[flat(T, D), flat(T, D), flat(I, D), whole(8, D), big, big, big, big, big, big],
        out_specs=(
            lead(T, D), lead(T, D), lead(I, D), whole(n_gains, D), col,
            pl.BlockSpec((D // steps, 2, C), lambda i: (i, 0, 0)), col, big, big,
            pl.BlockSpec((3, D // steps, C), lambda i: (0, i, 0)), col, big, big,
        ),
        out_shape=(
            S((1, T, D), bf16), S((1, T, D), f32), S((1, I, D), f32), S((n_gains, D), f32), S((D, C), f32),
            S((D, 2, C), f32), S((D, C), f32), S((D, F), f32), S((D, F), f32),
            S((3, D, C), f32), S((D, C), f32), S((D, F), f32), S((D, F), f32),
        ),
        compiler_params=pltpu.CompilerParams(vmem_limit_bytes=62 * 2**20),
        name="widen_kernel",
    )(*[o[n] for n in ins])
    outs = list(outs)
    outs[9] = jnp.moveaxis(outs[9], 0, 1)
    return tuple(outs)


def per_device_fast(
    latents, inputs, latent_group, latent_valid, input_group, input_valid, gains,
    w_q_cross, w_kv_cross, w_o_cross, w_in_a, w_out_a, w_qkv_self, w_o_self, w_in_b, w_out_b, out_grad,
):
    D = latents.shape[2]
    C = w_q_cross.shape[1]
    weights = dict(
        w_q_c=w_q_cross, w_kv_c=w_kv_cross.reshape(D, 2 * C), w_o_c=w_o_cross, w_in_a=w_in_a,
        w_out_a=w_out_a, w_qkv_s=jnp.moveaxis(w_qkv_self, 1, 0), w_o_s=w_o_self, w_in_b=w_in_b, w_out_b=w_out_b,
    )
    o = block_call(
        latents[0], inputs[0], latent_group, latent_valid, input_group, input_valid, gains, weights, out_grad[0]
    )
    return widen_call(o, C, gains.shape[0])


def solution(mesh):
    fast = dict(mesh.shape) == {"group": 4, "blk": 2, "head": 4}
    return jax.shard_map(
        per_device_fast if fast else per_device,
        mesh=mesh,
        in_specs=(
            P("group", "blk", None),
            P("group", "blk", None),
            P("group", "blk"),
            P("group", "blk"),
            P("group", "blk"),
            P("group", "blk"),
            P(),
            P(None, "head"),
            P(None, None, "head"),
            P(None, "head"),
            P(None, "head"),
            P(None, "head"),
            P(None, None, "head"),
            P(None, "head"),
            P(None, "head"),
            P(None, "head"),
            P("group", "blk", None),
        ),
        out_specs=(
            P("group", "blk", None),
            P("group", "blk", None),
            P("group", "blk", None),
            P(),
            P(None, "head"),
            P(None, None, "head"),
            P(None, "head"),
            P(None, "head"),
            P(None, "head"),
            P(None, None, "head"),
            P(None, "head"),
            P(None, "head"),
            P(None, "head"),
        ),
        check_vma=False,
    )
```
